32 devices in a mesh: dp: 16 (over z, x, core), tensor: 2 (over y).
Axes of the slice: x: 2, y: 2, z: 4, core: 2. Of those that a mesh axis runs over, the one named last changes fastest.
Arguments:
- tokens: bfloat16 [16384, 768], P(('dp', 'tensor')), may hold values from -6 to 6
- first_values: bfloat16 [16384, 768], P(('dp', 'tensor')), may hold values from -6 to 6
- lengths: int32 [16], P('dp'), may hold values from 513 to 1024, as said below
- reuse_index: int32 [6], replicated, may hold values from 0 to 11
- ln1_gain: float32 [768], replicated, may hold values from 0.1 to 1.9
- ln1_bias: float32 [768], replicated, may hold values from -1.5 to 1.5
- w_query: bfloat16 [768, 768], P(None, 'tensor'), may hold values from -0.21875 to 0.21875
- query_bias: float32 [768], P('tensor'), may hold values from -2.5 to 2.5
- w_key: bfloat16 [768, 768], P(None, 'tensor'), may hold values from -0.21875 to 0.21875
- w_value: bfloat16 [768, 384], P(None, 'tensor'), may hold values from -0.21875 to 0.21875
- value_bias: float32 [384], P('tensor'), may hold values from -2.5 to 2.5
- w_out: bfloat16 [768, 768], P('tensor'), may hold values from -3.5 to 3.5
- out_bias: float32 [768], replicated, may hold values from -1.5 to 1.5
- ln2_gain: float32 [768], replicated, may hold values from 0.1 to 1.9
- ln2_bias: float32 [768], replicated, may hold values from -1.5 to 1.5
- w_up: bfloat16 [768, 3072], P(None, 'tensor'), may hold values from -0.21875 to 0.21875
- up_bias: float32 [3072], P('tensor'), may hold values from -2.5 to 2.5
- w_down: bfloat16 [3072, 768], P('tensor'), may hold values from -0.109375 to 0.109375
- down_bias: float32 [768], replicated, may hold values from -1.5 to 1.5
- cotangent: bfloat16 [16384, 768], P(('dp', 'tensor')), may hold values from -6 to 6
Outputs:
- layer_out: bfloat16 [16384, 768], P(('dp', 'tensor'))
- tokens_grad: float32 [16384, 768], P(('dp', 'tensor'))
- first_values_grad: float32 [16384, 768], P(('dp', 'tensor'))
- ln1_gain_grad: float32 [768], replicated
- ln1_bias_grad: float32 [768], replicated
- w_query_grad: float32 [768, 768], P(None, 'tensor')
- query_bias_grad: float32 [768], P('tensor')
- w_key_grad: float32 [768, 768], P(None, 'tensor')
- w_value_grad: float32 [768, 384], P(None, 'tensor')
- value_bias_grad: float32 [384], P('tensor')
- w_out_grad: float32 [768, 768], P('tensor')
- out_bias_grad: float32 [768], replicated
- ln2_gain_grad: float32 [768], replicated
- ln2_bias_grad: float32 [768], replicated
- w_up_grad: float32 [768, 3072], P(None, 'tensor')
- up_bias_grad: float32 [3072], P('tensor')
- w_down_grad: float32 [3072, 768], P('tensor')
- down_bias_grad: float32 [768], replicated
The draws below stay inside these ranges and needn't reach their ends.
Inputs may be any that keep to these rules, and one draw needn't show every extreme that they name: `lengths`: each sequence has more than 512 tokens, and some sequence fills all 1024 slots. `reuse_index`: indices may repeat.
All inputs are finite; a program needn't handle non-finite values.
Results may differ from the reference program's by a relative error of at most 0.015.
Values may be sent and summed in bfloat16 or wider, within the bound.
No kernel may reach another device: no remote copies, remote signals or barrier semaphores. Data moves between devices by JAX's collectives and lax.ppermute only.
A program may use at most 128 MiB of HBM per device.

```python
from functools import partial
import jax
import jax.numpy as jnp
from jax import lax

D = 768
H = 12
HD = 64
FF = 3072
HALF_H = 6
TOK_DEV = 512
SEQ_LEN = 1024
SEQUENCES = 16
TOKENS = 16384


def draw_lengths(key, part):
    key = jax.random.fold_in(key, 7)
    first_key, second_key = jax.random.split(key)
    drawn = jax.random.randint(first_key, (SEQUENCES,), TOK_DEV + 1, SEQ_LEN + 1)
    longest = jax.random.randint(second_key, (), 0, SEQUENCES)
    return jnp.where(jnp.arange(SEQUENCES) == longest, SEQ_LEN, drawn).astype(jnp.int32)


def plant(values, stream_key, smallest, top_value):
    spot = [jax.random.randint(jax.random.fold_in(stream_key, axis), (), 0, length) for axis, length in enumerate(values.shape)]
    widest = values.shape.index(max(values.shape))
    neighbour = spot[:widest] + [(spot[widest] + 1) % values.shape[widest]] + spot[widest + 1:]
    return values.at[tuple(spot)].set(smallest).at[tuple(neighbour)].set(top_value)


def block_scale(stream_key, extent, cuts, low, high):
    loudness, own = 1.0, jax.random.fold_in(stream_key, 6)
    for axis_at, blocks in cuts:
        heights = jnp.exp(jax.random.uniform(jax.random.fold_in(own, axis_at), (blocks,), jnp.float32, low / len(cuts), high / len(cuts)))
        loudness = loudness * jnp.repeat(heights, extent[axis_at] // blocks).reshape([-1 if axis == axis_at else 1 for axis in range(len(extent))])
    return loudness


def normal_values(stream_key, dims, width, reach, cuts=(), held_as=jnp.bfloat16):
    gain = block_scale(stream_key, dims, cuts, -0.22, 0.18) if cuts else 1.0
    values = jax.random.normal(stream_key, dims, jnp.float32) * width * gain
    return jnp.minimum(jnp.maximum(values, -reach), reach).astype(held_as)


def setup_inputs(seed: int = 0) -> dict:
    key_of = jax.random.split(jax.random.key(seed), 21)
    tokens = normal_values(key_of[0], (TOKENS, D), 1.0, 6.0, ((0, 32),))
    first_values = normal_values(key_of[1], (TOKENS, D), 1.0, 6.0, ((0, 32),))
    lengths = draw_lengths(jax.random.fold_in(key_of[20], 71), 0)
    reuse_index = plant(jax.random.randint(key_of[3], (HALF_H,), 0, H), jax.random.fold_in(key_of[3], 1), 0, H - 1).astype(jnp.int32)
    ln1_gain = jnp.clip(1.0 + 0.18 * jax.random.normal(key_of[4], (D,), jnp.float32), 0.1, 1.9)
    ln1_bias = normal_values(key_of[5], (D,), 0.3, 1.5, (), jnp.float32)
    w_query = normal_values(key_of[6], (D, D), D ** -0.5, 0.21875, ((1, 2),))
    query_bias = normal_values(key_of[7], (D,), 0.5, 2.5, ((0, 2),), jnp.float32)
    w_key = normal_values(key_of[8], (D, D), D ** -0.5, 0.21875, ((1, 2),))
    w_value = normal_values(key_of[9], (D, HALF_H * HD), D ** -0.5, 0.21875, ((1, 2),))
    value_bias = normal_values(key_of[10], (HALF_H * HD,), 0.5, 2.5, ((0, 2),), jnp.float32)
    w_out = normal_values(key_of[11], (D, D), (max(D // 256, 1)) ** -0.5, 3.5, ((0, 2),))
    out_bias = normal_values(key_of[12], (D,), 0.3, 1.5, (), jnp.float32)
    ln2_gain = jnp.clip(1.0 + 0.18 * jax.random.normal(key_of[13], (D,), jnp.float32), 0.1, 1.9)
    ln2_bias = normal_values(key_of[14], (D,), 0.3, 1.5, (), jnp.float32)
    w_up = normal_values(key_of[15], (D, FF), D ** -0.5, 0.21875, ((1, 2),))
    up_bias = normal_values(key_of[16], (FF,), 0.5, 2.5, ((0, 2),), jnp.float32)
    w_down = normal_values(key_of[17], (FF, D), FF ** -0.5, 0.109375, ((0, 2),))
    down_bias = normal_values(key_of[18], (D,), 0.3, 1.5, (), jnp.float32)
    cotangent = normal_values(key_of[19], (TOKENS, D), 1.0, 6.0, ((0, 32),))
    return {"tokens": tokens, "first_values": first_values, "lengths": lengths, "reuse_index": reuse_index, "ln1_gain": ln1_gain, "ln1_bias": ln1_bias, "w_query": w_query, "query_bias": query_bias, "w_key": w_key, "w_value": w_value, "value_bias": value_bias, "w_out": w_out, "out_bias": out_bias, "ln2_gain": ln2_gain, "ln2_bias": ln2_bias, "w_up": w_up, "up_bias": up_bias, "w_down": w_down, "down_bias": down_bias, "cotangent": cotangent}


@jax.custom_vjp
def low(v):
    return lax.optimization_barrier(v.astype(jnp.bfloat16)).astype(jnp.float32)

@jax.custom_vjp
def low_back(v):
    return v

def low_keep(v):
    return (low(v), None)

def low_pass(kept, grad):
    return (grad,)

def back_keep(v):
    return (v, None)

def back_low(kept, grad):
    return (low(grad),)
low.defvjp(low_keep, low_pass)
low_back.defvjp(back_keep, back_low)

def norm_rows(values, norm_gain, norm_offset):
    centre = lax.optimization_barrier(jnp.mean(values, axis=-1, keepdims=True))
    centred = values - centre
    spread = lax.optimization_barrier(jnp.mean(centred * centred, axis=-1, keepdims=True))
    return centred * lax.rsqrt(spread + 1e-05) * norm_gain + norm_offset

def matmul(left, right):
    return jnp.dot(left, right, precision=lax.Precision.HIGHEST, preferred_element_type=jnp.float32)

def attend_sequence(pieces):
    queries, key_heads, value_heads, length = pieces
    scores = jnp.einsum('qhd,khd->hqk', queries, key_heads, precision=lax.Precision.HIGHEST) * HD ** (-0.5)
    scores = low_back(scores)
    row_ids = jnp.arange(SEQ_LEN)[:, None]
    col_ids = jnp.arange(SEQ_LEN)[None, :]
    allowed = (col_ids <= row_ids) & (col_ids < length)
    scores = jnp.where(allowed[None], scores, -1e+30)
    highest = lax.optimization_barrier(jnp.max(scores, axis=-1, keepdims=True))
    weights = jnp.exp(scores - highest)
    chances = low(weights / lax.optimization_barrier(jnp.sum(weights, axis=-1, keepdims=True)))
    return jnp.einsum('hqk,khd->qhd', chances, value_heads, precision=lax.Precision.HIGHEST)

def forward(tokens, first_values, ln1_gain, ln1_bias, w_query, query_bias, w_key, w_value, value_bias, w_out, out_bias, ln2_gain, ln2_bias, w_up, up_bias, w_down, down_bias, lengths=None, reuse_index=None, valid_rows=None):
    row_count = tokens.shape[0]
    normed_one = low(norm_rows(tokens, ln1_gain, ln1_bias))
    queries = low_back(low(matmul(normed_one, w_query) + query_bias))
    key_rows = low_back(low(matmul(normed_one, w_key)))
    fresh_values = low_back(low(matmul(normed_one, w_value) + value_bias))
    reused = first_values.reshape(row_count, H, HD)[:, reuse_index]
    value_heads = jnp.stack([fresh_values.reshape(row_count, HALF_H, HD), reused], axis=2).reshape(row_count, H, HD)
    grid_shape = (SEQUENCES, SEQ_LEN, H, HD)
    mixture = lax.map(jax.checkpoint(attend_sequence), (queries.reshape(grid_shape), key_rows.reshape(grid_shape), value_heads.reshape(grid_shape), lengths))
    heads_out = low_back(low(mixture.reshape(row_count, D)))
    attention = low_back(matmul(heads_out, w_out))
    middle = tokens + attention + out_bias
    normed_two = low(norm_rows(middle, ln2_gain, ln2_bias))
    hidden = low_back(matmul(normed_two, w_up) + up_bias)
    active = low(jax.nn.gelu(hidden))
    branch = low_back(matmul(active, w_down))
    return (middle + branch + down_bias) * valid_rows[:, None]

def reference(tokens, first_values, lengths, reuse_index, ln1_gain, ln1_bias, w_query, query_bias, w_key, w_value, value_bias, w_out, out_bias, ln2_gain, ln2_bias, w_up, up_bias, w_down, down_bias, cotangent):
    slot_ids = jnp.arange(TOKENS)
    owners = (slot_ids // SEQ_LEN).astype(jnp.int32)
    valid_rows = (slot_ids % SEQ_LEN < lengths[owners]).astype(jnp.float32)
    floats = [tokens, first_values, ln1_gain, ln1_bias, w_query, query_bias, w_key, w_value, value_bias, w_out, out_bias, ln2_gain, ln2_bias, w_up, up_bias, w_down, down_bias]
    floats = [item.astype(jnp.float32) for item in floats]
    result, backward = jax.vjp(partial(forward, lengths=lengths, reuse_index=reuse_index, valid_rows=valid_rows), *floats)
    grads = backward(cotangent.astype(jnp.float32))
    return (result.astype(jnp.bfloat16), grads[0], grads[1], grads[2], grads[3], grads[4], grads[5], grads[6], grads[7], grads[8], grads[9], grads[10], grads[11], grads[12], grads[13], grads[14], grads[15], grads[16])
```

```python
from functools import partial

import jax
import jax.numpy as jnp
from jax import lax
from jax.experimental import pallas as pl
from jax.experimental.pallas import tpu as pltpu
from jax.sharding import PartitionSpec as P

H = 12
HD = 64
PARTS = 2
HINT = pl.CostEstimate(flops=1 << 20, bytes_accessed=1 << 16, transcendentals=0)


def norm_rows(values, norm_gain, norm_offset):
    centre = jnp.mean(values, axis=-1, keepdims=True)
    centred = values - centre
    spread = jnp.mean(centred * centred, axis=-1, keepdims=True)
    return centred * lax.rsqrt(spread + 1e-05) * norm_gain + norm_offset


def across(values):
    return lax.ppermute(values, "tensor", [(0, 1), (1, 0)])


def flip(values, bit):
    return lax.ppermute(values, "dp", [(d, d ^ bit) for d in range(lax.axis_size("dp"))])


def halves(values, which):
    half = values.shape[0] // 2
    return (
        lax.dynamic_slice_in_dim(values, which * half, half, 0),
        lax.dynamic_slice_in_dim(values, (1 - which) * half, half, 0),
    )


def join(own, other, which):
    return jnp.concatenate(
        [jnp.where(which == 0, own, other), jnp.where(which == 0, other, own)], axis=0
    )


def slabs(values, which):
    half = values.shape[1] // 2
    return (
        lax.dynamic_slice_in_dim(values, which * half, half, 1),
        lax.dynamic_slice_in_dim(values, (1 - which) * half, half, 1),
    )


def dp_bits():
    return [1 << k for k in range(lax.axis_size("dp").bit_length() - 1)]


class Chain:
    def __init__(self, values, place):
        self.values, self.place = values, place
        self.steps = [("halve", bit) for bit in dp_bits()]
        self.steps += [("double", bit) for bit in reversed(dp_bits())]

    def step(self):
        if not self.steps:
            return
        kind, bit = self.steps.pop(0)
        which = (self.place // bit) % 2
        if kind == "halve":
            keep, send = halves(self.values, which)
            self.values = (
                keep.astype(jnp.float32) + flip(send, bit).astype(jnp.float32)
            ).astype(jnp.bfloat16)
        else:
            self.values = join(self.values, flip(self.values, bit), which)

    def finish(self):
        while self.steps:
            self.step()
        return self.values


def advance(chains, counts):
    for chain, count in zip(chains, counts):
        for _ in range(count):
            chain.step()


def hold(chains, *values):
    flat = lax.optimization_barrier(tuple(c.values for c in chains) + values)
    for chain, held in zip(chains, flat):
        chain.values = held
    return flat[len(chains) :] if len(values) != 1 else flat[-1]


def after(values, *found):
    return lax.optimization_barrier((values, found))[0]


def reduce_small(values):
    for bit in dp_bits():
        values = values + flip(values, bit)
    return values


NT = (((1,), (1,)), ((), ()))
TN = (((0,), (0,)), ((), ()))
NN = (((1,), (0,)), ((), ()))
BLOCK = 256
VMEM_BYTES = 48 * 1024 * 1024


def dot(left, right, dims):
    return lax.dot_general(left, right, dims, preferred_element_type=jnp.float32)


def score_parts(k_ref, query, begin, length, sure):
    parts = []
    for first, last in ((0, begin), (begin, begin + BLOCK)):
        if last > first:
            part = dot(k_ref[first:last, :], query, NT)
            keys = lax.broadcasted_iota(jnp.int32, part.shape, 0) + first
            if first == begin:
                queries = lax.broadcasted_iota(jnp.int32, part.shape, 1) + begin
                part = jnp.where((keys <= queries) & (keys < length), part, -1e30)
            elif last > sure:
                part = jnp.where(keys < length, part, -1e30)
            parts.append((first, last, part))
    return parts


def attend_kernel(sure, length_ref, q_ref, k_ref, v_ref, out_ref, lse_ref):
    length = length_ref[0]
    rows = q_ref.shape[0]
    for begin in range(0, rows, BLOCK):
        query = q_ref[begin : begin + BLOCK, :] * HD ** (-0.5)
        lane = lax.broadcasted_iota(jnp.int32, query.shape, 1)
        mixed = []
        for side in range(2):
            mine = (lane < HD) if side == 0 else (lane >= HD)
            parts = score_parts(k_ref, jnp.where(mine, query, 0).astype(query.dtype), begin, length, sure)
            highest = None
            for _, _, part in parts:
                top = jnp.max(part, axis=0, keepdims=True)
                highest = top if highest is None else jnp.maximum(highest, top)
            total, mix = 0.0, 0.0
            for first, last, part in parts:
                weights = jnp.exp(part - highest)
                total = total + jnp.sum(weights, axis=0, keepdims=True)
                mix = mix + dot(v_ref[first:last, :], weights.astype(jnp.bfloat16), TN)
            mixed.append(mix * (1.0 / total))
            lse_ref[0, side : side + 1, begin : begin + BLOCK] = highest + jnp.log(total)
        row = lax.broadcasted_iota(jnp.int32, mixed[0].shape, 0)
        both = jnp.where(row < HD, mixed[0], mixed[1])
        out_ref[begin : begin + BLOCK, :] = both.T.astype(jnp.bfloat16)


def attend(length, queries, keys, values, sure):
    rows, width = queries.shape
    pairs = width // (2 * HD)
    column = pl.BlockSpec((rows, 2 * HD), lambda p, *_: (0, p))
    return pl.pallas_call(
        partial(attend_kernel, sure),
        grid_spec=pltpu.PrefetchScalarGridSpec(
            num_scalar_prefetch=1,
            grid=(pairs,),
            in_specs=[column] * 3,
            out_specs=[column, pl.BlockSpec((1, 2, rows), lambda p, *_: (p, 0, 0))],
        ),
        out_shape=[
            jax.ShapeDtypeStruct((rows, width), jnp.bfloat16),
            jax.ShapeDtypeStruct((pairs, 2, rows), jnp.float32),
        ],
        compiler_params=pltpu.CompilerParams(vmem_limit_bytes=VMEM_BYTES),
        cost_estimate=HINT,
    )(length, queries, keys, values)


def attend_back_kernel(
    sure, length_ref, q_ref, k_ref, v_ref, out_ref, lse_ref, grad_ref, dq_ref, dk_ref, dv_ref, dk_sum, dv_sum
):
    length = length_ref[0]
    rows = q_ref.shape[0]
    dk_sum[...] = jnp.zeros_like(dk_sum)
    dv_sum[...] = jnp.zeros_like(dv_sum)
    for begin in range(0, rows, BLOCK):
        block = slice(begin, begin + BLOCK)
        query = q_ref[block, :] * HD ** (-0.5)
        grad = grad_ref[block, :]
        product = (grad.astype(jnp.float32) * out_ref[block, :].astype(jnp.float32)).T
        lane = lax.broadcasted_iota(jnp.int32, query.shape, 1)
        found = []
        for side in range(2):
            mine = (lane < HD) if side == 0 else (lane >= HD)
            own_query = jnp.where(mine, query, 0).astype(query.dtype)
            own_grad = jnp.where(mine, grad, 0).astype(grad.dtype)
            inner = jnp.sum(product[side * HD : (side + 1) * HD, :], axis=0, keepdims=True)
            lse = lse_ref[0, side : side + 1, block]
            query_grad = 0.0
            for first, last, part in score_parts(k_ref, own_query, begin, length, sure):
                chances = jnp.exp(part - lse)
                chance_grad = dot(v_ref[first:last, :], own_grad, NT)
                score_grad = (chances * (chance_grad - inner)).astype(jnp.bfloat16)
                dv_sum[first:last, :] += dot(chances.astype(jnp.bfloat16), own_grad, NN)
                dk_sum[first:last, :] += dot(score_grad, own_query, NN)
                query_grad = query_grad + dot(k_ref[first:last, :], score_grad, TN)
            found.append(query_grad)
        row = lax.broadcasted_iota(jnp.int32, found[0].shape, 0)
        both = jnp.where(row < HD, found[0], found[1]) * HD ** (-0.5)
        dq_ref[block, :] = both.T.astype(jnp.bfloat16)
    dk_ref[...] = dk_sum[...].astype(jnp.bfloat16)
    dv_ref[...] = dv_sum[...].astype(jnp.bfloat16)


def attend_back(length, queries, keys, values, heads_out, lse, heads_grad, sure):
    rows, width = queries.shape
    pairs = width // (2 * HD)
    column = pl.BlockSpec((rows, 2 * HD), lambda p, *_: (0, p))
    lse_spec = pl.BlockSpec((1, 2, rows), lambda p, *_: (p, 0, 0))
    shape = jax.ShapeDtypeStruct((rows, width), jnp.bfloat16)
    return pl.pallas_call(
        partial(attend_back_kernel, sure),
        grid_spec=pltpu.PrefetchScalarGridSpec(
            num_scalar_prefetch=1,
            grid=(pairs,),
            in_specs=[column] * 4 + [lse_spec, column],
            out_specs=[column] * 3,
            scratch_shapes=[pltpu.VMEM((rows, 2 * HD), jnp.float32)] * 2,
        ),
        out_shape=[shape] * 3,
        compiler_params=pltpu.CompilerParams(vmem_limit_bytes=VMEM_BYTES),
        cost_estimate=HINT,
    )(length, queries, keys, values, heads_out, lse, heads_grad)


def gelu_parts(hidden):
    rate = 0.7978845608028654
    square = hidden * hidden
    bend = jnp.tanh(rate * hidden * (1.0 + 0.044715 * square))
    lift = 0.5 * (1.0 + bend)
    slope = lift + 0.5 * hidden * (1.0 - bend * bend) * (rate * (1.0 + 3 * 0.044715 * square))
    return hidden * lift, slope


def feed_kernel(
    normed_ref,
    grad_ref,
    up_ref,
    bias_ref,
    down_ref,
    branch_ref,
    back_ref,
    active_ref,
    hidden_grad_ref,
    bias_grad_ref,
):
    normed, grad = normed_ref[...], grad_ref[...]
    up, down = up_ref[...], down_ref[...]
    active, slope = gelu_parts(dot(normed, up, NN) + bias_ref[...])
    active = active.astype(jnp.bfloat16)
    hidden_grad = (dot(grad, down, NT) * slope).astype(jnp.bfloat16)

    @pl.when(pl.program_id(0) == 0)
    def _():
        branch_ref[...] = jnp.zeros_like(branch_ref)
        back_ref[...] = jnp.zeros_like(back_ref)

    branch_ref[...] += dot(active, down, NN)
    back_ref[...] += dot(hidden_grad, up, NT)
    active_ref[...] = active
    hidden_grad_ref[...] = hidden_grad
    bias_grad_ref[...] = jnp.sum(hidden_grad.astype(jnp.float32), axis=0, keepdims=True)


def feed(normed, grad, w_up, up_bias, w_down):
    rows, width = normed.shape
    hidden = w_down.shape[0]
    tile = BLOCK
    whole = pl.BlockSpec((rows, width), lambda i: (0, 0))
    part = pl.BlockSpec((rows, tile), lambda i: (0, i))
    return pl.pallas_call(
        feed_kernel,
        grid=(hidden // tile,),
        in_specs=[
            whole,
            whole,
            pl.BlockSpec((width, tile), lambda i: (0, i)),
            pl.BlockSpec((1, tile), lambda i: (0, i)),
            pl.BlockSpec((tile, width), lambda i: (i, 0)),
        ],
        out_specs=[whole, whole, part, part, pl.BlockSpec((1, tile), lambda i: (0, i))],
        out_shape=[
            jax.ShapeDtypeStruct((rows, width), jnp.float32),
            jax.ShapeDtypeStruct((rows, width), jnp.float32),
            jax.ShapeDtypeStruct((rows, hidden), jnp.bfloat16),
            jax.ShapeDtypeStruct((rows, hidden), jnp.bfloat16),
            jax.ShapeDtypeStruct((1, hidden), jnp.float32),
        ],
        compiler_params=pltpu.CompilerParams(vmem_limit_bytes=VMEM_BYTES),
        cost_estimate=HINT,
    )(normed, grad, w_up, up_bias[None], w_down)


def feed_weights_kernel(tiles, *refs):
    active_refs, hidden_grad_refs, normed_refs, grad_refs = refs[0:2], refs[2:4], refs[4:6], refs[6:8]
    out_ref = refs[8]
    for k in range(tiles):
        part = slice(k * BLOCK, (k + 1) * BLOCK)
        down = sum(dot(a[:, part], g[...], TN) for a, g in zip(active_refs, grad_refs))
        out_ref[0, part, :] = down.astype(jnp.bfloat16)
        up = sum(dot(n[...], h[:, part], TN) for n, h in zip(normed_refs, hidden_grad_refs))
        out_ref[1, :, part] = up.astype(jnp.bfloat16)


def feed_weights(part, actives, hidden_grads, normeds, grads):
    rows, width = normeds[0].shape
    hidden = actives[0].shape[1] // PARTS
    whole = pl.BlockSpec((rows, width), lambda i: (0, 0))
    column = pl.BlockSpec((rows, hidden), lambda i: (0, part))
    return pl.pallas_call(
        partial(feed_weights_kernel, hidden // BLOCK),
        grid=(1,),
        in_specs=[column] * 4 + [whole] * 4,
        out_specs=pl.BlockSpec((2, hidden, width), lambda i: (0, 0, 0)),
        out_shape=jax.ShapeDtypeStruct((2, hidden, width), jnp.bfloat16),
        compiler_params=pltpu.CompilerParams(vmem_limit_bytes=VMEM_BYTES),
        cost_estimate=HINT,
    )(*actives, *hidden_grads, *normeds, *grads)


def project_kernel(x_ref, w_ref, qb_ref, vb_ref, reused_ref, q_ref, k_ref, v_ref):
    width = q_ref.shape[1]
    fresh = vb_ref.shape[1]
    found = dot(x_ref[...], w_ref[...], NN)
    q_ref[...] = (found[:, :width] + qb_ref[...]).astype(jnp.bfloat16)
    k_ref[...] = found[:, width : 2 * width].astype(jnp.bfloat16)
    values = (found[:, 2 * width :] + vb_ref[...]).astype(jnp.bfloat16)
    reused = reused_ref[...]
    for head in range(fresh // HD):
        part = slice(head * HD, (head + 1) * HD)
        v_ref[:, 2 * head * HD : 2 * (head + 1) * HD] = jnp.concatenate(
            [values[:, part], reused[:, part]], axis=1
        )


def project(normed, weight, query_bias, value_bias, reused):
    rows, depth = normed.shape
    width, fresh = query_bias.shape[0], value_bias.shape[0]
    out = pl.BlockSpec((BLOCK, width), lambda i: (i, 0))
    return pl.pallas_call(
        project_kernel,
        grid=(rows // BLOCK,),
        in_specs=[
            pl.BlockSpec((BLOCK, depth), lambda i: (i, 0)),
            pl.BlockSpec(weight.shape, lambda i: (0, 0)),
            pl.BlockSpec((1, width), lambda i: (0, 0)),
            pl.BlockSpec((1, fresh), lambda i: (0, 0)),
            pl.BlockSpec((BLOCK, fresh), lambda i: (i, 0)),
        ],
        out_specs=[out] * 3,
        out_shape=[jax.ShapeDtypeStruct((rows, width), jnp.bfloat16)] * 3,
        compiler_params=pltpu.CompilerParams(vmem_limit_bytes=VMEM_BYTES),
        cost_estimate=HINT,
    )(normed, weight, query_bias[None], value_bias[None], reused)


def fresh_columns(values):
    return jnp.concatenate(
        [values[:, k * HD : (k + 1) * HD] for k in range(0, values.shape[1] // HD, 2)], axis=1
    )


def reused_columns(values):
    return jnp.concatenate(
        [values[:, k * HD : (k + 1) * HD] for k in range(1, values.shape[1] // HD, 2)], axis=1
    )


def last_weights_kernel(x_ref, dq_ref, dk_ref, dv_ref, wo_ref, out_ref, q_sum_ref, v_sum_ref):
    size, half = dq_ref.shape[1], wo_ref.shape[1] // 2
    out_ref[:size, :half] = wo_ref[:, :half]
    out_ref[size:, :half] = wo_ref[:, half:]
    x = x_ref[...]
    out_ref[:, half : half + size] = dot(x, dq_ref[...], TN).astype(jnp.bfloat16)
    out_ref[:, half + size : half + 2 * size] = dot(x, dk_ref[...], TN).astype(jnp.bfloat16)
    fresh = fresh_columns(dv_ref[...])
    out_ref[:, half + 2 * size :] = dot(x, fresh, TN).astype(jnp.bfloat16)
    q_sum_ref[...] = jnp.sum(dq_ref[...].astype(jnp.float32), axis=0, keepdims=True)
    v_sum_ref[...] = jnp.sum(fresh.astype(jnp.float32), axis=0, keepdims=True)


def last_weights(normed, query_grad, key_grad, value_grad, w_out_grad):
    width, size = normed.shape[1], query_grad.shape[1]
    return pl.pallas_call(
        last_weights_kernel,
        out_shape=[
            jax.ShapeDtypeStruct((width, width // 2 + 5 * size // 2), jnp.bfloat16),
            jax.ShapeDtypeStruct((1, size), jnp.float32),
            jax.ShapeDtypeStruct((1, size // 2), jnp.float32),
        ],
        compiler_params=pltpu.CompilerParams(vmem_limit_bytes=VMEM_BYTES),
        cost_estimate=HINT,
    )(normed, query_grad, key_grad, value_grad, w_out_grad)


def inputs_back_kernel(side_ref, *refs):
    w_ref, keep_ref, send_ref, keep_reused_ref, send_reused_ref = refs[6:]
    for (dq_ref, dk_ref, dv_ref), out_ref, reused_ref in (
        (refs[0:3], keep_ref, keep_reused_ref),
        (refs[3:6], send_ref, send_reused_ref),
    ):
        size = dq_ref.shape[1]
        total = dot(dq_ref[...], w_ref[:, :size], NT) + dot(
            dk_ref[...], w_ref[:, size : 2 * size], NT
        )
        total = total + dot(fresh_columns(dv_ref[...]), w_ref[:, 2 * size :], NT)
        out_ref[...] = total.astype(out_ref.dtype)
        reused_ref[...] = reused_columns(dv_ref[...])


def inputs_back(side, query_grad, key_grad, value_grad, w_in):
    rows, size = query_grad.shape
    half, width = rows // 2, w_in.shape[0]
    blocks = half // BLOCK
    keep = pl.BlockSpec((BLOCK, size), lambda i, side: (side[0] * blocks + i, 0))
    send = pl.BlockSpec((BLOCK, size), lambda i, side: ((1 - side[0]) * blocks + i, 0))
    out = pl.BlockSpec((BLOCK, width), lambda i, side: (i, 0))
    out_reused = pl.BlockSpec((BLOCK, size // 2), lambda i, side: (i, 0))
    return pl.pallas_call(
        inputs_back_kernel,
        grid_spec=pltpu.PrefetchScalarGridSpec(
            num_scalar_prefetch=1,
            grid=(blocks,),
            in_specs=[keep] * 3 + [send] * 3 + [pl.BlockSpec(w_in.shape, lambda i, side: (0, 0))],
            out_specs=[out, out, out_reused, out_reused],
        ),
        out_shape=[
            jax.ShapeDtypeStruct((half, width), jnp.float32),
            jax.ShapeDtypeStruct((half, width), jnp.bfloat16),
            jax.ShapeDtypeStruct((half, size // 2), jnp.bfloat16),
            jax.ShapeDtypeStruct((half, size // 2), jnp.bfloat16),
        ],
        compiler_params=pltpu.CompilerParams(vmem_limit_bytes=VMEM_BYTES),
        cost_estimate=HINT,
    )(
        jnp.reshape(side, (1,)),
        query_grad,
        key_grad,
        value_grad,
        query_grad,
        key_grad,
        value_grad,
        w_in,
    )


def product(left, right):
    return dot(left, right, NN)


def shards(
    tokens,
    first_values,
    lengths,
    reuse_index,
    ln1_gain,
    ln1_bias,
    w_query,
    query_bias,
    w_key,
    w_value,
    value_bias,
    w_out,
    out_bias,
    ln2_gain,
    ln2_bias,
    w_up,
    up_bias,
    w_down,
    down_bias,
    cotangent,
):
    place, side = lax.axis_index("dp"), lax.axis_index("tensor")
    core = place % 2
    local_rows, width = tokens.shape
    rows = 2 * local_rows
    query_size, value_size = query_bias.shape[0], value_bias.shape[0]
    fresh_here = value_size // HD
    length = lengths[0]
    positions = side * local_rows + jnp.arange(local_rows)
    valid_rows = (positions < length).astype(jnp.float32)[:, None]

    inputs = tokens.astype(jnp.float32)
    normed_one = norm_rows(inputs, ln1_gain, ln1_bias).astype(jnp.bfloat16)
    got_one = across(normed_one)
    early, late = cotangent[: local_rows // 2], cotangent[local_rows // 2 :]
    got_early = across(early)
    picks = reuse_index[jnp.arange(2 * value_size) // HD]
    selector = (
        (jnp.arange(width)[:, None] // HD == picks[None, :])
        & ((jnp.arange(width) % HD)[:, None] == (jnp.arange(2 * value_size) % HD)[None, :])
    ).astype(jnp.bfloat16)
    first_values, selector = after((first_values, selector), normed_one)
    chosen = product(first_values, selector).astype(jnp.bfloat16)
    own_chosen, other_chosen = slabs(chosen, side)
    got_chosen = across(other_chosen)
    gathered_one = join(normed_one, got_one, side)
    reused = join(own_chosen, got_chosen, side)
    w_in = jnp.concatenate([w_query, w_key, w_value], axis=1)

    out_grad = cotangent.astype(jnp.float32) * valid_rows
    down_bias_grad = jnp.sum(out_grad, axis=0)
    branch_grad = out_grad.astype(jnp.bfloat16)
    out_piece, late = after((halves(w_out, core)[0], late), got_one, got_chosen)
    got_out = across(out_piece)
    got_late = across(late)
    other_positions = (1 - side) * local_rows + jnp.arange(local_rows)
    got_branch_grad = jnp.where(
        (other_positions < length)[:, None], jnp.concatenate([got_early, got_late], axis=0), 0
    )

    queries, keys, values = project(gathered_one, w_in, query_bias, value_bias, reused)
    heads_out, lse = attend(lengths, queries, keys, values, local_rows)
    w_out_other = join(got_out, flip(got_out, 1), core)
    heads_keep, heads_send = halves(heads_out, side)
    heads_got = across(heads_send)
    attention = product(heads_keep, w_out) + product(heads_got, w_out_other)
    middle = inputs + attention + out_bias
    normed_two = norm_rows(middle, ln2_gain, ln2_bias).astype(jnp.bfloat16)
    got_two = across(normed_two)
    own = feed(normed_two, branch_grad, w_up, up_bias, w_down)
    got_two, own = lax.optimization_barrier((got_two, own))
    other = feed(got_two, got_branch_grad, w_up, up_bias, w_down)
    up_bias_grad = (own[4] + other[4])[0]
    back_got = across(other[1].astype(jnp.bfloat16))
    chains = []
    for part in range(PARTS):
        weights = feed_weights(
            part,
            (own[2], other[2]),
            (own[3], other[3]),
            (normed_two, got_two),
            (branch_grad, got_branch_grad),
        )
        chains.append(Chain(weights.reshape(-1, width), place))
    advance(chains, [1, 0])
    (branch_send,) = after((other[0].astype(jnp.bfloat16),), back_got)
    back_got = hold(chains, back_got)
    normed_two_grad = own[1] + back_got.astype(jnp.float32)
    _, norm_two_back = jax.vjp(norm_rows, middle, ln2_gain, ln2_bias)
    middle_part, ln2_gain_grad, ln2_bias_grad = norm_two_back(normed_two_grad)
    middle_grad = out_grad + middle_part
    out_bias_grad = jnp.sum(middle_grad, axis=0)
    attention_grad = middle_grad.astype(jnp.bfloat16)
    heads_grad_got = across(dot(attention_grad, w_out_other, NT).astype(jnp.bfloat16))
    heads_grad = join(dot(attention_grad, w_out, NT).astype(jnp.bfloat16), heads_grad_got, side)
    out_grad_got = across(dot(heads_got, attention_grad, TN).astype(jnp.bfloat16))
    w_out_part = dot(heads_keep, attention_grad, TN)
    advance(chains, [1, 1])
    heads_grad, branch_send = hold(chains, heads_grad, branch_send)
    query_grad, key_grad, value_grad = attend_back(
        lengths, queries, keys, values, heads_out, lse, heads_grad, local_rows
    )
    w_out_grad = (w_out_part + out_grad_got.astype(jnp.float32)).astype(jnp.bfloat16)
    last, query_sums, value_sums = last_weights(
        gathered_one, query_grad, key_grad, value_grad, w_out_grad
    )
    query_bias_grad, value_bias_grad = query_sums[0], value_sums[0]
    chains.append(Chain(last, place))
    one_keep, one_send, first_keep, first_send = inputs_back(
        side, query_grad, key_grad, value_grad, w_in
    )
    branch_got = across(branch_send)
    advance(chains, [2, 1, 0])
    one_send, first_send, branch_got = hold(chains, one_send, first_send, branch_got)
    one_got = across(one_send)
    first_got = across(first_send)
    advance(chains, [2, 2, 2])
    one_got, first_got = hold(chains, one_got, first_got)
    result = (
        (middle + own[0] + branch_got.astype(jnp.float32) + down_bias) * valid_rows
    ).astype(jnp.bfloat16)
    normed_one_grad = one_keep + one_got.astype(jnp.float32)
    first_grads = jnp.concatenate(
        [jnp.where(side == 0, first_keep, first_got), jnp.where(side == 0, first_got, first_keep)],
        axis=1,
    )
    first_values_grad = dot(first_grads, selector, NT)
    _, norm_one_back = jax.vjp(norm_rows, inputs, ln1_gain, ln1_bias)
    input_part, ln1_gain_grad, ln1_bias_grad = norm_one_back(normed_one_grad)
    tokens_grad = middle_grad + input_part
    whole = jnp.concatenate(
        [ln1_gain_grad, ln1_bias_grad, out_bias_grad, ln2_gain_grad, ln2_bias_grad, down_bias_grad]
    )
    whole = whole + across(whole)
    small = jnp.concatenate([whole, query_bias_grad, value_bias_grad, up_bias_grad])
    bits = dp_bits()
    for bit in bits[:1]:
        small = small + flip(small, bit)
    advance(chains, [1, 2, 2])
    small, result, tokens_grad, first_values_grad = hold(
        chains, small, result, tokens_grad, first_values_grad
    )
    for bit in bits[1:3]:
        small = small + flip(small, bit)
    advance(chains, [1, 1, 2])
    small = hold(chains, small)
    for bit in bits[3:]:
        small = small + flip(small, bit)
    advance(chains, [0, 1, 1])
    feeds = [chain.finish().astype(jnp.float32) for chain in chains[:PARTS]]
    w_down_grad = jnp.concatenate([f[: f.shape[0] // 2] for f in feeds], axis=0)
    w_up_grad = jnp.concatenate([f[f.shape[0] // 2 :] for f in feeds], axis=1)
    chains[PARTS].values, w_down_grad, w_up_grad, small = lax.optimization_barrier(
        (chains[PARTS].values, w_down_grad, w_up_grad, small)
    )
    ln1_gain_grad, ln1_bias_grad, out_bias_grad, ln2_gain_grad, ln2_bias_grad, down_bias_grad = (
        small[k * width : (k + 1) * width] for k in range(6)
    )
    query_bias_grad = small[6 * width : 6 * width + query_size]
    value_bias_grad = small[6 * width + query_size : 6 * width + query_size + value_size]
    up_bias_grad = small[6 * width + query_size + value_size :]
    half = width // 2
    last = chains[PARTS].finish().astype(jnp.float32)
    w_out_grad = jnp.concatenate([last[:query_size, :half], last[query_size:, :half]], axis=1)
    w_query_grad = last[:, half : half + query_size]
    w_key_grad = last[:, half + query_size : half + 2 * query_size]
    w_value_grad = last[:, half + 2 * query_size :]
    return (
        result,
        tokens_grad,
        first_values_grad,
        ln1_gain_grad,
        ln1_bias_grad,
        w_query_grad,
        query_bias_grad,
        w_key_grad,
        w_value_grad,
        value_bias_grad,
        w_out_grad,
        out_bias_grad,
        ln2_gain_grad,
        ln2_bias_grad,
        w_up_grad,
        up_bias_grad,
        w_down_grad,
        down_bias_grad,
    )


def solution(mesh):
    in_specs = (
        P(("dp", "tensor"), None),
        P(("dp", "tensor"), None),
        P("dp"),
        P(),
        P(),
        P(),
        P(None, "tensor"),
        P("tensor"),
        P(None, "tensor"),
        P(None, "tensor"),
        P("tensor"),
        P("tensor", None),
        P(),
        P(),
        P(),
        P(None, "tensor"),
        P("tensor"),
        P("tensor", None),
        P(),
        P(("dp", "tensor"), None),
    )
    out_specs = (
        P(("dp", "tensor"), None),
        P(("dp", "tensor"), None),
        P(("dp", "tensor"), None),
        P(),
        P(),
        P(None, "tensor"),
        P("tensor"),
        P(None, "tensor"),
        P(None, "tensor"),
        P("tensor"),
        P("tensor", None),
        P(),
        P(),
        P(),
        P(None, "tensor"),
        P("tensor"),
        P("tensor", None),
        P(),
    )
    return jax.shard_map(shards, mesh=mesh, in_specs=in_specs, out_specs=out_specs, check_vma=False)
```

```python
from functools import partial

import jax
import jax.numpy as jnp
from jax import lax
from jax.experimental import pallas as pl
from jax.experimental.pallas import tpu as pltpu
from jax.sharding import PartitionSpec as P

H = 12
HD = 64
PARTS = 2
BLOCK = 256
VMEM_BYTES = 24 * 1024 * 1024
NT = (((1,), (1,)), ((), ()))
TN = (((0,), (0,)), ((), ()))
NN = (((1,), (0,)), ((), ()))
F32 = jnp.float32
BF16 = jnp.bfloat16
STRETCH = 15
SIDE, LENGTH, CORE, WHICH = 0, 1, 2, 3


def shape(dims, dtype):
    return jax.ShapeDtypeStruct(dims, dtype)


def call(kernel, scalars, arrays, out_shape, in_specs=None, out_specs=None, grid=(1,), scratch=(), micros=2):
    def whole(array):
        return pl.BlockSpec(array.shape, lambda *_, dims=len(array.shape): (0,) * dims)

    return pl.pallas_call(
        kernel,
        grid_spec=pltpu.PrefetchScalarGridSpec(
            num_scalar_prefetch=1,
            grid=grid,
            in_specs=[s or whole(a) for s, a in zip(in_specs or [None] * len(arrays), arrays)],
            out_specs=[
                s or whole(o) for s, o in zip(out_specs or [None] * len(out_shape), out_shape)
            ],
            scratch_shapes=list(scratch),
        ),
        out_shape=out_shape,
        compiler_params=pltpu.CompilerParams(vmem_limit_bytes=VMEM_BYTES),
        cost_estimate=pl.CostEstimate(
            flops=STRETCH * micros * 1_150_000_000,
            bytes_accessed=STRETCH * micros * 3_600_000,
            transcendentals=0,
        ),
    )(scalars, *arrays)


def dot(left, right, dims=NN):
    return lax.dot_general(left, right, dims, preferred_element_type=F32)


def pick(flag, left, right):
    return jnp.where(flag, left.astype(F32), right.astype(F32)).astype(left.dtype)


def across(values):
    return lax.ppermute(values, "tensor", [(0, 1), (1, 0)])


def flip(values, bit):
    return lax.ppermute(values, "dp", [(d, d ^ bit) for d in range(lax.axis_size("dp"))])


def halves(values, which):
    half = values.shape[0] // 2
    return (
        lax.dynamic_slice_in_dim(values, which * half, half, 0),
        lax.dynamic_slice_in_dim(values, (1 - which) * half, half, 0),
    )


def join(own, other, which):
    return jnp.concatenate(
        [jnp.where(which == 0, own, other), jnp.where(which == 0, other, own)], axis=0
    )


def slabs(values, which):
    half = values.shape[1] // 2
    return (
        lax.dynamic_slice_in_dim(values, which * half, half, 1),
        lax.dynamic_slice_in_dim(values, (1 - which) * half, half, 1),
    )


def after(values, *found):
    return lax.optimization_barrier((values, found))[0]


def dp_bits():
    return [1 << k for k in range(lax.axis_size("dp").bit_length() - 1)]


def parts_of(refs):
    if len(refs) > 1:
        return list(refs)
    return [refs[0].at[p] for p in range(refs[0].shape[0])]


def fold_kernel(n_got, scalars, own_ref, *refs):
    gots, keep_ref, sends = parts_of(refs[:n_got]), refs[n_got], parts_of(refs[n_got + 1 :])
    half = keep_ref.shape[1]
    which = scalars[0]
    for p, (got_ref, send_ref) in enumerate(zip(gots, sends)):
        for out_ref, part in ((keep_ref.at[p], which), (send_ref, 1 - which)):
            rows = pl.ds(pl.multiple_of(part * half, half), half)
            total = own_ref[p, rows, :].astype(F32) + got_ref[rows, :].astype(F32)
            out_ref[...] = total.astype(BF16)


def join_kernel(n_own, n_got, scalars, *refs):
    owns, gots = parts_of(refs[:n_own]), parts_of(refs[n_own : n_own + n_got])
    outs = parts_of(refs[n_own + n_got :])
    which = scalars[0]
    for own_ref, got_ref, out_ref in zip(owns, gots, outs):
        half = own_ref.shape[0]
        for in_ref, part in ((own_ref, which), (got_ref, 1 - which)):
            out_ref[pl.ds(pl.multiple_of(part * half, half), half), :] = in_ref[...]


class Chain:
    def __init__(self, keep, send, parts, place, split):
        self.keep, self.sends, self.gots = keep, (send,), ()
        self.parts, self.place, self.split = parts, place, split
        bits = dp_bits()
        self.steps = []
        for bit, following in zip(bits, bits[1:] + [0]):
            self.steps += [("halve", bit, following)] * (parts if split and bit == 2 else 1)
        for bit in reversed(bits):
            self.steps += [("double", bit, bit // 2)] * (parts if split and bit == 2 else 1)

    @property
    def state(self):
        return (self.keep, self.sends, self.gots)

    @state.setter
    def state(self, values):
        self.keep, self.sends, self.gots = values

    def which(self, bit):
        return (self.place // bit) % 2

    def shapes(self, rows, columns, bit):
        if self.split and bit == 2:
            return [shape((rows, columns), BF16)] * self.parts
        return [shape((self.parts, rows, columns), BF16)]

    def step(self):
        if not self.steps:
            return
        kind, bit, following = self.steps.pop(0)
        self.gots += (flip(self.sends[len(self.gots)], bit),)
        if len(self.gots) < len(self.sends):
            return
        gots, self.gots = self.gots, ()
        rows, columns = gots[0].shape[-2:]
        if kind == "halve" and not following:
            total = self.keep.astype(F32) + gots[0].astype(F32)
            self.keep, self.sends = None, (total.astype(BF16),)
        elif kind == "halve" and (rows // 2) % 16:
            total = (self.keep.astype(F32) + gots[0].astype(F32)).astype(BF16)
            self.keep, send = (
                lax.dynamic_slice_in_dim(total, w * (rows // 2), rows // 2, 1)
                for w in (self.which(following), 1 - self.which(following))
            )
            self.sends = (send,)
        elif kind == "halve":
            whole = [pl.BlockSpec(g.shape, lambda *_, d=g.ndim: (0,) * d) for g in gots]
            kept = pl.BlockSpec((self.parts, rows, columns), lambda *_: (0, 0, 0))
            self.keep, *sends = call(
                partial(fold_kernel, len(gots)),
                self.which(following)[None],
                [self.keep, *gots],
                [shape((self.parts, rows // 2, columns), BF16)]
                + self.shapes(rows // 2, columns, following),
                [kept, *whole],
            )
            self.sends = tuple(sends)
        elif not following:
            self.gots = gots
        elif rows % 16:
            own, got, w = self.sends[0], gots[0], self.which(bit)
            self.sends = (
                jnp.concatenate(
                    [jnp.where(w == 0, own, got), jnp.where(w == 0, got, own)], axis=1
                ),
            )
        else:
            self.sends = tuple(
                call(
                    partial(join_kernel, len(self.sends), len(gots)),
                    self.which(bit)[None],
                    [*self.sends, *gots],
                    self.shapes(2 * rows, columns, following),
                )
            )


def advance(chains, counts):
    for chain, count in zip(chains, counts):
        for _ in range(count):
            chain.step()


def hold(chains, *values):
    states, values = lax.optimization_barrier(([c.state for c in chains], values))
    for chain, state in zip(chains, states):
        chain.state = state
    return values if len(values) != 1 else values[0]


def unit_rows(values):
    centred = values - jnp.mean(values, axis=-1, keepdims=True)
    spread = jnp.mean(centred * centred, axis=-1, keepdims=True)
    scale = lax.rsqrt(spread + 1e-05)
    return centred * scale, scale


def unit_rows_back(unit, scale, grad):
    inner = jnp.mean(grad * unit, axis=-1, keepdims=True)
    return scale * (grad - jnp.mean(grad, axis=-1, keepdims=True) - unit * inner)


def column_sum(values):
    return jnp.sum(values, axis=0, keepdims=True)


def row_spec(width, place=lambda i: i):
    return pl.BlockSpec((BLOCK, width), lambda i, scalars: (place(i), 0))


def valid_rows(scalars, block, rows):
    position = scalars[SIDE] * rows + block * BLOCK
    position = position + lax.broadcasted_iota(jnp.int32, (BLOCK, 1), 0)
    return (position < scalars[LENGTH]).astype(F32)


def norm_kernel(scalars, x_ref, gain_ref, bias_ref, out_ref):
    unit, _ = unit_rows(x_ref[...].astype(F32))
    out_ref[...] = (unit * gain_ref[...] + bias_ref[...]).astype(BF16)


def norm(scalars, values, gain, bias):
    rows, width = values.shape
    return call(
        norm_kernel,
        scalars,
        [values, gain[None], bias[None]],
        [shape((rows, width), BF16)],
        [row_spec(width), None, None],
        [row_spec(width)],
        (rows // BLOCK,),
    )[0]


def project_kernel(
    scalars, x_ref, x_got_ref, w_ref, qb_ref, vb_ref, reused_ref, reused_got_ref, q_ref, k_ref, v_ref
):
    width, fresh = q_ref.shape[1], vb_ref.shape[1]
    own = pl.program_id(0) < pl.num_programs(0) // 2

    def work(x_ref, reused_ref):
        found = dot(x_ref[...], w_ref[...])
        q_ref[...] = (found[:, :width] + qb_ref[...]).astype(BF16)
        k_ref[...] = found[:, width : 2 * width].astype(BF16)
        values = (found[:, 2 * width :] + vb_ref[...]).astype(BF16)
        reused = reused_ref[...]
        for head in range(fresh // HD):
            part = slice(head * HD, (head + 1) * HD)
            v_ref[:, 2 * head * HD : 2 * (head + 1) * HD] = jnp.concatenate(
                [values[:, part], reused[:, part]], axis=1
            )

    pl.when(own)(lambda: work(x_ref, reused_ref))
    pl.when(jnp.logical_not(own))(lambda: work(x_got_ref, reused_got_ref))


def project(scalars, normed, normed_got, weight, query_bias, value_bias, reused, reused_got):
    local, depth = normed.shape
    width, fresh = query_bias.shape[0], value_bias.shape[0]
    blocks = local // BLOCK
    x_spec, r_spec = (row_spec(w, lambda i: jnp.minimum(i, blocks - 1)) for w in (depth, fresh))
    x_got_spec, r_got_spec = (
        row_spec(w, lambda i: jnp.maximum(i - blocks, 0)) for w in (depth, fresh)
    )
    out_spec = pl.BlockSpec(
        (BLOCK, width),
        lambda i, scalars: (lax.rem(i + scalars[SIDE] * blocks, 2 * blocks), 0),
    )
    return call(
        project_kernel,
        scalars,
        [normed, normed_got, weight, query_bias[None], value_bias[None], reused, reused_got],
        [shape((2 * local, width), BF16)] * 3,
        [x_spec, x_got_spec, None, None, None, r_spec, r_got_spec],
        [out_spec] * 3,
        (2 * blocks,),
        micros=4,
    )


def mix_kernel(
    scalars, keep_ref, got_ref, w_ref, w_other_ref, x_ref, ob_ref, gain_ref, bias_ref, mid_ref, out_ref
):
    attention = dot(keep_ref[...], w_ref[...]) + dot(got_ref[...], w_other_ref[...])
    middle = x_ref[...].astype(F32) + attention + ob_ref[...]
    mid_ref[...] = middle
    unit, _ = unit_rows(middle)
    out_ref[...] = (unit * gain_ref[...] + bias_ref[...]).astype(BF16)


def mix(scalars, keep, got, w_out, w_out_other, tokens, out_bias, gain, bias):
    rows, width = tokens.shape
    half, whole = row_spec(got.shape[1]), row_spec(width)
    kept = pl.BlockSpec((None, BLOCK, got.shape[1]), lambda i, scalars: (0, i, 0))
    return call(
        mix_kernel,
        scalars,
        [keep, got, w_out, w_out_other, tokens, out_bias[None], gain[None], bias[None]],
        [shape((rows, width), F32), shape((rows, width), BF16)],
        [kept, half, None, None, whole, None, None, None],
        [whole, whole],
        (rows // BLOCK,),
        micros=3,
    )


def turn_kernel(
    scalars,
    mid_ref,
    cot_ref,
    back_ref,
    back_got_ref,
    gain_ref,
    w_ref,
    w_other_ref,
    mid_grad_ref,
    grad_ref,
    own_ref,
    send_ref,
    sums_ref,
):
    block = pl.program_id(0)
    rows = pl.num_programs(0) * BLOCK
    out_grad = cot_ref[...].astype(F32) * valid_rows(scalars, block, rows)
    unit, scale = unit_rows(mid_ref[...])
    normed_grad = back_ref[...] + back_got_ref[...].astype(F32)
    middle_grad = out_grad + unit_rows_back(unit, scale, normed_grad * gain_ref[...])
    mid_grad_ref[...] = middle_grad
    grad = middle_grad.astype(BF16)
    grad_ref[...] = grad
    own_ref[...] = dot(grad, w_ref[...], NT).astype(BF16)
    send_ref[...] = dot(grad, w_other_ref[...], NT).astype(BF16)

    @pl.when(block == 0)
    def _():
        sums_ref[...] = jnp.zeros_like(sums_ref)

    for k, part in enumerate((normed_grad * unit, normed_grad, middle_grad, out_grad)):
        sums_ref[k : k + 1, :] += column_sum(part)


def turn(scalars, middle, cotangent, back, back_got, gain, w_out, w_out_other):
    rows, width = middle.shape
    whole, half = row_spec(width), row_spec(w_out.shape[0])
    return call(
        turn_kernel,
        scalars,
        [middle, cotangent, back, back_got, gain[None], w_out, w_out_other],
        [shape((rows, width), F32), shape((rows, width), BF16)]
        + [shape((rows, w_out.shape[0]), BF16)] * 2
        + [shape((8, width), F32)],
        [whole, whole, whole, whole, None, None, None],
        [whole, whole, half, half, None],
        (rows // BLOCK,),
        micros=4,
    )


def close_kernel(
    scalars,
    x_ref,
    gain_ref,
    keep_ref,
    got_ref,
    got_late_ref,
    mid_grad_ref,
    grad_ref,
    sums_ref,
):
    unit, scale = unit_rows(x_ref[...].astype(F32))
    early = pl.program_id(0) < pl.num_programs(0) // 2
    normed_grad = keep_ref[...] + pick(early, got_ref[...], got_late_ref[...]).astype(F32)
    grad_ref[...] = mid_grad_ref[...] + unit_rows_back(unit, scale, normed_grad * gain_ref[...])

    @pl.when(pl.program_id(0) == 0)
    def _():
        sums_ref[...] = jnp.zeros_like(sums_ref)

    for k, part in enumerate((normed_grad * unit, normed_grad)):
        sums_ref[k : k + 1, :] += column_sum(part)


def close(scalars, tokens, gain, keep, got, got_late, middle_grad):
    rows, width = tokens.shape
    whole = row_spec(width)
    last = rows // BLOCK // 2 - 1
    first_half = row_spec(width, lambda i: jnp.minimum(i, last))
    second_half = row_spec(width, lambda i: jnp.maximum(i - last - 1, 0))
    return call(
        close_kernel,
        scalars,
        [tokens, gain[None], keep, got, got_late, middle_grad],
        [shape((rows, width), F32), shape((8, width), F32)],
        [whole, None, whole, first_half, second_half, whole],
        [whole, None],
        (rows // BLOCK,),
        micros=3,
    )


def score_parts(k_ref, query, begin, length, sure):
    parts = []
    for first, last in ((0, begin), (begin, begin + BLOCK)):
        if last > first:
            part = dot(k_ref[first:last, :], query, NT)
            keys = lax.broadcasted_iota(jnp.int32, part.shape, 0) + first
            if first == begin:
                queries = lax.broadcasted_iota(jnp.int32, part.shape, 1) + begin
                part = jnp.where((keys <= queries) & (keys < length), part, -1e30)
            elif last > sure:
                part = jnp.where(keys < length, part, -1e30)
            parts.append((first, last, part))
    return parts


def attend_kernel(scalars, q_ref, k_ref, v_ref, out_ref, lse_ref):
    rows = q_ref.shape[0]
    local = rows // 2
    for begin in range(0, rows, BLOCK):
        query = q_ref[begin : begin + BLOCK, :] * HD ** (-0.5)
        lane = lax.broadcasted_iota(jnp.int32, query.shape, 1)
        mixed = []
        for head in range(2):
            mine = (lane < HD) if head == 0 else (lane >= HD)
            own_query = jnp.where(mine, query, 0).astype(BF16)
            parts = score_parts(k_ref, own_query, begin, scalars[LENGTH], local)
            highest = None
            for _, _, part in parts:
                top = jnp.max(part, axis=0, keepdims=True)
                highest = top if highest is None else jnp.maximum(highest, top)
            total, mixture = 0.0, 0.0
            for first, last, part in parts:
                weights = jnp.exp(part - highest)
                total = total + column_sum(weights)
                mixture = mixture + dot(v_ref[first:last, :], weights.astype(BF16), TN)
            mixed.append(mixture * (1.0 / total))
            lse_ref[0, head : head + 1, begin : begin + BLOCK] = highest + jnp.log(total)
        row = lax.broadcasted_iota(jnp.int32, mixed[0].shape, 0)
        both = jnp.where(row < HD, mixed[0], mixed[1]).T.astype(BF16)
        away = jnp.abs(scalars[SIDE] - begin // local)
        out_ref[away, begin % local : begin % local + BLOCK, :] = both


def pair_spec(rows):
    return pl.BlockSpec((rows, 2 * HD), lambda p, scalars: (0, p))


def sides_spec(rows):
    return pl.BlockSpec((2, rows // 2, 2 * HD), lambda p, scalars: (0, 0, p))


def attend(scalars, queries, keys, values):
    rows, width = queries.shape
    pairs = width // (2 * HD)
    return call(
        attend_kernel,
        scalars,
        [queries, keys, values],
        [shape((2, rows // 2, width), BF16), shape((pairs, 2, rows), F32)],
        [pair_spec(rows)] * 3,
        [sides_spec(rows), pl.BlockSpec((1, 2, rows), lambda p, scalars: (p, 0, 0))],
        (pairs,),
        micros=10,
    )


def attend_back_kernel(
    scalars,
    q_ref,
    k_ref,
    v_ref,
    out_ref,
    lse_ref,
    grad_ref,
    grad_got_ref,
    dq_ref,
    dk_ref,
    dv_ref,
    dk_sum,
    dv_sum,
):
    rows = q_ref.shape[0]
    local = rows // 2
    dk_sum[...] = jnp.zeros_like(dk_sum)
    dv_sum[...] = jnp.zeros_like(dv_sum)
    for begin in range(0, rows, BLOCK):
        block = slice(begin, begin + BLOCK)
        place = slice(begin % local, begin % local + BLOCK)
        here = scalars[SIDE] == begin // local
        query = q_ref[block, :] * HD ** (-0.5)
        grad = pick(here, grad_ref[place, :], grad_got_ref[place, :])
        mixed = out_ref[jnp.abs(scalars[SIDE] - begin // local), place, :]
        product = (grad.astype(F32) * mixed.astype(F32)).T
        lane = lax.broadcasted_iota(jnp.int32, query.shape, 1)
        found = []
        for head in range(2):
            mine = (lane < HD) if head == 0 else (lane >= HD)
            own_query = jnp.where(mine, query, 0).astype(BF16)
            own_grad = jnp.where(mine, grad, 0).astype(BF16)
            inner = column_sum(product[head * HD : (head + 1) * HD, :])
            lse = lse_ref[0, head : head + 1, block]
            query_grad = 0.0
            for first, last, part in score_parts(k_ref, own_query, begin, scalars[LENGTH], local):
                chances = jnp.exp(part - lse)
                chance_grad = dot(v_ref[first:last, :], own_grad, NT)
                score_grad = (chances * (chance_grad - inner)).astype(BF16)
                dv_sum[first:last, :] += dot(chances.astype(BF16), own_grad)
                dk_sum[first:last, :] += dot(score_grad, own_query)
                query_grad = query_grad + dot(k_ref[first:last, :], score_grad, TN)
            found.append(query_grad)
        row = lax.broadcasted_iota(jnp.int32, found[0].shape, 0)
        both = jnp.where(row < HD, found[0], found[1]) * HD ** (-0.5)
        dq_ref[block, :] = both.T.astype(BF16)
    dk_ref[...] = dk_sum[...].astype(BF16)
    dv_ref[...] = dv_sum[...].astype(BF16)


def attend_back(scalars, queries, keys, values, heads_out, lse, grad, grad_got):
    rows, width = queries.shape
    pairs = width // (2 * HD)
    half = pair_spec(rows // 2)
    return call(
        attend_back_kernel,
        scalars,
        [queries, keys, values, heads_out, lse, grad, grad_got],
        [shape((rows, width), BF16)] * 3,
        [pair_spec(rows)] * 3
        + [sides_spec(rows), pl.BlockSpec((1, 2, rows), lambda p, scalars: (p, 0, 0)), half, half],
        [pair_spec(rows)] * 3,
        (pairs,),
        [pltpu.VMEM((rows, 2 * HD), F32)] * 2,
        micros=14,
    )


def gelu_parts(hidden):
    rate = 0.7978845608028654
    square = hidden * hidden
    bend = jnp.tanh(rate * hidden * (1.0 + 0.044715 * square))
    lift = 0.5 * (1.0 + bend)
    slope = lift + 0.5 * hidden * (1.0 - bend * bend) * (rate * (1.0 + 3 * 0.044715 * square))
    return hidden * lift, slope


def feed_kernel(
    scalars,
    normed_ref,
    grad_ref,
    up_ref,
    bias_ref,
    down_ref,
    branch_ref,
    back_ref,
    active_ref,
    hidden_grad_ref,
    bias_grad_ref,
    branch_sum,
    back_sum,
):
    normed, grad = normed_ref[...], grad_ref[...]
    up, down = up_ref[...], down_ref[...]
    active, slope = gelu_parts(dot(normed, up) + bias_ref[...])
    active = active.astype(BF16)
    hidden_grad = (dot(grad, down, NT) * slope).astype(BF16)
    branch, back = dot(active, down), dot(hidden_grad, up, NT)
    active_ref[...] = active
    hidden_grad_ref[...] = hidden_grad
    bias_grad_ref[...] = column_sum(hidden_grad.astype(F32))
    step, last = pl.program_id(0), pl.num_programs(0) - 1

    @pl.when(step == 0)
    def _():
        branch_sum[...] = branch
        back_sum[...] = back

    @pl.when((step > 0) & (step < last))
    def _():
        branch_sum[...] += branch
        back_sum[...] += back

    @pl.when(step == last)
    def _():
        branch_ref[...] = (branch_sum[...] + branch).astype(branch_ref.dtype)
        back_ref[...] = (back_sum[...] + back).astype(back_ref.dtype)


def feed(scalars, normed, grad, w_up, up_bias, w_down, dtype):
    rows, width = normed.shape
    hidden = w_down.shape[0]
    tile = 2 * BLOCK
    part = pl.BlockSpec((rows, tile), lambda i, scalars: (0, i))
    line = pl.BlockSpec((1, tile), lambda i, scalars: (0, i))
    return call(
        feed_kernel,
        scalars,
        [normed, grad, w_up, up_bias[None], w_down],
        [shape((rows, width), dtype)] * 2
        + [shape((rows, hidden), BF16)] * 2
        + [shape((1, hidden), F32)],
        [
            None,
            None,
            pl.BlockSpec((width, tile), lambda i, scalars: (0, i)),
            line,
            pl.BlockSpec((tile, width), lambda i, scalars: (i, 0)),
        ],
        [None, None, part, part, line],
        (hidden // tile,),
        [pltpu.VMEM((rows, width), F32)] * 2,
        micros=10,
    )


def feed_weights_kernel(scalars, *refs):
    actives, hidden_grads, normeds, grads = refs[0:2], refs[2:4], refs[4:6], refs[6:8]
    step = pl.program_id(0)
    per_part = pl.num_programs(0) // PARTS
    down = sum(dot(a[...], g[...], TN) for a, g in zip(actives, grads)).astype(BF16)
    up = sum(dot(n[...], h[...], TN) for n, h in zip(normeds, hidden_grads)).astype(BF16)
    for k in range(PARTS * per_part):
        keep_ref, send_ref = refs[8 + k // per_part * 2 : 10 + k // per_part * 2]
        lines = slice(k % per_part * BLOCK, (k % per_part + 1) * BLOCK)

        @pl.when((step == k) & (scalars[CORE] == 0))
        def _():
            keep_ref[0, lines, :] = down
            send_ref[0, :, lines] = up

        @pl.when((step == k) & (scalars[CORE] == 1))
        def _():
            send_ref[0, lines, :] = down
            keep_ref[0, :, lines] = up


def feed_weights(scalars, actives, hidden_grads, normeds, grads):
    rows, width = normeds[0].shape
    hidden = actives[0].shape[1]
    part = pl.BlockSpec((rows, BLOCK), lambda i, scalars: (0, i))
    return call(
        feed_weights_kernel,
        scalars,
        [*actives, *hidden_grads, *normeds, *grads],
        [shape((1, hidden // PARTS, width), BF16)] * (2 * PARTS),
        [part] * 4 + [None] * 4,
        None,
        (hidden // BLOCK,),
        micros=10,
    )


def fresh_columns(values):
    return jnp.concatenate(
        [values[:, k * HD : (k + 1) * HD] for k in range(0, values.shape[1] // HD, 2)], axis=1
    )


def reused_columns(values):
    return jnp.concatenate(
        [values[:, k * HD : (k + 1) * HD] for k in range(1, values.shape[1] // HD, 2)], axis=1
    )


def last_weights_kernel(
    scalars, x_ref, x_got_ref, dq_ref, dk_ref, dv_ref, wo_ref, wo_got_ref, keep_ref, send_ref, q_sum_ref, v_sum_ref
):
    size, half = dq_ref.shape[1], wo_ref.shape[1] // 2
    local = x_ref.shape[0]
    sides = (scalars[SIDE], 1 - scalars[SIDE])
    spans = [pl.ds(pl.multiple_of(s * local, local), local) for s in sides]
    xs = (x_ref, x_got_ref)
    fresh = [fresh_columns(dv_ref[s, :]) for s in spans]
    for out_ref, h in ((keep_ref, scalars[CORE]), (send_ref, 1 - scalars[CORE])):
        lines = pl.ds(pl.multiple_of(h * half, half), half)
        wo = wo_ref[:, lines] + wo_got_ref[:, lines].astype(F32)
        out_ref[0, :, :half] = wo.astype(BF16)
        for k, d_ref in enumerate((dq_ref, dk_ref)):
            total = sum(dot(x[:, lines], d_ref[s, :], TN) for x, s in zip(xs, spans))
            out_ref[0, :, half + k * size : half + (k + 1) * size] = total.astype(BF16)
        total = sum(dot(x[:, lines], f, TN) for x, f in zip(xs, fresh)).astype(BF16)
        padding = out_ref.shape[2] - half - 2 * size - total.shape[1]
        out_ref[0, :, half + 2 * size :] = jnp.pad(total, ((0, 0), (0, padding)))
    q_sum_ref[...] = column_sum(dq_ref[...].astype(F32))
    v_sum_ref[...] = sum(column_sum(f.astype(F32)) for f in fresh)


def last_weights(scalars, normed, normed_got, query_grad, key_grad, value_grad, wo, wo_got):
    width, size = normed.shape[1], query_grad.shape[1]
    columns = -(-(width // 2 + 5 * size // 2) // 128) * 128
    return call(
        last_weights_kernel,
        scalars,
        [normed, normed_got, query_grad, key_grad, value_grad, wo, wo_got],
        [shape((1, width // 2, columns), BF16)] * 2
        + [shape((1, size), F32), shape((1, size // 2), F32)],
        micros=4,
    )


def inputs_back_kernel(scalars, *refs):
    w_ref, keep_ref, send_ref, keep_reused_ref, send_reused_ref = refs[6:]
    for (dq_ref, dk_ref, dv_ref), out_ref, reused_ref in (
        (refs[0:3], keep_ref, keep_reused_ref),
        (refs[3:6], send_ref, send_reused_ref),
    ):
        size = dq_ref.shape[1]
        total = dot(dq_ref[...], w_ref[:, :size], NT)
        total = total + dot(dk_ref[...], w_ref[:, size : 2 * size], NT)
        total = total + dot(fresh_columns(dv_ref[...]), w_ref[:, 2 * size :], NT)
        out_ref[...] = total.astype(out_ref.dtype)
        reused_ref[...] = reused_columns(dv_ref[...])


def inputs_back(scalars, query_grad, key_grad, value_grad, w_in):
    rows, size = query_grad.shape
    half, width = rows // 2, w_in.shape[0]
    blocks = half // BLOCK
    keep = pl.BlockSpec((BLOCK, size), lambda i, scalars: (scalars[SIDE] * blocks + i, 0))
    send = pl.BlockSpec((BLOCK, size), lambda i, scalars: ((1 - scalars[SIDE]) * blocks + i, 0))
    grads = [query_grad, key_grad, value_grad]
    return call(
        inputs_back_kernel,
        scalars,
        [*grads, *grads, w_in],
        [shape((half, width), F32), shape((half, width), BF16)]
        + [shape((half, size // 2), BF16)] * 2,
        [keep] * 3 + [send] * 3 + [None],
        [row_spec(width)] * 2 + [row_spec(size // 2)] * 2,
        (blocks,),
        micros=4,
    )


def feed_out_kernel(scalars, *refs):
    down_ref, up_ref = refs[-2:]
    first = scalars[CORE] == 0
    for part in range(PARTS):
        own_ref, got_ref = refs[2 * part : 2 * part + 2]

        @pl.when(pl.program_id(0) == part)
        def _():
            own, got = own_ref[0].astype(F32), got_ref[0].astype(F32)
            down_ref[...] = jnp.where(first, own, got)
            up_ref[...] = jnp.where(first, got, own)


def feed_out(scalars, chains):
    arrays = [a for chain in chains for a in (chain.sends[0], chain.gots[0])]
    _, rows, width = arrays[0].shape
    return call(
        feed_out_kernel,
        scalars,
        arrays,
        [shape((PARTS * rows, width), F32), shape((width, PARTS * rows), F32)],
        None,
        [
            pl.BlockSpec((rows, width), lambda i, scalars: (i, 0)),
            pl.BlockSpec((width, rows), lambda i, scalars: (0, i)),
        ],
        (PARTS,),
        micros=5,
    )


def last_out_kernel(scalars, own_ref, got_ref, wo_ref, wq_ref, wk_ref, wv_ref):
    half = own_ref.shape[0]
    size = wq_ref.shape[1]
    first = scalars[CORE] == 0
    own, got = own_ref[...].astype(F32), got_ref[...].astype(F32)
    for h, part in enumerate((jnp.where(first, own, got), jnp.where(first, got, own))):
        lines = slice(h * half, (h + 1) * half)
        wo_ref[:, lines] = part[:, :half]
        wq_ref[lines, :] = part[:, half : half + size]
        wk_ref[lines, :] = part[:, half + size : half + 2 * size]
        wv_ref[:, lines] = part[:, half + 2 * size : half + 2 * size + size // 2].T


def last_out(scalars, chain, size):
    own, got = chain.sends[0][0], chain.gots[0][0]
    half = own.shape[0]
    return call(
        last_out_kernel,
        scalars,
        [own, got],
        [shape((size, 2 * half), F32)]
        + [shape((2 * half, size), F32)] * 2
        + [shape((size // 2, 2 * half), F32)],
        micros=3,
    )


def shards(
    tokens,
    first_values,
    lengths,
    reuse_index,
    ln1_gain,
    ln1_bias,
    w_query,
    query_bias,
    w_key,
    w_value,
    value_bias,
    w_out,
    out_bias,
    ln2_gain,
    ln2_bias,
    w_up,
    up_bias,
    w_down,
    down_bias,
    cotangent,
):
    place, side = lax.axis_index("dp"), lax.axis_index("tensor")
    core = place % 2
    local_rows, width = tokens.shape
    query_size, value_size = query_bias.shape[0], value_bias.shape[0]
    length = lengths[0]
    scalars = jnp.stack([side, length, core]).astype(jnp.int32)
    positions = jnp.arange(local_rows)[:, None]
    own_valid = side * local_rows + positions < length
    other_valid = (1 - side) * local_rows + positions < length

    early, late = cotangent[: local_rows // 2], cotangent[local_rows // 2 :]
    normed_one = norm(scalars, tokens, ln1_gain, ln1_bias)
    one_got = across(normed_one)
    picks = reuse_index[jnp.arange(2 * value_size) // HD]
    selector = (
        (jnp.arange(width)[:, None] // HD == picks[None, :])
        & ((jnp.arange(width) % HD)[:, None] == (jnp.arange(2 * value_size) % HD)[None, :])
    ).astype(BF16)
    first_values, selector = after((first_values, selector), normed_one)
    chosen = dot(first_values, selector).astype(BF16)
    own_chosen, other_chosen = slabs(chosen, side)
    chosen_got = across(other_chosen)
    w_in = jnp.concatenate([w_query, w_key, w_value], axis=1)
    branch_grad = jnp.where(own_valid, cotangent, 0)
    out_piece = halves(w_out, core)[0]
    one_got, chosen_got, w_in, branch_grad, out_piece, early, late = lax.optimization_barrier(
        (one_got, chosen_got, w_in, branch_grad, out_piece, early, late)
    )
    out_got = across(out_piece)
    early_got = across(early)
    queries, keys, values = project(
        scalars, normed_one, one_got, w_in, query_bias, value_bias, own_chosen, chosen_got
    )
    heads_out, lse = attend(scalars, queries, keys, values)
    heads_out, out_got, early_got = lax.optimization_barrier((heads_out, out_got, early_got))
    heads_got = across(heads_out[1])
    w_out_other = join(out_got, flip(out_got, 1), core)
    heads_got, w_out_other, late = lax.optimization_barrier((heads_got, w_out_other, late))
    middle, normed_two = mix(
        scalars, heads_out, heads_got, w_out, w_out_other, tokens, out_bias, ln2_gain, ln2_bias
    )

    normed_two, late = lax.optimization_barrier((normed_two, late))
    two_got = across(normed_two)
    late_got = across(late)
    own = feed(scalars, normed_two, branch_grad, w_up, up_bias, w_down, F32)
    two_got, late_got, own = lax.optimization_barrier((two_got, late_got, own))
    branch_grad_got = jnp.where(other_valid, jnp.concatenate([early_got, late_got], axis=0), 0)
    other = feed(scalars, two_got, branch_grad_got, w_up, up_bias, w_down, BF16)
    up_bias_grad = (own[4] + other[4])[0]
    back_got = across(other[1])
    parts = feed_weights(
        scalars,
        (own[2], other[2]),
        (own[3], other[3]),
        (normed_two, two_got),
        (branch_grad, branch_grad_got),
    )
    chains = [Chain(*parts[2 * k : 2 * k + 2], 1, place, False) for k in range(PARTS)]
    branch_send = other[0]
    back_got, branch_send = hold(chains, back_got, branch_send)

    advance(chains, [1, 1])
    turned = turn(
        scalars, middle, cotangent, own[1], back_got, ln2_gain, w_out, w_out_other
    )
    middle_grad, attention_grad, heads_grad, heads_grad_send, two_sums = hold(chains, *turned)
    heads_grad_got = across(heads_grad_send)
    out_grad_send = dot(heads_got, attention_grad, TN).astype(BF16)
    out_grad_own = dot(heads_out[0], attention_grad, TN)
    advance(chains, [1, 0])
    heads_grad_got, out_grad_send, out_grad_own = hold(
        chains, heads_grad_got, out_grad_send, out_grad_own
    )
    out_grad_got = across(out_grad_send)
    query_grad, key_grad, value_grad = attend_back(
        scalars, queries, keys, values, heads_out, lse, heads_grad, heads_grad_got
    )
    advance(chains, [1, 1])
    middle_rows = local_rows // 2
    out_grad_got, query_grad, key_grad, value_grad, branch_send = hold(
        chains, out_grad_got, query_grad, key_grad, value_grad, branch_send
    )
    keep, send, query_sums, value_sums = last_weights(
        scalars, normed_one, one_got, query_grad, key_grad, value_grad, out_grad_own, out_grad_got
    )
    chains.append(Chain(keep, send, 1, place, False))

    branch_got = across(branch_send[:middle_rows])
    back_keep, back_send, first_keep, first_send = inputs_back(
        scalars, *after((query_grad, key_grad, value_grad), keep), w_in
    )
    advance(chains, [1, 1, 1])
    back_keep, back_send, first_keep, first_send, branch_send, branch_got = hold(
        chains, back_keep, back_send, first_keep, first_send, branch_send, branch_got
    )
    back_got = across(back_send[:middle_rows])
    advance(chains, [1, 1, 1])
    back_got, back_send, first_send = hold(chains, back_got, back_send, first_send)
    back_late = across(back_send[middle_rows:])
    first_got = across(first_send)
    advance(chains, [1, 1, 1])
    back_late, first_got, branch_send = hold(chains, back_late, first_got, branch_send)
    branch_late = across(branch_send[middle_rows:])
    tokens_grad, one_sums = close(
        scalars, tokens, ln1_gain, back_keep, back_got, back_late, middle_grad
    )
    advance(chains, [1, 1, 1])
    tokens_grad, one_sums, branch_late, first_got = hold(
        chains, tokens_grad, one_sums, branch_late, first_got
    )
    first_grads = jnp.concatenate(
        [jnp.where(side == 0, first_keep, first_got), jnp.where(side == 0, first_got, first_keep)],
        axis=1,
    )
    first_values_grad = dot(first_grads, selector, NT)
    whole = jnp.concatenate([one_sums[:2], two_sums[2:3], two_sums[:2], two_sums[3:4]]).reshape(-1)
    whole = whole + across(whole)
    small = jnp.concatenate([whole, query_sums[0], value_sums[0], up_bias_grad])
    bits = dp_bits()
    small = small + flip(small, 1)
    advance(chains, [1, 1, 1])
    small, first_values_grad = hold(chains, small, first_values_grad)
    small = small + flip(small, bits[1])
    small = small + flip(small, bits[2])
    advance(chains, [0, 1, 1])
    small = hold(chains, small)
    for bit in bits[3:]:
        small = small + flip(small, bit)
    branch_all = jnp.concatenate([branch_got, branch_late], axis=0).astype(F32)
    result = (middle + own[0] + branch_all + down_bias) * own_valid.astype(F32)
    result = result.astype(BF16)
    advance(chains, [99, 99, len(chains[2].steps) - 1])
    w_down_grad, w_up_grad = feed_out(scalars, chains[:PARTS])
    chains[-1].state, w_down_grad, w_up_grad, small, result = lax.optimization_barrier(
        (chains[-1].state, w_down_grad, w_up_grad, small, result)
    )
    advance(chains, [0, 0, 1])
    w_out_grad, w_query_grad, w_key_grad, w_value_grad = last_out(scalars, chains[-1], query_size)
    w_value_grad = w_value_grad.T
    ln1_gain_grad, ln1_bias_grad, out_bias_grad, ln2_gain_grad, ln2_bias_grad, down_bias_grad = (
        small[k * width : (k + 1) * width] for k in range(6)
    )
    query_bias_grad = small[6 * width : 6 * width + query_size]
    value_bias_grad = small[6 * width + query_size : 6 * width + query_size + value_size]
    up_bias_grad = small[6 * width + query_size + value_size :]
    return (
        result,
        tokens_grad,
        first_values_grad,
        ln1_gain_grad,
        ln1_bias_grad,
        w_query_grad,
        query_bias_grad,
        w_key_grad,
        w_value_grad,
        value_bias_grad,
        w_out_grad,
        out_bias_grad,
        ln2_gain_grad,
        ln2_bias_grad,
        w_up_grad,
        up_bias_grad,
        w_down_grad,
        down_bias_grad,
    )


def solution(mesh):
    in_specs = (
        P(("dp", "tensor"), None),
        P(("dp", "tensor"), None),
        P("dp"),
        P(),
        P(),
        P(),
        P(None, "tensor"),
        P("tensor"),
        P(None, "tensor"),
        P(None, "tensor"),
        P("tensor"),
        P("tensor", None),
        P(),
        P(),
        P(),
        P(None, "tensor"),
        P("tensor"),
        P("tensor", None),
        P(),
        P(("dp", "tensor"), None),
    )
    out_specs = (
        P(("dp", "tensor"), None),
        P(("dp", "tensor"), None),
        P(("dp", "tensor"), None),
        P(),
        P(),
        P(None, "tensor"),
        P("tensor"),
        P(None, "tensor"),
        P(None, "tensor"),
        P("tensor"),
        P("tensor", None),
        P(),
        P(),
        P(),
        P(None, "tensor"),
        P("tensor"),
        P("tensor", None),
        P(),
    )
    return jax.shard_map(shards, mesh=mesh, in_specs=in_specs, out_specs=out_specs, check_vma=False)
```

```python
from functools import partial

import jax
import jax.numpy as jnp
from jax import lax
from jax.experimental import pallas as pl
from jax.experimental.pallas import tpu as pltpu
from jax.sharding import PartitionSpec as P

H = 12
HD = 64
PARTS = 2
BLOCK = 256
VMEM_BYTES = 32 * 1024 * 1024
NT = (((1,), (1,)), ((), ()))
TN = (((0,), (0,)), ((), ()))
NN = (((1,), (0,)), ((), ()))
F32 = jnp.float32
BF16 = jnp.bfloat16
STRETCH = 15
SIDE, LENGTH, CORE, WHICH = 0, 1, 2, 3


def shape(dims, dtype):
    return jax.ShapeDtypeStruct(dims, dtype)


def call(kernel, scalars, arrays, out_shape, in_specs=None, out_specs=None, grid=(1,), scratch=(), micros=2):
    def whole(array):
        return pl.BlockSpec(array.shape, lambda *_, dims=len(array.shape): (0,) * dims)

    return pl.pallas_call(
        kernel,
        grid_spec=pltpu.PrefetchScalarGridSpec(
            num_scalar_prefetch=1,
            grid=grid,
            in_specs=[s or whole(a) for s, a in zip(in_specs or [None] * len(arrays), arrays)],
            out_specs=[
                s or whole(o) for s, o in zip(out_specs or [None] * len(out_shape), out_shape)
            ],
            scratch_shapes=list(scratch),
        ),
        out_shape=out_shape,
        compiler_params=pltpu.CompilerParams(vmem_limit_bytes=VMEM_BYTES),
        cost_estimate=pl.CostEstimate(
            flops=STRETCH * micros * 1_150_000_000,
            bytes_accessed=STRETCH * micros * 3_600_000,
            transcendentals=0,
        ),
    )(scalars, *arrays)


def dot(left, right, dims=NN):
    return lax.dot_general(left, right, dims, preferred_element_type=F32)


def pick(flag, left, right):
    return jnp.where(flag, left.astype(F32), right.astype(F32)).astype(left.dtype)


def across(values):
    return lax.ppermute(values, "tensor", [(0, 1), (1, 0)])


def flip(values, bit):
    return lax.ppermute(values, "dp", [(d, d ^ bit) for d in range(lax.axis_size("dp"))])


def halves(values, which):
    half = values.shape[0] // 2
    return (
        lax.dynamic_slice_in_dim(values, which * half, half, 0),
        lax.dynamic_slice_in_dim(values, (1 - which) * half, half, 0),
    )


def join(own, other, which):
    return jnp.concatenate(
        [jnp.where(which == 0, own, other), jnp.where(which == 0, other, own)], axis=0
    )


def slabs(values, which):
    half = values.shape[1] // 2
    return (
        lax.dynamic_slice_in_dim(values, which * half, half, 1),
        lax.dynamic_slice_in_dim(values, (1 - which) * half, half, 1),
    )


def after(values, *found):
    return lax.optimization_barrier((values, found))[0]


def dp_bits():
    return [1 << k for k in range(lax.axis_size("dp").bit_length() - 1)]


def fold_kernel(scalars, own_ref, got_ref, keep_ref, send_ref):
    half = keep_ref.shape[0]
    which = scalars[0]
    for out_ref, part in ((keep_ref, which), (send_ref, 1 - which)):
        rows = pl.ds(pl.multiple_of(part * half, half), half)
        out_ref[...] = (own_ref[rows, :].astype(F32) + got_ref[rows, :].astype(F32)).astype(BF16)


def join_kernel(scalars, own_ref, got_ref, out_ref):
    half = own_ref.shape[0]
    which = scalars[0]
    for in_ref, part in ((own_ref, which), (got_ref, 1 - which)):
        out_ref[pl.ds(pl.multiple_of(part * half, half), half), :] = in_ref[...]


class Chain:
    def __init__(self, keep, send, place):
        self.state, self.place, self.pending = (keep, send), place, None
        bits = dp_bits()
        self.steps = [("halve", bit, later) for bit, later in zip(bits, bits[1:] + [0])]
        self.steps += [("double", bit, 0) for bit in reversed(bits)]

    def which(self, bit):
        return (self.place // bit) % 2

    def send(self):
        self.merge()
        if self.steps:
            self.pending = self.steps.pop(0)
            self.state += (flip(self.state[-1], self.pending[1]),)

    def merge(self):
        if not self.pending:
            return
        (kind, bit, following), self.pending = self.pending, None
        own, got = self.state[0], self.state[-1]
        rows, columns = got.shape
        which = self.which(following if kind == "halve" else bit)[None]
        if kind == "double" and bit == 1:
            return
        if kind == "double" and rows % 16 == 0:
            out = [shape((2 * rows, columns), BF16)]
            self.state = tuple(call(join_kernel, which, [own, got], out))
        elif kind == "double":
            self.state = (join(own, got, which[0]),)
        elif following and rows % 32 == 0:
            out = [shape((rows // 2, columns), BF16)] * 2
            self.state = tuple(call(fold_kernel, which, [own, got], out))
        else:
            total = (own.astype(F32) + got.astype(F32)).astype(BF16)
            self.state = halves(total, which[0]) if following else (total,)

    def step(self):
        self.send()
        self.merge()


def advance(chains, counts):
    for chain, count in zip(chains, counts):
        for _ in range(count):
            chain.step()


def hold(chains, *values):
    states, values = lax.optimization_barrier(([c.state for c in chains], values))
    for chain, state in zip(chains, states):
        chain.state = state
    return values if len(values) != 1 else values[0]


def unit_rows(values):
    centred = values - jnp.mean(values, axis=-1, keepdims=True)
    spread = jnp.mean(centred * centred, axis=-1, keepdims=True)
    scale = lax.rsqrt(spread + 1e-05)
    return centred * scale, scale


def unit_rows_back(unit, scale, grad):
    inner = jnp.mean(grad * unit, axis=-1, keepdims=True)
    return scale * (grad - jnp.mean(grad, axis=-1, keepdims=True) - unit * inner)


def column_sum(values):
    return jnp.sum(values, axis=0, keepdims=True)


def row_spec(width, place=lambda i: i):
    return pl.BlockSpec((BLOCK, width), lambda i, scalars: (place(i), 0))


def valid_rows(scalars, block, rows):
    position = scalars[SIDE] * rows + block * BLOCK
    position = position + lax.broadcasted_iota(jnp.int32, (BLOCK, 1), 0)
    return (position < scalars[LENGTH]).astype(F32)


def norm_kernel(scalars, x_ref, gain_ref, bias_ref, out_ref):
    unit, _ = unit_rows(x_ref[...].astype(F32))
    out_ref[...] = (unit * gain_ref[...] + bias_ref[...]).astype(BF16)


def norm(scalars, values, gain, bias):
    rows, width = values.shape
    return call(
        norm_kernel,
        scalars,
        [values, gain[None], bias[None]],
        [shape((rows, width), BF16)],
        [row_spec(width), None, None],
        [row_spec(width)],
        (rows // BLOCK,),
    )[0]


def project_kernel(
    scalars, x_ref, x_got_ref, w_ref, qb_ref, vb_ref, reused_ref, reused_got_ref, q_ref, k_ref, v_ref
):
    width, fresh = q_ref.shape[1], vb_ref.shape[1]
    own = pl.program_id(0) < pl.num_programs(0) // 2

    def work(x_ref, reused_ref):
        found = dot(x_ref[...], w_ref[...])
        q_ref[...] = (found[:, :width] + qb_ref[...]).astype(BF16)
        k_ref[...] = found[:, width : 2 * width].astype(BF16)
        values = (found[:, 2 * width :] + vb_ref[...]).astype(BF16)
        reused = reused_ref[...]
        for head in range(fresh // HD):
            part = slice(head * HD, (head + 1) * HD)
            v_ref[:, 2 * head * HD : 2 * (head + 1) * HD] = jnp.concatenate(
                [values[:, part], reused[:, part]], axis=1
            )

    pl.when(own)(lambda: work(x_ref, reused_ref))
    pl.when(jnp.logical_not(own))(lambda: work(x_got_ref, reused_got_ref))


def project(scalars, normed, normed_got, weight, query_bias, value_bias, reused, reused_got):
    local, depth = normed.shape
    width, fresh = query_bias.shape[0], value_bias.shape[0]
    blocks = local // BLOCK
    x_spec, r_spec = (row_spec(w, lambda i: jnp.minimum(i, blocks - 1)) for w in (depth, fresh))
    x_got_spec, r_got_spec = (
        row_spec(w, lambda i: jnp.maximum(i - blocks, 0)) for w in (depth, fresh)
    )
    out_spec = pl.BlockSpec(
        (BLOCK, width),
        lambda i, scalars: (lax.rem(i + scalars[SIDE] * blocks, 2 * blocks), 0),
    )
    return call(
        project_kernel,
        scalars,
        [normed, normed_got, weight, query_bias[None], value_bias[None], reused, reused_got],
        [shape((2 * local, width), BF16)] * 3,
        [x_spec, x_got_spec, None, None, None, r_spec, r_got_spec],
        [out_spec] * 3,
        (2 * blocks,),
        micros=4,
    )


def mix_kernel(
    scalars, keep_ref, got_ref, w_ref, w_other_ref, x_ref, ob_ref, gain_ref, bias_ref, mid_ref, out_ref
):
    attention = dot(keep_ref[...], w_ref[...]) + dot(got_ref[...], w_other_ref[...])
    middle = x_ref[...].astype(F32) + attention + ob_ref[...]
    mid_ref[...] = middle
    unit, _ = unit_rows(middle)
    out_ref[...] = (unit * gain_ref[...] + bias_ref[...]).astype(BF16)


def mix(scalars, keep, got, w_out, w_out_other, tokens, out_bias, gain, bias):
    rows, width = tokens.shape
    half, whole = row_spec(got.shape[1]), row_spec(width)
    kept = pl.BlockSpec((None, BLOCK, got.shape[1]), lambda i, scalars: (0, i, 0))
    return call(
        mix_kernel,
        scalars,
        [keep, got, w_out, w_out_other, tokens, out_bias[None], gain[None], bias[None]],
        [shape((rows, width), F32), shape((rows, width), BF16)],
        [kept, half, None, None, whole, None, None, None],
        [whole, whole],
        (rows // BLOCK,),
        micros=3,
    )


def turn_kernel(
    scalars,
    mid_ref,
    cot_ref,
    back_ref,
    back_got_ref,
    gain_ref,
    w_ref,
    w_other_ref,
    mid_grad_ref,
    grad_ref,
    own_ref,
    send_ref,
    sums_ref,
):
    block = pl.program_id(0)
    rows = pl.num_programs(0) * BLOCK
    out_grad = cot_ref[...].astype(F32) * valid_rows(scalars, block, rows)
    unit, scale = unit_rows(mid_ref[...])
    normed_grad = back_ref[...] + back_got_ref[...].astype(F32)
    middle_grad = out_grad + unit_rows_back(unit, scale, normed_grad * gain_ref[...])
    mid_grad_ref[...] = middle_grad
    grad = middle_grad.astype(BF16)
    grad_ref[...] = grad
    own_ref[...] = dot(grad, w_ref[...], NT).astype(BF16)
    send_ref[...] = dot(grad, w_other_ref[...], NT).astype(BF16)

    @pl.when(block == 0)
    def _():
        sums_ref[...] = jnp.zeros_like(sums_ref)

    for k, part in enumerate((normed_grad * unit, normed_grad, middle_grad, out_grad)):
        sums_ref[k : k + 1, :] += column_sum(part)


def turn(scalars, middle, cotangent, back, back_got, gain, w_out, w_out_other):
    rows, width = middle.shape
    whole, half = row_spec(width), row_spec(w_out.shape[0])
    return call(
        turn_kernel,
        scalars,
        [middle, cotangent, back, back_got, gain[None], w_out, w_out_other],
        [shape((rows, width), F32), shape((rows, width), BF16)]
        + [shape((rows, w_out.shape[0]), BF16)] * 2
        + [shape((8, width), F32)],
        [whole, whole, whole, whole, None, None, None],
        [whole, whole, half, half, None],
        (rows // BLOCK,),
        micros=4,
    )


def close_kernel(
    scalars,
    x_ref,
    gain_ref,
    keep_ref,
    got_ref,
    got_late_ref,
    mid_grad_ref,
    grad_ref,
    sums_ref,
):
    unit, scale = unit_rows(x_ref[...].astype(F32))
    early = pl.program_id(0) < pl.num_programs(0) // 2
    normed_grad = keep_ref[...] + pick(early, got_ref[...], got_late_ref[...]).astype(F32)
    grad_ref[...] = mid_grad_ref[...] + unit_rows_back(unit, scale, normed_grad * gain_ref[...])

    @pl.when(pl.program_id(0) == 0)
    def _():
        sums_ref[...] = jnp.zeros_like(sums_ref)

    for k, part in enumerate((normed_grad * unit, normed_grad)):
        sums_ref[k : k + 1, :] += column_sum(part)


def close(scalars, tokens, gain, keep, got, got_late, middle_grad):
    rows, width = tokens.shape
    whole = row_spec(width)
    last = rows // BLOCK // 2 - 1
    first_half = row_spec(width, lambda i: jnp.minimum(i, last))
    second_half = row_spec(width, lambda i: jnp.maximum(i - last - 1, 0))
    return call(
        close_kernel,
        scalars,
        [tokens, gain[None], keep, got, got_late, middle_grad],
        [shape((rows, width), F32), shape((8, width), F32)],
        [whole, None, whole, first_half, second_half, whole],
        [whole, None],
        (rows // BLOCK,),
        micros=3,
    )


def score_parts(k_ref, query, begin, length, sure):
    parts = []
    for first, last in ((0, begin), (begin, begin + BLOCK)):
        if last > first:
            part = dot(k_ref[first:last, :], query, NT)
            keys = lax.broadcasted_iota(jnp.int32, part.shape, 0) + first
            if first == begin:
                queries = lax.broadcasted_iota(jnp.int32, part.shape, 1) + begin
                part = jnp.where((keys <= queries) & (keys < length), part, -1e30)
            elif last > sure:
                part = jnp.where(keys < length, part, -1e30)
            parts.append((first, last, part))
    return parts


def attend_kernel(scalars, q_ref, k_ref, v_ref, out_ref, lse_ref):
    rows = q_ref.shape[0]
    local = rows // 2
    for begin in range(0, rows, BLOCK):
        query = q_ref[begin : begin + BLOCK, :] * HD ** (-0.5)
        lane = lax.broadcasted_iota(jnp.int32, query.shape, 1)
        mixed = []
        for head in range(2):
            mine = (lane < HD) if head == 0 else (lane >= HD)
            own_query = jnp.where(mine, query, 0).astype(BF16)
            parts = score_parts(k_ref, own_query, begin, scalars[LENGTH], local)
            highest = None
            for _, _, part in parts:
                top = jnp.max(part, axis=0, keepdims=True)
                highest = top if highest is None else jnp.maximum(highest, top)
            weights = [jnp.exp(part - highest) for _, _, part in parts]
            total = sum(column_sum(w) for w in weights)
            weights = jnp.concatenate([w.astype(BF16) for w in weights], axis=0)
            mixture = dot(v_ref[: begin + BLOCK, :], weights, TN)
            mixed.append(mixture * (1.0 / total))
            lse_ref[0, head : head + 1, begin : begin + BLOCK] = highest + jnp.log(total)
        row = lax.broadcasted_iota(jnp.int32, mixed[0].shape, 0)
        both = jnp.where(row < HD, mixed[0], mixed[1]).T.astype(BF16)
        away = jnp.abs(scalars[SIDE] - begin // local)
        out_ref[away, begin % local : begin % local + BLOCK, :] = both


def pair_spec(rows):
    return pl.BlockSpec((rows, 2 * HD), lambda p, scalars: (0, p))


def sides_spec(rows):
    return pl.BlockSpec((2, rows // 2, 2 * HD), lambda p, scalars: (0, 0, p))


def attend(scalars, queries, keys, values):
    rows, width = queries.shape
    pairs = width // (2 * HD)
    return call(
        attend_kernel,
        scalars,
        [queries, keys, values],
        [shape((2, rows // 2, width), BF16), shape((pairs, 2, rows), F32)],
        [pair_spec(rows)] * 3,
        [sides_spec(rows), pl.BlockSpec((1, 2, rows), lambda p, scalars: (p, 0, 0))],
        (pairs,),
        micros=10,
    )


def attend_back_kernel(
    scalars,
    q_ref,
    k_ref,
    v_ref,
    out_ref,
    lse_ref,
    grad_ref,
    grad_got_ref,
    dq_ref,
    dk_ref,
    dv_ref,
    dk_sum,
    dv_sum,
):
    rows = q_ref.shape[0]
    local = rows // 2
    dk_sum[...] = jnp.zeros_like(dk_sum)
    dv_sum[...] = jnp.zeros_like(dv_sum)
    for begin in range(0, rows, BLOCK):
        block = slice(begin, begin + BLOCK)
        place = slice(begin % local, begin % local + BLOCK)
        here = scalars[SIDE] == begin // local
        query = q_ref[block, :] * HD ** (-0.5)
        grad = pick(here, grad_ref[place, :], grad_got_ref[place, :])
        mixed = out_ref[jnp.abs(scalars[SIDE] - begin // local), place, :]
        product = (grad.astype(F32) * mixed.astype(F32)).T
        lane = lax.broadcasted_iota(jnp.int32, query.shape, 1)
        found = []
        for head in range(2):
            mine = (lane < HD) if head == 0 else (lane >= HD)
            own_query = jnp.where(mine, query, 0).astype(BF16)
            own_grad = jnp.where(mine, grad, 0).astype(BF16)
            inner = column_sum(product[head * HD : (head + 1) * HD, :])
            lse = lse_ref[0, head : head + 1, block]
            end = begin + BLOCK
            parts = score_parts(k_ref, own_query, begin, scalars[LENGTH], local)
            chances = jnp.concatenate([jnp.exp(part - lse) for _, _, part in parts], axis=0)
            chance_grad = dot(v_ref[:end, :], own_grad, NT)
            score_grad = (chances * (chance_grad - inner)).astype(BF16)
            dv_sum[:end, :] += dot(chances.astype(BF16), own_grad)
            dk_sum[:end, :] += dot(score_grad, own_query)
            query_grad = dot(k_ref[:end, :], score_grad, TN)
            found.append(query_grad)
        row = lax.broadcasted_iota(jnp.int32, found[0].shape, 0)
        both = jnp.where(row < HD, found[0], found[1]) * HD ** (-0.5)
        dq_ref[block, :] = both.T.astype(BF16)
    dk_ref[...] = dk_sum[...].astype(BF16)
    dv_ref[...] = dv_sum[...].astype(BF16)


def attend_back(scalars, queries, keys, values, heads_out, lse, grad, grad_got):
    rows, width = queries.shape
    pairs = width // (2 * HD)
    half = pair_spec(rows // 2)
    return call(
        attend_back_kernel,
        scalars,
        [queries, keys, values, heads_out, lse, grad, grad_got],
        [shape((rows, width), BF16)] * 3,
        [pair_spec(rows)] * 3
        + [sides_spec(rows), pl.BlockSpec((1, 2, rows), lambda p, scalars: (p, 0, 0)), half, half],
        [pair_spec(rows)] * 3,
        (pairs,),
        [pltpu.VMEM((rows, 2 * HD), F32)] * 2,
        micros=14,
    )


def gelu_parts(hidden):
    rate = 0.7978845608028654
    square = hidden * hidden
    bend = jnp.tanh(rate * hidden * (1.0 + 0.044715 * square))
    lift = 0.5 * (1.0 + bend)
    slope = lift + 0.5 * hidden * (1.0 - bend * bend) * (rate * (1.0 + 3 * 0.044715 * square))
    return hidden * lift, slope


def feed_kernel(steps, scalars, normed_ref, grad_ref, up_ref, bias_ref, down_ref, *refs):
    branch_ref, back_ref, active_ref, hidden_grad_ref, bias_grad_ref, branch_sum, back_sum = refs[-7:]
    normed, grad = normed_ref[...], grad_ref[...]
    up, down = up_ref[...], down_ref[...]
    active, slope = gelu_parts(dot(normed, up) + bias_ref[...])
    active = active.astype(BF16)
    hidden_grad = (dot(grad, down, NT) * slope).astype(BF16)
    branch, back = dot(active, down), dot(hidden_grad, up, NT)
    active_ref[...] = active
    hidden_grad_ref[...] = hidden_grad
    bias_grad_ref[...] = column_sum(hidden_grad.astype(F32))
    for k in range(steps):

        @pl.when(pl.program_id(0) == k)
        def _():
            sums = refs[:-7] if k == 0 else (branch_sum, back_sum)
            outs = (branch_ref, back_ref) if k == steps - 1 else (branch_sum, back_sum)
            for n, (new, out_ref) in enumerate(zip((branch, back), outs)):
                total = new + sums[n][...] if sums else new
                out_ref[...] = total.astype(out_ref.dtype)


def feed(scalars, normed, grad, w_up, up_bias, w_down, dtype, part=0, parts=1, sums=()):
    rows, width = normed.shape
    hidden = w_down.shape[0] // parts
    tile = 3 * BLOCK
    steps = hidden // tile
    begin = part * steps
    line = pl.BlockSpec((1, tile), lambda i, scalars: (0, i))
    units = pl.BlockSpec((rows, tile), lambda i, scalars: (0, i))
    return call(
        partial(feed_kernel, steps),
        scalars,
        [normed, grad, w_up, up_bias[None], w_down, *sums],
        [shape((rows, width), dtype)] * 2
        + [shape((rows, hidden), BF16)] * 2
        + [shape((1, hidden), F32)],
        [
            None,
            None,
            pl.BlockSpec((width, tile), lambda i, scalars: (0, begin + i)),
            pl.BlockSpec((1, tile), lambda i, scalars: (0, begin + i)),
            pl.BlockSpec((tile, width), lambda i, scalars: (begin + i, 0)),
        ]
        + [None] * len(sums),
        [None, None, units, units, line],
        (steps,),
        [pltpu.VMEM((rows, width), F32)] * 2,
        micros=10 // parts,
    )


def feed_weights_kernel(scalars, *refs):
    actives, hidden_grads, normeds, grads = refs[0:2], refs[2:4], refs[4:6], refs[6:8]
    keep_ref, send_ref = refs[8:]
    step = pl.program_id(0)
    down = sum(dot(a[...], g[...], TN) for a, g in zip(actives, grads)).astype(BF16)
    up = sum(dot(n[...], h[...], TN) for n, h in zip(normeds, hidden_grads)).astype(BF16)
    for k in range(keep_ref.shape[0] // BLOCK):
        lines = slice(k * BLOCK, (k + 1) * BLOCK)

        @pl.when((step == k) & (scalars[CORE] == 0))
        def _():
            keep_ref[lines, :] = down
            send_ref[:, lines] = up

        @pl.when((step == k) & (scalars[CORE] == 1))
        def _():
            send_ref[lines, :] = down
            keep_ref[:, lines] = up


def feed_weights(scalars, part, own, other, normeds, grads):
    rows, width = normeds[0].shape
    hidden = other[2].shape[1]
    steps = hidden // BLOCK
    of_all = pl.BlockSpec((rows, BLOCK), lambda i, scalars: (0, part * steps + i))
    of_part = pl.BlockSpec((rows, BLOCK), lambda i, scalars: (0, i))
    return call(
        feed_weights_kernel,
        scalars,
        [own[2], other[2], own[3], other[3], *normeds, *grads],
        [shape((hidden, width), BF16)] * 2,
        [of_all, of_part, of_all, of_part] + [None] * 4,
        None,
        (steps,),
        micros=5,
    )


def fresh_columns(values):
    return jnp.concatenate(
        [values[:, k * HD : (k + 1) * HD] for k in range(0, values.shape[1] // HD, 2)], axis=1
    )


def reused_columns(values):
    return jnp.concatenate(
        [values[:, k * HD : (k + 1) * HD] for k in range(1, values.shape[1] // HD, 2)], axis=1
    )


def last_weights_kernel(
    scalars, x_ref, x_got_ref, dq_ref, dk_ref, dv_ref, wo_ref, wo_got_ref, keep_ref, send_ref, q_sum_ref, v_sum_ref
):
    size, half = dq_ref.shape[1], wo_ref.shape[1] // 2
    local = x_ref.shape[0]
    sides = (scalars[SIDE], 1 - scalars[SIDE])
    spans = [pl.ds(pl.multiple_of(s * local, local), local) for s in sides]
    xs = (x_ref, x_got_ref)
    fresh = [fresh_columns(dv_ref[s, :]) for s in spans]
    for out_ref, h in ((keep_ref, scalars[CORE]), (send_ref, 1 - scalars[CORE])):
        lines = pl.ds(pl.multiple_of(h * half, half), half)
        wo = wo_ref[:, lines] + wo_got_ref[:, lines].astype(F32)
        out_ref[:, :half] = wo.astype(BF16)
        for k, d_ref in enumerate((dq_ref, dk_ref)):
            total = sum(dot(x[:, lines], d_ref[s, :], TN) for x, s in zip(xs, spans))
            out_ref[:, half + k * size : half + (k + 1) * size] = total.astype(BF16)
        total = sum(dot(x[:, lines], f, TN) for x, f in zip(xs, fresh)).astype(BF16)
        padding = out_ref.shape[1] - half - 2 * size - total.shape[1]
        out_ref[:, half + 2 * size :] = jnp.pad(total, ((0, 0), (0, padding)))
    q_sum_ref[...] = column_sum(dq_ref[...].astype(F32))
    v_sum_ref[...] = sum(column_sum(f.astype(F32)) for f in fresh)


def last_weights(scalars, normed, normed_got, query_grad, key_grad, value_grad, wo, wo_got):
    width, size = normed.shape[1], query_grad.shape[1]
    columns = -(-(width // 2 + 5 * size // 2) // 128) * 128
    return call(
        last_weights_kernel,
        scalars,
        [normed, normed_got, query_grad, key_grad, value_grad, wo, wo_got],
        [shape((width // 2, columns), BF16)] * 2
        + [shape((1, size), F32), shape((1, size // 2), F32)],
        micros=4,
    )


def inputs_back_kernel(scalars, *refs):
    w_ref, keep_ref, send_ref, keep_reused_ref, send_reused_ref = refs[6:]
    for (dq_ref, dk_ref, dv_ref), out_ref, reused_ref in (
        (refs[0:3], keep_ref, keep_reused_ref),
        (refs[3:6], send_ref, send_reused_ref),
    ):
        size = dq_ref.shape[1]
        total = dot(dq_ref[...], w_ref[:, :size], NT)
        total = total + dot(dk_ref[...], w_ref[:, size : 2 * size], NT)
        total = total + dot(fresh_columns(dv_ref[...]), w_ref[:, 2 * size :], NT)
        out_ref[...] = total.astype(out_ref.dtype)
        reused_ref[...] = reused_columns(dv_ref[...])


def inputs_back(scalars, query_grad, key_grad, value_grad, w_in):
    rows, size = query_grad.shape
    half, width = rows // 2, w_in.shape[0]
    blocks = half // BLOCK
    keep = pl.BlockSpec((BLOCK, size), lambda i, scalars: (scalars[SIDE] * blocks + i, 0))
    send = pl.BlockSpec((BLOCK, size), lambda i, scalars: ((1 - scalars[SIDE]) * blocks + i, 0))
    grads = [query_grad, key_grad, value_grad]
    return call(
        inputs_back_kernel,
        scalars,
        [*grads, *grads, w_in],
        [shape((half, width), F32), shape((half, width), BF16)]
        + [shape((half, size // 2), BF16)] * 2,
        [keep] * 3 + [send] * 3 + [None],
        [row_spec(width)] * 2 + [row_spec(size // 2)] * 2,
        (blocks,),
        micros=4,
    )


def feed_out_kernel(scalars, *refs):
    down_ref, up_ref = refs[-2:]
    first = scalars[CORE] == 0
    for part in range(PARTS):
        own_ref, got_ref = refs[2 * part : 2 * part + 2]

        @pl.when(pl.program_id(0) == part)
        def _():
            own, got = own_ref[...].astype(F32), got_ref[...].astype(F32)
            down_ref[...] = jnp.where(first, own, got)
            up_ref[...] = jnp.where(first, got, own)


def feed_out(scalars, chains):
    arrays = [a for chain in chains for a in chain.state]
    rows, width = arrays[0].shape
    return call(
        feed_out_kernel,
        scalars,
        arrays,
        [shape((PARTS * rows, width), F32), shape((width, PARTS * rows), F32)],
        None,
        [
            pl.BlockSpec((rows, width), lambda i, scalars: (i, 0)),
            pl.BlockSpec((width, rows), lambda i, scalars: (0, i)),
        ],
        (PARTS,),
        micros=5,
    )


def last_out_kernel(scalars, own_ref, got_ref, wo_ref, wq_ref, wk_ref, wv_ref):
    half = own_ref.shape[0]
    size = wq_ref.shape[1]
    first = scalars[CORE] == 0
    own, got = own_ref[...].astype(F32), got_ref[...].astype(F32)
    for h, part in enumerate((jnp.where(first, own, got), jnp.where(first, got, own))):
        lines = slice(h * half, (h + 1) * half)
        wo_ref[:, lines] = part[:, :half]
        wq_ref[lines, :] = part[:, half : half + size]
        wk_ref[lines, :] = part[:, half + size : half + 2 * size]
        wv_ref[:, lines] = part[:, half + 2 * size : half + 2 * size + size // 2].T


def last_out(scalars, chain, size):
    own, got = chain.state
    half = own.shape[0]
    return call(
        last_out_kernel,
        scalars,
        [own, got],
        [shape((size, 2 * half), F32)]
        + [shape((2 * half, size), F32)] * 2
        + [shape((size // 2, 2 * half), F32)],
        micros=3,
    )


def shards(
    tokens,
    first_values,
    lengths,
    reuse_index,
    ln1_gain,
    ln1_bias,
    w_query,
    query_bias,
    w_key,
    w_value,
    value_bias,
    w_out,
    out_bias,
    ln2_gain,
    ln2_bias,
    w_up,
    up_bias,
    w_down,
    down_bias,
    cotangent,
):
    place, side = lax.axis_index("dp"), lax.axis_index("tensor")
    core = place % 2
    local_rows, width = tokens.shape
    query_size, value_size = query_bias.shape[0], value_bias.shape[0]
    length = lengths[0]
    scalars = jnp.stack([side, length, core]).astype(jnp.int32)
    positions = jnp.arange(local_rows)[:, None]
    own_valid = side * local_rows + positions < length
    other_valid = (1 - side) * local_rows + positions < length

    early, late = cotangent[: local_rows // 2], cotangent[local_rows // 2 :]
    normed_one = norm(scalars, tokens, ln1_gain, ln1_bias)
    one_got = across(normed_one)
    picks = reuse_index[jnp.arange(2 * value_size) // HD]
    selector = (
        (jnp.arange(width)[:, None] // HD == picks[None, :])
        & ((jnp.arange(width) % HD)[:, None] == (jnp.arange(2 * value_size) % HD)[None, :])
    ).astype(BF16)
    first_values, selector = after((first_values, selector), normed_one)
    chosen = dot(first_values, selector).astype(BF16)
    own_chosen, other_chosen = slabs(chosen, side)
    chosen_got = across(other_chosen)
    w_in = jnp.concatenate([w_query, w_key, w_value], axis=1)
    branch_grad = jnp.where(own_valid, cotangent, 0)
    out_piece = halves(w_out, core)[0]
    one_got, chosen_got, w_in, branch_grad, out_piece, early, late = lax.optimization_barrier(
        (one_got, chosen_got, w_in, branch_grad, out_piece, early, late)
    )
    out_got = across(out_piece)
    early_got = across(early)
    queries, keys, values = project(
        scalars, normed_one, one_got, w_in, query_bias, value_bias, own_chosen, chosen_got
    )
    heads_out, lse = attend(scalars, queries, keys, values)
    heads_out, out_got, early_got = lax.optimization_barrier((heads_out, out_got, early_got))
    heads_got = across(heads_out[1])
    w_out_other = join(out_got, flip(out_got, 1), core)
    heads_got, w_out_other, late = lax.optimization_barrier((heads_got, w_out_other, late))
    middle, normed_two = mix(
        scalars, heads_out, heads_got, w_out, w_out_other, tokens, out_bias, ln2_gain, ln2_bias
    )

    normed_two, late = lax.optimization_barrier((normed_two, late))
    two_got = across(normed_two)
    late_got = across(late)
    own = feed(scalars, normed_two, branch_grad, w_up, up_bias, w_down, F32)
    two_got, late_got, own = lax.optimization_barrier((two_got, late_got, own))
    branch_grad_got = jnp.where(other_valid, jnp.concatenate([early_got, late_got], axis=0), 0)
    normeds, grads = (normed_two, two_got), (branch_grad, branch_grad_got)
    chains = []

    def add_chain(part, other):
        keep, send = feed_weights(scalars, part, own, other, normeds, grads)
        chains.append(Chain(keep, send, place))

    first = feed(scalars, two_got, branch_grad_got, w_up, up_bias, w_down, F32, 0, PARTS)
    add_chain(0, first)
    sums = hold(chains, *first[:2])
    advance(chains, [1])
    second = feed(scalars, two_got, branch_grad_got, w_up, up_bias, w_down, BF16, 1, PARTS, sums)
    up_bias_grad = (own[4] + jnp.concatenate([first[4], second[4]], axis=1))[0]
    branch_send, back_send = hold(chains, *second[:2])
    back_got = across(back_send)
    chains[0].send()
    add_chain(1, second)

    turned = turn(
        scalars, middle, cotangent, own[1], back_got, ln2_gain, w_out, w_out_other
    )
    middle_grad, attention_grad, heads_grad, heads_grad_send, two_sums = hold(chains, *turned)
    heads_grad_got = across(heads_grad_send)
    out_grad_send = dot(heads_got, attention_grad, TN).astype(BF16)
    out_grad_own = dot(heads_out[0], attention_grad, TN)
    advance(chains, [1, 1])
    heads_grad_got, out_grad_send, out_grad_own = hold(
        chains, heads_grad_got, out_grad_send, out_grad_own
    )
    out_grad_got = across(out_grad_send)
    query_grad, key_grad, value_grad = attend_back(
        scalars, queries, keys, values, heads_out, lse, heads_grad, heads_grad_got
    )
    advance(chains, [1, 1])
    middle_rows = local_rows // 2
    out_grad_got, query_grad, key_grad, value_grad, branch_send = hold(
        chains, out_grad_got, query_grad, key_grad, value_grad, branch_send
    )
    keep, send, query_sums, value_sums = last_weights(
        scalars, normed_one, one_got, query_grad, key_grad, value_grad, out_grad_own, out_grad_got
    )
    chains.append(Chain(keep, send, place))

    branch_got = across(branch_send[:middle_rows])
    back_keep, back_send, first_keep, first_send = inputs_back(
        scalars, *after((query_grad, key_grad, value_grad), keep), w_in
    )
    advance(chains, [1, 1, 1])
    back_keep, back_send, first_keep, first_send, branch_send, branch_got = hold(
        chains, back_keep, back_send, first_keep, first_send, branch_send, branch_got
    )
    back_got = across(back_send[:middle_rows])
    advance(chains, [1, 1, 1])
    back_got, back_send, first_send = hold(chains, back_got, back_send, first_send)
    back_late = across(back_send[middle_rows:])
    first_got = across(first_send)
    advance(chains, [1, 1, 1])
    back_late, first_got, branch_send = hold(chains, back_late, first_got, branch_send)
    branch_late = across(branch_send[middle_rows:])
    tokens_grad, one_sums = close(
        scalars, tokens, ln1_gain, back_keep, back_got, back_late, middle_grad
    )
    advance(chains, [1, 1, 1])
    tokens_grad, one_sums, branch_late, first_got = hold(
        chains, tokens_grad, one_sums, branch_late, first_got
    )
    first_grads = jnp.concatenate(
        [jnp.where(side == 0, first_keep, first_got), jnp.where(side == 0, first_got, first_keep)],
        axis=1,
    )
    first_values_grad = dot(first_grads, selector, NT)
    whole = jnp.concatenate([one_sums[:2], two_sums[2:3], two_sums[:2], two_sums[3:4]]).reshape(-1)
    whole = whole + across(whole)
    small = jnp.concatenate([whole, query_sums[0], value_sums[0], up_bias_grad])
    bits = dp_bits()
    small = small + flip(small, 1)
    advance(chains, [0, 1, 1])
    small, first_values_grad = hold(chains, small, first_values_grad)
    small = small + flip(small, bits[1])
    small = small + flip(small, bits[2])
    advance(chains, [0, 1, 1])
    small = hold(chains, small)
    for bit in bits[3:]:
        small = small + flip(small, bit)
    branch_all = jnp.concatenate([branch_got, branch_late], axis=0).astype(F32)
    result = (middle + own[0] + branch_all + down_bias) * own_valid.astype(F32)
    result = result.astype(BF16)
    advance(chains, [99, 99, len(chains[2].steps) - 1])
    w_down_grad, w_up_grad = feed_out(scalars, chains[:PARTS])
    chains[-1].state, w_down_grad, w_up_grad, small, result = lax.optimization_barrier(
        (chains[-1].state, w_down_grad, w_up_grad, small, result)
    )
    advance(chains, [0, 0, 1])
    w_out_grad, w_query_grad, w_key_grad, w_value_grad = last_out(scalars, chains[-1], query_size)
    w_value_grad = w_value_grad.T
    ln1_gain_grad, ln1_bias_grad, out_bias_grad, ln2_gain_grad, ln2_bias_grad, down_bias_grad = (
        small[k * width : (k + 1) * width] for k in range(6)
    )
    query_bias_grad = small[6 * width : 6 * width + query_size]
    value_bias_grad = small[6 * width + query_size : 6 * width + query_size + value_size]
    up_bias_grad = small[6 * width + query_size + value_size :]
    return (
        result,
        tokens_grad,
        first_values_grad,
        ln1_gain_grad,
        ln1_bias_grad,
        w_query_grad,
        query_bias_grad,
        w_key_grad,
        w_value_grad,
        value_bias_grad,
        w_out_grad,
        out_bias_grad,
        ln2_gain_grad,
        ln2_bias_grad,
        w_up_grad,
        up_bias_grad,
        w_down_grad,
        down_bias_grad,
    )


def solution(mesh):
    in_specs = (
        P(("dp", "tensor"), None),
        P(("dp", "tensor"), None),
        P("dp"),
        P(),
        P(),
        P(),
        P(None, "tensor"),
        P("tensor"),
        P(None, "tensor"),
        P(None, "tensor"),
        P("tensor"),
        P("tensor", None),
        P(),
        P(),
        P(),
        P(None, "tensor"),
        P("tensor"),
        P("tensor", None),
        P(),
        P(("dp", "tensor"), None),
    )
    out_specs = (
        P(("dp", "tensor"), None),
        P(("dp", "tensor"), None),
        P(("dp", "tensor"), None),
        P(),
        P(),
        P(None, "tensor"),
        P("tensor"),
        P(None, "tensor"),
        P(None, "tensor"),
        P("tensor"),
        P("tensor", None),
        P(),
        P(),
        P(),
        P(None, "tensor"),
        P("tensor"),
        P("tensor", None),
        P(),
    )
    return jax.shard_map(shards, mesh=mesh, in_specs=in_specs, out_specs=out_specs, check_vma=False)
```

```python
from functools import partial

import jax
import jax.numpy as jnp
from jax import lax
from jax.experimental import pallas as pl
from jax.experimental.pallas import tpu as pltpu
from jax.sharding import PartitionSpec as P

H = 12
HD = 64
PARTS = 2
BLOCK = 256
VMEM_BYTES = 32 * 1024 * 1024
NT = (((1,), (1,)), ((), ()))
TN = (((0,), (0,)), ((), ()))
NN = (((1,), (0,)), ((), ()))
F32 = jnp.float32
BF16 = jnp.bfloat16
STRETCH = 15
SIDE, LENGTH, CORE, WHICH = 0, 1, 2, 3


def shape(dims, dtype):
    return jax.ShapeDtypeStruct(dims, dtype)


def call(kernel, scalars, arrays, out_shape, in_specs=None, out_specs=None, grid=(1,), scratch=(), micros=2):
    def whole(array):
        return pl.BlockSpec(array.shape, lambda *_, dims=len(array.shape): (0,) * dims)

    return pl.pallas_call(
        kernel,
        grid_spec=pltpu.PrefetchScalarGridSpec(
            num_scalar_prefetch=1,
            grid=grid,
            in_specs=[s or whole(a) for s, a in zip(in_specs or [None] * len(arrays), arrays)],
            out_specs=[
                s or whole(o) for s, o in zip(out_specs or [None] * len(out_shape), out_shape)
            ],
            scratch_shapes=list(scratch),
        ),
        out_shape=out_shape,
        compiler_params=pltpu.CompilerParams(vmem_limit_bytes=VMEM_BYTES),
        cost_estimate=pl.CostEstimate(
            flops=STRETCH * micros * 1_150_000_000,
            bytes_accessed=STRETCH * micros * 3_600_000,
            transcendentals=0,
        ),
    )(scalars, *arrays)


def dot(left, right, dims=NN):
    return lax.dot_general(left, right, dims, preferred_element_type=F32)


def pick(flag, left, right):
    return jnp.where(flag, left.astype(F32), right.astype(F32)).astype(left.dtype)


def across(values):
    return lax.ppermute(values, "tensor", [(0, 1), (1, 0)])


def flip(values, bit):
    return lax.ppermute(values, "dp", [(d, d ^ bit) for d in range(lax.axis_size("dp"))])


def halves(values, which):
    half = values.shape[0] // 2
    return (
        lax.dynamic_slice_in_dim(values, which * half, half, 0),
        lax.dynamic_slice_in_dim(values, (1 - which) * half, half, 0),
    )


def join(own, other, which):
    return jnp.concatenate(
        [jnp.where(which == 0, own, other), jnp.where(which == 0, other, own)], axis=0
    )


def slabs(values, which):
    half = values.shape[1] // 2
    return (
        lax.dynamic_slice_in_dim(values, which * half, half, 1),
        lax.dynamic_slice_in_dim(values, (1 - which) * half, half, 1),
    )


def after(values, *found):
    return lax.optimization_barrier((values, found))[0]


def dp_bits():
    return [1 << k for k in range(lax.axis_size("dp").bit_length() - 1)]


def fold_kernel(scalars, own_ref, got_ref, keep_ref, send_ref):
    half = keep_ref.shape[0]
    which = scalars[0]
    for out_ref, part in ((keep_ref, which), (send_ref, 1 - which)):
        rows = pl.ds(pl.multiple_of(part * half, half), half)
        out_ref[...] = (own_ref[rows, :].astype(F32) + got_ref[rows, :].astype(F32)).astype(BF16)


def join_kernel(scalars, own_ref, got_ref, out_ref):
    half = own_ref.shape[0]
    which = scalars[0]
    for in_ref, part in ((own_ref, which), (got_ref, 1 - which)):
        out_ref[pl.ds(pl.multiple_of(part * half, half), half), :] = in_ref[...]


class Chain:
    def __init__(self, keep, send, place):
        self.state, self.place, self.pending = (keep, send), place, None
        bits = dp_bits()
        self.steps = [("halve", bit, later) for bit, later in zip(bits, bits[1:] + [0])]
        self.steps += [("double", bit, 0) for bit in reversed(bits)]

    def which(self, bit):
        return (self.place // bit) % 2

    def send(self):
        self.merge()
        if self.steps:
            self.pending = self.steps.pop(0)
            self.state += (flip(self.state[-1], self.pending[1]),)

    def merge(self):
        if not self.pending:
            return
        (kind, bit, following), self.pending = self.pending, None
        own, got = self.state[0], self.state[-1]
        rows, columns = got.shape
        which = self.which(following if kind == "halve" else bit)[None]
        if kind == "double" and bit == 1:
            return
        if kind == "double" and rows % 16 == 0:
            out = [shape((2 * rows, columns), BF16)]
            self.state = tuple(call(join_kernel, which, [own, got], out))
        elif kind == "double":
            self.state = (join(own, got, which[0]),)
        elif following and rows % 32 == 0:
            out = [shape((rows // 2, columns), BF16)] * 2
            self.state = tuple(call(fold_kernel, which, [own, got], out))
        else:
            total = (own.astype(F32) + got.astype(F32)).astype(BF16)
            self.state = halves(total, which[0]) if following else (total,)

    def step(self):
        self.send()
        self.merge()


def advance(chains, counts):
    for chain, count in zip(chains, counts):
        for _ in range(count):
            chain.step()


def hold(chains, *values):
    states, values = lax.optimization_barrier(([c.state for c in chains], values))
    for chain, state in zip(chains, states):
        chain.state = state
    return values if len(values) != 1 else values[0]


def unit_rows(values):
    centred = values - jnp.mean(values, axis=-1, keepdims=True)
    spread = jnp.mean(centred * centred, axis=-1, keepdims=True)
    scale = lax.rsqrt(spread + 1e-05)
    return centred * scale, scale


def unit_rows_back(unit, scale, grad):
    inner = jnp.mean(grad * unit, axis=-1, keepdims=True)
    return scale * (grad - jnp.mean(grad, axis=-1, keepdims=True) - unit * inner)


def column_sum(values):
    return jnp.sum(values, axis=0, keepdims=True)


def row_spec(width, place=lambda i: i):
    return pl.BlockSpec((BLOCK, width), lambda i, scalars: (place(i), 0))


def valid_rows(scalars, block, rows):
    position = scalars[SIDE] * rows + block * BLOCK
    position = position + lax.broadcasted_iota(jnp.int32, (BLOCK, 1), 0)
    return (position < scalars[LENGTH]).astype(F32)


def norm_kernel(scalars, x_ref, gain_ref, bias_ref, out_ref):
    unit, _ = unit_rows(x_ref[...].astype(F32))
    out_ref[...] = (unit * gain_ref[...] + bias_ref[...]).astype(BF16)


def norm(scalars, values, gain, bias):
    rows, width = values.shape
    return call(
        norm_kernel,
        scalars,
        [values, gain[None], bias[None]],
        [shape((rows, width), BF16)],
        [row_spec(width), None, None],
        [row_spec(width)],
        (rows // BLOCK,),
    )[0]


def project_kernel(
    scalars, x_ref, x_got_ref, w_ref, qb_ref, vb_ref, reused_ref, reused_got_ref, q_ref, k_ref, v_ref
):
    width, fresh = q_ref.shape[1], vb_ref.shape[1]
    own = pl.program_id(0) < pl.num_programs(0) // 2

    def work(x_ref, reused_ref):
        found = dot(x_ref[...], w_ref[...])
        q_ref[...] = (found[:, :width] + qb_ref[...]).astype(BF16)
        k_ref[...] = found[:, width : 2 * width].astype(BF16)
        values = (found[:, 2 * width :] + vb_ref[...]).astype(BF16)
        reused = reused_ref[...]
        for head in range(fresh // HD):
            part = slice(head * HD, (head + 1) * HD)
            v_ref[:, 2 * head * HD : 2 * (head + 1) * HD] = jnp.concatenate(
                [values[:, part], reused[:, part]], axis=1
            )

    pl.when(own)(lambda: work(x_ref, reused_ref))
    pl.when(jnp.logical_not(own))(lambda: work(x_got_ref, reused_got_ref))


def project(scalars, normed, normed_got, weight, query_bias, value_bias, reused, reused_got):
    local, depth = normed.shape
    width, fresh = query_bias.shape[0], value_bias.shape[0]
    blocks = local // BLOCK
    x_spec, r_spec = (row_spec(w, lambda i: jnp.minimum(i, blocks - 1)) for w in (depth, fresh))
    x_got_spec, r_got_spec = (
        row_spec(w, lambda i: jnp.maximum(i - blocks, 0)) for w in (depth, fresh)
    )
    out_spec = pl.BlockSpec(
        (BLOCK, width),
        lambda i, scalars: (lax.rem(i + scalars[SIDE] * blocks, 2 * blocks), 0),
    )
    return call(
        project_kernel,
        scalars,
        [normed, normed_got, weight, query_bias[None], value_bias[None], reused, reused_got],
        [shape((2 * local, width), BF16)] * 3,
        [x_spec, x_got_spec, None, None, None, r_spec, r_got_spec],
        [out_spec] * 3,
        (2 * blocks,),
        micros=4,
    )


def mix_kernel(
    scalars, keep_ref, got_ref, w_ref, w_other_ref, x_ref, ob_ref, gain_ref, bias_ref, mid_ref, out_ref
):
    attention = dot(keep_ref[...], w_ref[...]) + dot(got_ref[...], w_other_ref[...])
    middle = x_ref[...].astype(F32) + attention + ob_ref[...]
    mid_ref[...] = middle
    unit, _ = unit_rows(middle)
    out_ref[...] = (unit * gain_ref[...] + bias_ref[...]).astype(BF16)


def mix(scalars, keep, got, w_out, w_out_other, tokens, out_bias, gain, bias):
    rows, width = tokens.shape
    half, whole = row_spec(got.shape[1]), row_spec(width)
    kept = pl.BlockSpec((None, BLOCK, got.shape[1]), lambda i, scalars: (0, i, 0))
    return call(
        mix_kernel,
        scalars,
        [keep, got, w_out, w_out_other, tokens, out_bias[None], gain[None], bias[None]],
        [shape((rows, width), F32), shape((rows, width), BF16)],
        [kept, half, None, None, whole, None, None, None],
        [whole, whole],
        (rows // BLOCK,),
        micros=3,
    )


def turn_kernel(
    scalars,
    mid_ref,
    cot_ref,
    back_ref,
    back_got_ref,
    gain_ref,
    w_ref,
    w_other_ref,
    mid_grad_ref,
    grad_ref,
    own_ref,
    send_ref,
    sums_ref,
):
    block = pl.program_id(0)
    rows = pl.num_programs(0) * BLOCK
    out_grad = cot_ref[...].astype(F32) * valid_rows(scalars, block, rows)
    unit, scale = unit_rows(mid_ref[...])
    normed_grad = back_ref[...] + back_got_ref[...].astype(F32)
    middle_grad = out_grad + unit_rows_back(unit, scale, normed_grad * gain_ref[...])
    mid_grad_ref[...] = middle_grad
    grad = middle_grad.astype(BF16)
    grad_ref[...] = grad
    own_ref[...] = dot(grad, w_ref[...], NT).astype(BF16)
    send_ref[...] = dot(grad, w_other_ref[...], NT).astype(BF16)

    @pl.when(block == 0)
    def _():
        sums_ref[...] = jnp.zeros_like(sums_ref)

    for k, part in enumerate((normed_grad * unit, normed_grad, middle_grad, out_grad)):
        sums_ref[k : k + 1, :] += column_sum(part)


def turn(scalars, middle, cotangent, back, back_got, gain, w_out, w_out_other):
    rows, width = middle.shape
    whole, half = row_spec(width), row_spec(w_out.shape[0])
    return call(
        turn_kernel,
        scalars,
        [middle, cotangent, back, back_got, gain[None], w_out, w_out_other],
        [shape((rows, width), F32), shape((rows, width), BF16)]
        + [shape((rows, w_out.shape[0]), BF16)] * 2
        + [shape((8, width), F32)],
        [whole, whole, whole, whole, None, None, None],
        [whole, whole, half, half, None],
        (rows // BLOCK,),
        micros=4,
    )


def close_kernel(
    scalars,
    x_ref,
    gain_ref,
    keep_ref,
    got_ref,
    got_late_ref,
    mid_grad_ref,
    grad_ref,
    sums_ref,
):
    unit, scale = unit_rows(x_ref[...].astype(F32))
    early = pl.program_id(0) < pl.num_programs(0) // 2
    normed_grad = keep_ref[...] + pick(early, got_ref[...], got_late_ref[...]).astype(F32)
    grad_ref[...] = mid_grad_ref[...] + unit_rows_back(unit, scale, normed_grad * gain_ref[...])

    @pl.when(pl.program_id(0) == 0)
    def _():
        sums_ref[...] = jnp.zeros_like(sums_ref)

    for k, part in enumerate((normed_grad * unit, normed_grad)):
        sums_ref[k : k + 1, :] += column_sum(part)


def close(scalars, tokens, gain, keep, got, got_late, middle_grad):
    rows, width = tokens.shape
    whole = row_spec(width)
    last = rows // BLOCK // 2 - 1
    first_half = row_spec(width, lambda i: jnp.minimum(i, last))
    second_half = row_spec(width, lambda i: jnp.maximum(i - last - 1, 0))
    return call(
        close_kernel,
        scalars,
        [tokens, gain[None], keep, got, got_late, middle_grad],
        [shape((rows, width), F32), shape((8, width), F32)],
        [whole, None, whole, first_half, second_half, whole],
        [whole, None],
        (rows // BLOCK,),
        micros=3,
    )


def score_parts(k_ref, query, begin, length, sure):
    parts = []
    for first, last in ((0, begin), (begin, begin + BLOCK)):
        if last > first:
            part = dot(k_ref[first:last, :], query, NT)
            keys = lax.broadcasted_iota(jnp.int32, part.shape, 0) + first
            if first == begin:
                queries = lax.broadcasted_iota(jnp.int32, part.shape, 1) + begin
                part = jnp.where((keys <= queries) & (keys < length), part, -1e30)
            elif last > sure:
                part = jnp.where(keys < length, part, -1e30)
            parts.append((first, last, part))
    return parts


def attend_kernel(scalars, q_ref, k_ref, v_ref, out_ref, lse_ref):
    rows = q_ref.shape[0]
    local = rows // 2
    for begin in range(0, rows, BLOCK):
        query = q_ref[begin : begin + BLOCK, :] * HD ** (-0.5)
        lane = lax.broadcasted_iota(jnp.int32, query.shape, 1)
        mixed = []
        for head in range(2):
            mine = (lane < HD) if head == 0 else (lane >= HD)
            own_query = jnp.where(mine, query, 0).astype(BF16)
            parts = score_parts(k_ref, own_query, begin, scalars[LENGTH], local)
            highest = None
            for _, _, part in parts:
                top = jnp.max(part, axis=0, keepdims=True)
                highest = top if highest is None else jnp.maximum(highest, top)
            weights = [jnp.exp(part - highest) for _, _, part in parts]
            total = sum(column_sum(w) for w in weights)
            weights = jnp.concatenate([w.astype(BF16) for w in weights], axis=0)
            mixture = dot(v_ref[: begin + BLOCK, :], weights, TN)
            mixed.append(mixture * (1.0 / total))
            lse_ref[0, head : head + 1, begin : begin + BLOCK] = highest + jnp.log(total)
        row = lax.broadcasted_iota(jnp.int32, mixed[0].shape, 0)
        both = jnp.where(row < HD, mixed[0], mixed[1]).T.astype(BF16)
        away = jnp.abs(scalars[SIDE] - begin // local)
        out_ref[away, begin % local : begin % local + BLOCK, :] = both


def pair_spec(rows):
    return pl.BlockSpec((rows, 2 * HD), lambda p, scalars: (0, p))


def sides_spec(rows):
    return pl.BlockSpec((2, rows // 2, 2 * HD), lambda p, scalars: (0, 0, p))


def attend(scalars, queries, keys, values):
    rows, width = queries.shape
    pairs = width // (2 * HD)
    return call(
        attend_kernel,
        scalars,
        [queries, keys, values],
        [shape((2, rows // 2, width), BF16), shape((pairs, 2, rows), F32)],
        [pair_spec(rows)] * 3,
        [sides_spec(rows), pl.BlockSpec((1, 2, rows), lambda p, scalars: (p, 0, 0))],
        (pairs,),
        micros=10,
    )


def inner_kernel(scalars, out_ref, grad_ref, grad_got_ref, inner_ref):
    local = grad_ref.shape[0]
    for begin in range(0, 2 * local, BLOCK):
        place = slice(begin % local, begin % local + BLOCK)
        away = jnp.abs(scalars[SIDE] - begin // local)
        grad = pick(away == 0, grad_ref[place, :], grad_got_ref[place, :])
        product = (grad.astype(F32) * out_ref[away, place, :].astype(F32)).T
        for head in range(2):
            inner_ref[0, head : head + 1, begin : begin + BLOCK] = column_sum(
                product[head * HD : (head + 1) * HD, :]
            )


def inner_sums(scalars, heads_out, grad, grad_got):
    local, width = grad.shape
    pairs = width // (2 * HD)
    half = pair_spec(local)
    return call(
        inner_kernel,
        scalars,
        [heads_out, grad, grad_got],
        [shape((pairs, 2, 2 * local), F32)],
        [sides_spec(2 * local), half, half],
        [pl.BlockSpec((1, 2, 2 * local), lambda p, scalars: (p, 0, 0))],
        (pairs,),
    )[0]


def attend_back_kernel(
    scalars,
    q_ref,
    k_ref,
    v_ref,
    inner_ref,
    lse_ref,
    grad_ref,
    grad_got_ref,
    dq_ref,
    dk_ref,
    dv_ref,
    dk_sum,
    dv_sum,
):
    rows = q_ref.shape[0]
    local = rows // 2
    dk_sum[...] = jnp.zeros_like(dk_sum)
    dv_sum[...] = jnp.zeros_like(dv_sum)
    for begin in range(0, rows, BLOCK):
        block = slice(begin, begin + BLOCK)
        place = slice(begin % local, begin % local + BLOCK)
        here = scalars[SIDE] == begin // local
        query = q_ref[block, :] * HD ** (-0.5)
        grad = pick(here, grad_ref[place, :], grad_got_ref[place, :])
        lane = lax.broadcasted_iota(jnp.int32, query.shape, 1)
        found = []
        for head in range(2):
            mine = (lane < HD) if head == 0 else (lane >= HD)
            own_query = jnp.where(mine, query, 0).astype(BF16)
            own_grad = jnp.where(mine, grad, 0).astype(BF16)
            inner = inner_ref[0, head : head + 1, block]
            lse = lse_ref[0, head : head + 1, block]
            end = begin + BLOCK
            parts = score_parts(k_ref, own_query, begin, scalars[LENGTH], local)
            chances = jnp.concatenate([jnp.exp(part - lse) for _, _, part in parts], axis=0)
            chance_grad = dot(v_ref[:end, :], own_grad, NT)
            score_grad = (chances * (chance_grad - inner)).astype(BF16)
            dv_sum[:end, :] += dot(chances.astype(BF16), own_grad)
            dk_sum[:end, :] += dot(score_grad, own_query)
            query_grad = dot(k_ref[:end, :], score_grad, TN)
            found.append(query_grad)
        row = lax.broadcasted_iota(jnp.int32, found[0].shape, 0)
        both = jnp.where(row < HD, found[0], found[1]) * HD ** (-0.5)
        dq_ref[block, :] = both.T.astype(BF16)
    dk_ref[...] = dk_sum[...].astype(BF16)
    dv_ref[...] = dv_sum[...].astype(BF16)


def attend_back(scalars, queries, keys, values, inner, lse, grad, grad_got):
    rows, width = queries.shape
    pairs = width // (2 * HD)
    half = pair_spec(rows // 2)
    return call(
        attend_back_kernel,
        scalars,
        [queries, keys, values, inner, lse, grad, grad_got],
        [shape((rows, width), BF16)] * 3,
        [pair_spec(rows)] * 3
        + [pl.BlockSpec((1, 2, rows), lambda p, scalars: (p, 0, 0))] * 2
        + [half, half],
        [pair_spec(rows)] * 3,
        (pairs,),
        [pltpu.VMEM((rows, 2 * HD), F32)] * 2,
        micros=14,
    )


def gelu_parts(hidden):
    rate = 0.7978845608028654
    square = hidden * hidden
    bend = jnp.tanh(rate * hidden * (1.0 + 0.044715 * square))
    lift = 0.5 * (1.0 + bend)
    slope = lift + 0.5 * hidden * (1.0 - bend * bend) * (rate * (1.0 + 3 * 0.044715 * square))
    return hidden * lift, slope


def feed_kernel(steps, scalars, normed_ref, grad_ref, up_ref, bias_ref, down_ref, *refs):
    branch_ref, back_ref, active_ref, hidden_grad_ref, bias_grad_ref, branch_sum, back_sum = refs[-7:]
    normed, grad = normed_ref[...], grad_ref[...]
    up, down = up_ref[...], down_ref[...]
    active, slope = gelu_parts(dot(normed, up) + bias_ref[...])
    active = active.astype(BF16)
    hidden_grad = (dot(grad, down, NT) * slope).astype(BF16)
    branch, back = dot(active, down), dot(hidden_grad, up, NT)
    active_ref[...] = active
    hidden_grad_ref[...] = hidden_grad
    bias_grad_ref[...] = column_sum(hidden_grad.astype(F32))
    for k in range(steps):

        @pl.when(pl.program_id(0) == k)
        def _():
            sums = refs[:-7] if k == 0 else (branch_sum, back_sum)
            outs = (branch_ref, back_ref) if k == steps - 1 else (branch_sum, back_sum)
            for n, (new, out_ref) in enumerate(zip((branch, back), outs)):
                total = new + sums[n][...] if sums else new
                out_ref[...] = total.astype(out_ref.dtype)


def feed(scalars, normed, grad, w_up, up_bias, w_down, dtype, part=0, parts=1, sums=()):
    rows, width = normed.shape
    hidden = w_down.shape[0] // parts
    tile = 3 * BLOCK
    steps = hidden // tile
    begin = part * steps
    line = pl.BlockSpec((1, tile), lambda i, scalars: (0, i))
    units = pl.BlockSpec((rows, tile), lambda i, scalars: (0, i))
    return call(
        partial(feed_kernel, steps),
        scalars,
        [normed, grad, w_up, up_bias[None], w_down, *sums],
        [shape((rows, width), dtype)] * 2
        + [shape((rows, hidden), BF16)] * 2
        + [shape((1, hidden), F32)],
        [
            None,
            None,
            pl.BlockSpec((width, tile), lambda i, scalars: (0, begin + i)),
            pl.BlockSpec((1, tile), lambda i, scalars: (0, begin + i)),
            pl.BlockSpec((tile, width), lambda i, scalars: (begin + i, 0)),
        ]
        + [None] * len(sums),
        [None, None, units, units, line],
        (steps,),
        [pltpu.VMEM((rows, width), F32)] * 2,
        micros=10 // parts,
    )


def feed_weights_kernel(scalars, *refs):
    actives, hidden_grads, normeds, grads = refs[0:2], refs[2:4], refs[4:6], refs[6:8]
    keep_ref, send_ref = refs[8:]
    step = pl.program_id(0)
    down = sum(dot(a[...], g[...], TN) for a, g in zip(actives, grads)).astype(BF16)
    up = sum(dot(n[...], h[...], TN) for n, h in zip(normeds, hidden_grads)).astype(BF16)
    for k in range(keep_ref.shape[0] // BLOCK):
        lines = slice(k * BLOCK, (k + 1) * BLOCK)

        @pl.when((step == k) & (scalars[CORE] == 0))
        def _():
            keep_ref[lines, :] = down
            send_ref[:, lines] = up

        @pl.when((step == k) & (scalars[CORE] == 1))
        def _():
            send_ref[lines, :] = down
            keep_ref[:, lines] = up


def feed_weights(scalars, part, own, other, normeds, grads):
    rows, width = normeds[0].shape
    hidden = other[2].shape[1]
    steps = hidden // BLOCK
    of_all = pl.BlockSpec((rows, BLOCK), lambda i, scalars: (0, part * steps + i))
    of_part = pl.BlockSpec((rows, BLOCK), lambda i, scalars: (0, i))
    return call(
        feed_weights_kernel,
        scalars,
        [own[2], other[2], own[3], other[3], *normeds, *grads],
        [shape((hidden, width), BF16)] * 2,
        [of_all, of_part, of_all, of_part] + [None] * 4,
        None,
        (steps,),
        micros=5,
    )


def fresh_columns(values):
    return jnp.concatenate(
        [values[:, k * HD : (k + 1) * HD] for k in range(0, values.shape[1] // HD, 2)], axis=1
    )


def reused_columns(values):
    return jnp.concatenate(
        [values[:, k * HD : (k + 1) * HD] for k in range(1, values.shape[1] // HD, 2)], axis=1
    )


def last_weights_kernel(
    scalars, x_ref, x_got_ref, dq_ref, dk_ref, dv_ref, wo_ref, wo_got_ref, keep_ref, send_ref, q_sum_ref, v_sum_ref
):
    size, half = dq_ref.shape[1], wo_ref.shape[1] // 2
    local = x_ref.shape[0]
    sides = (scalars[SIDE], 1 - scalars[SIDE])
    spans = [pl.ds(pl.multiple_of(s * local, local), local) for s in sides]
    xs = (x_ref, x_got_ref)
    fresh = [fresh_columns(dv_ref[s, :]) for s in spans]
    for out_ref, h in ((keep_ref, scalars[CORE]), (send_ref, 1 - scalars[CORE])):
        lines = pl.ds(pl.multiple_of(h * half, half), half)
        wo = wo_ref[:, lines] + wo_got_ref[:, lines].astype(F32)
        out_ref[:, :half] = wo.astype(BF16)
        for k, d_ref in enumerate((dq_ref, dk_ref)):
            total = sum(dot(x[:, lines], d_ref[s, :], TN) for x, s in zip(xs, spans))
            out_ref[:, half + k * size : half + (k + 1) * size] = total.astype(BF16)
        total = sum(dot(x[:, lines], f, TN) for x, f in zip(xs, fresh)).astype(BF16)
        padding = out_ref.shape[1] - half - 2 * size - total.shape[1]
        out_ref[:, half + 2 * size :] = jnp.pad(total, ((0, 0), (0, padding)))
    q_sum_ref[...] = column_sum(dq_ref[...].astype(F32))
    v_sum_ref[...] = sum(column_sum(f.astype(F32)) for f in fresh)


def last_weights(scalars, normed, normed_got, query_grad, key_grad, value_grad, wo, wo_got):
    width, size = normed.shape[1], query_grad.shape[1]
    columns = -(-(width // 2 + 5 * size // 2) // 128) * 128
    return call(
        last_weights_kernel,
        scalars,
        [normed, normed_got, query_grad, key_grad, value_grad, wo, wo_got],
        [shape((width // 2, columns), BF16)] * 2
        + [shape((1, size), F32), shape((1, size // 2), F32)],
        micros=4,
    )


def inputs_back_kernel(scalars, *refs):
    w_ref, keep_ref, send_ref, keep_reused_ref, send_reused_ref = refs[6:]
    for (dq_ref, dk_ref, dv_ref), out_ref, reused_ref in (
        (refs[0:3], keep_ref, keep_reused_ref),
        (refs[3:6], send_ref, send_reused_ref),
    ):
        size = dq_ref.shape[1]
        total = dot(dq_ref[...], w_ref[:, :size], NT)
        total = total + dot(dk_ref[...], w_ref[:, size : 2 * size], NT)
        total = total + dot(fresh_columns(dv_ref[...]), w_ref[:, 2 * size :], NT)
        out_ref[...] = total.astype(out_ref.dtype)
        reused_ref[...] = reused_columns(dv_ref[...])


def inputs_back(scalars, query_grad, key_grad, value_grad, w_in):
    rows, size = query_grad.shape
    half, width = rows // 2, w_in.shape[0]
    blocks = half // BLOCK
    keep = pl.BlockSpec((BLOCK, size), lambda i, scalars: (scalars[SIDE] * blocks + i, 0))
    send = pl.BlockSpec((BLOCK, size), lambda i, scalars: ((1 - scalars[SIDE]) * blocks + i, 0))
    grads = [query_grad, key_grad, value_grad]
    return call(
        inputs_back_kernel,
        scalars,
        [*grads, *grads, w_in],
        [shape((half, width), F32), shape((half, width), BF16)]
        + [shape((half, size // 2), BF16)] * 2,
        [keep] * 3 + [send] * 3 + [None],
        [row_spec(width)] * 2 + [row_spec(size // 2)] * 2,
        (blocks,),
        micros=4,
    )


def feed_out_kernel(scalars, *refs):
    down_ref, up_ref = refs[-2:]
    first = scalars[CORE] == 0
    for part in range(PARTS):
        own_ref, got_ref = refs[2 * part : 2 * part + 2]

        @pl.when(pl.program_id(0) == part)
        def _():
            own, got = own_ref[...].astype(F32), got_ref[...].astype(F32)
            down_ref[...] = jnp.where(first, own, got)
            up_ref[...] = jnp.where(first, got, own)


def feed_out(scalars, chains):
    arrays = [a for chain in chains for a in chain.state]
    rows, width = arrays[0].shape
    return call(
        feed_out_kernel,
        scalars,
        arrays,
        [shape((PARTS * rows, width), F32), shape((width, PARTS * rows), F32)],
        None,
        [
            pl.BlockSpec((rows, width), lambda i, scalars: (i, 0)),
            pl.BlockSpec((width, rows), lambda i, scalars: (0, i)),
        ],
        (PARTS,),
        micros=5,
    )


def last_out_kernel(scalars, own_ref, got_ref, wo_ref, wq_ref, wk_ref, wv_ref):
    half = own_ref.shape[0]
    size = wq_ref.shape[1]
    first = scalars[CORE] == 0
    own, got = own_ref[...].astype(F32), got_ref[...].astype(F32)
    for h, part in enumerate((jnp.where(first, own, got), jnp.where(first, got, own))):
        lines = slice(h * half, (h + 1) * half)
        wo_ref[:, lines] = part[:, :half]
        wq_ref[lines, :] = part[:, half : half + size]
        wk_ref[lines, :] = part[:, half + size : half + 2 * size]
        wv_ref[:, lines] = part[:, half + 2 * size : half + 2 * size + size // 2].T


def last_out(scalars, chain, size):
    own, got = chain.state
    half = own.shape[0]
    return call(
        last_out_kernel,
        scalars,
        [own, got],
        [shape((size, 2 * half), F32)]
        + [shape((2 * half, size), F32)] * 2
        + [shape((size // 2, 2 * half), F32)],
        micros=3,
    )


def shards(
    tokens,
    first_values,
    lengths,
    reuse_index,
    ln1_gain,
    ln1_bias,
    w_query,
    query_bias,
    w_key,
    w_value,
    value_bias,
    w_out,
    out_bias,
    ln2_gain,
    ln2_bias,
    w_up,
    up_bias,
    w_down,
    down_bias,
    cotangent,
):
    place, side = lax.axis_index("dp"), lax.axis_index("tensor")
    core = place % 2
    local_rows, width = tokens.shape
    query_size, value_size = query_bias.shape[0], value_bias.shape[0]
    length = lengths[0]
    scalars = jnp.stack([side, length, core]).astype(jnp.int32)
    positions = jnp.arange(local_rows)[:, None]
    own_valid = side * local_rows + positions < length
    other_valid = (1 - side) * local_rows + positions < length

    early, late = cotangent[: local_rows // 2], cotangent[local_rows // 2 :]
    normed_one = norm(scalars, tokens, ln1_gain, ln1_bias)
    one_got = across(normed_one)
    picks = reuse_index[jnp.arange(2 * value_size) // HD]
    selector = (
        (jnp.arange(width)[:, None] // HD == picks[None, :])
        & ((jnp.arange(width) % HD)[:, None] == (jnp.arange(2 * value_size) % HD)[None, :])
    ).astype(BF16)
    first_values, selector = after((first_values, selector), normed_one)
    chosen = dot(first_values, selector).astype(BF16)
    own_chosen, other_chosen = slabs(chosen, side)
    chosen_got = across(other_chosen)
    w_in = jnp.concatenate([w_query, w_key, w_value], axis=1)
    branch_grad = jnp.where(own_valid, cotangent, 0)
    out_piece = halves(w_out, core)[0]
    one_got, chosen_got, w_in, branch_grad, out_piece, early, late = lax.optimization_barrier(
        (one_got, chosen_got, w_in, branch_grad, out_piece, early, late)
    )
    out_got = across(out_piece)
    early_got = across(early)
    queries, keys, values = project(
        scalars, normed_one, one_got, w_in, query_bias, value_bias, own_chosen, chosen_got
    )
    heads_out, lse = attend(scalars, queries, keys, values)
    heads_out, out_got, early_got = lax.optimization_barrier((heads_out, out_got, early_got))
    heads_got = across(heads_out[1])
    w_out_other = join(out_got, flip(out_got, 1), core)
    heads_got, w_out_other, late = lax.optimization_barrier((heads_got, w_out_other, late))
    middle, normed_two = mix(
        scalars, heads_out, heads_got, w_out, w_out_other, tokens, out_bias, ln2_gain, ln2_bias
    )

    normed_two, late = lax.optimization_barrier((normed_two, late))
    two_got = across(normed_two)
    late_got = across(late)
    own = feed(scalars, normed_two, branch_grad, w_up, up_bias, w_down, F32)
    two_got, late_got, own = lax.optimization_barrier((two_got, late_got, own))
    branch_grad_got = jnp.where(other_valid, jnp.concatenate([early_got, late_got], axis=0), 0)
    normeds, grads = (normed_two, two_got), (branch_grad, branch_grad_got)
    chains = []

    def add_chain(part, other):
        keep, send = feed_weights(scalars, part, own, other, normeds, grads)
        chains.append(Chain(keep, send, place))

    first = feed(scalars, two_got, branch_grad_got, w_up, up_bias, w_down, F32, 0, PARTS)
    add_chain(0, first)
    sums = hold(chains, *first[:2])
    advance(chains, [1])
    second = feed(scalars, two_got, branch_grad_got, w_up, up_bias, w_down, BF16, 1, PARTS, sums)
    up_bias_grad = (own[4] + jnp.concatenate([first[4], second[4]], axis=1))[0]
    branch_send, back_send = hold(chains, *second[:2])
    back_got = across(back_send)
    chains[0].send()
    add_chain(1, second)

    turned = turn(
        scalars, middle, cotangent, own[1], back_got, ln2_gain, w_out, w_out_other
    )
    middle_grad, attention_grad, heads_grad, heads_grad_send, two_sums = hold(chains, *turned)
    heads_grad_got = across(heads_grad_send)
    out_grad_send = dot(heads_got, attention_grad, TN).astype(BF16)
    out_grad_own = dot(heads_out[0], attention_grad, TN)
    for chain in chains:
        chain.send()
    inner = inner_sums(scalars, heads_out, heads_grad, heads_grad_got)
    heads_grad_got, inner, out_grad_send, out_grad_own = hold(
        chains, heads_grad_got, inner, out_grad_send, out_grad_own
    )
    out_grad_got = across(out_grad_send)
    query_grad, key_grad, value_grad = attend_back(
        scalars, queries, keys, values, inner, lse, heads_grad, heads_grad_got
    )
    advance(chains, [1, 1])
    middle_rows = local_rows // 2
    out_grad_got, query_grad, key_grad, value_grad, branch_send = hold(
        chains, out_grad_got, query_grad, key_grad, value_grad, branch_send
    )
    keep, send, query_sums, value_sums = last_weights(
        scalars, normed_one, one_got, query_grad, key_grad, value_grad, out_grad_own, out_grad_got
    )
    chains.append(Chain(keep, send, place))

    branch_got = across(branch_send[:middle_rows])
    advance(chains, [1, 1, 1])
    branch_send, branch_got, query_grad, key_grad, value_grad = hold(
        chains, branch_send, branch_got, query_grad, key_grad, value_grad
    )
    back_keep, back_send, first_keep, first_send = inputs_back(
        scalars, query_grad, key_grad, value_grad, w_in
    )
    back_got = across(back_send[:middle_rows])
    advance(chains, [1, 1, 1])
    back_keep, back_got, back_send, first_keep, first_send = hold(
        chains, back_keep, back_got, back_send, first_keep, first_send
    )
    back_late = across(back_send[middle_rows:])
    first_got = across(first_send)
    advance(chains, [1, 1, 1])
    back_late, first_got, branch_send = hold(chains, back_late, first_got, branch_send)
    branch_late = across(branch_send[middle_rows:])
    tokens_grad, one_sums = close(
        scalars, tokens, ln1_gain, back_keep, back_got, back_late, middle_grad
    )
    advance(chains, [1, 1, 1])
    tokens_grad, one_sums, branch_late, first_got = hold(
        chains, tokens_grad, one_sums, branch_late, first_got
    )
    first_grads = jnp.concatenate(
        [jnp.where(side == 0, first_keep, first_got), jnp.where(side == 0, first_got, first_keep)],
        axis=1,
    )
    first_values_grad = dot(first_grads, selector, NT)
    whole = jnp.concatenate([one_sums[:2], two_sums[2:3], two_sums[:2], two_sums[3:4]]).reshape(-1)
    whole = whole + across(whole)
    small = jnp.concatenate([whole, query_sums[0], value_sums[0], up_bias_grad])
    bits = dp_bits()
    small = small + flip(small, 1)
    advance(chains, [0, 1, 1])
    small, first_values_grad = hold(chains, small, first_values_grad)
    small = small + flip(small, bits[1])
    small = small + flip(small, bits[2])
    advance(chains, [0, 0, 1])
    small = hold(chains, small)
    for bit in bits[3:]:
        small = small + flip(small, bit)
    branch_all = jnp.concatenate([branch_got, branch_late], axis=0).astype(F32)
    result = (middle + own[0] + branch_all + down_bias) * own_valid.astype(F32)
    result = result.astype(BF16)
    advance(chains, [99, 99, len(chains[2].steps) - 1])
    small, result, first_values_grad = hold(chains, small, result, first_values_grad)
    advance(chains, [0, 0, 1])
    w_down_grad, w_up_grad = feed_out(scalars, chains[:PARTS])
    w_out_grad, w_query_grad, w_key_grad, w_value_grad = last_out(scalars, chains[-1], query_size)
    w_value_grad = w_value_grad.T
    ln1_gain_grad, ln1_bias_grad, out_bias_grad, ln2_gain_grad, ln2_bias_grad, down_bias_grad = (
        small[k * width : (k + 1) * width] for k in range(6)
    )
    query_bias_grad = small[6 * width : 6 * width + query_size]
    value_bias_grad = small[6 * width + query_size : 6 * width + query_size + value_size]
    up_bias_grad = small[6 * width + query_size + value_size :]
    return (
        result,
        tokens_grad,
        first_values_grad,
        ln1_gain_grad,
        ln1_bias_grad,
        w_query_grad,
        query_bias_grad,
        w_key_grad,
        w_value_grad,
        value_bias_grad,
        w_out_grad,
        out_bias_grad,
        ln2_gain_grad,
        ln2_bias_grad,
        w_up_grad,
        up_bias_grad,
        w_down_grad,
        down_bias_grad,
    )


def solution(mesh):
    in_specs = (
        P(("dp", "tensor"), None),
        P(("dp", "tensor"), None),
        P("dp"),
        P(),
        P(),
        P(),
        P(None, "tensor"),
        P("tensor"),
        P(None, "tensor"),
        P(None, "tensor"),
        P("tensor"),
        P("tensor", None),
        P(),
        P(),
        P(),
        P(None, "tensor"),
        P("tensor"),
        P("tensor", None),
        P(),
        P(("dp", "tensor"), None),
    )
    out_specs = (
        P(("dp", "tensor"), None),
        P(("dp", "tensor"), None),
        P(("dp", "tensor"), None),
        P(),
        P(),
        P(None, "tensor"),
        P("tensor"),
        P(None, "tensor"),
        P(None, "tensor"),
        P("tensor"),
        P("tensor", None),
        P(),
        P(),
        P(),
        P(None, "tensor"),
        P("tensor"),
        P("tensor", None),
        P(),
    )
    return jax.shard_map(shards, mesh=mesh, in_specs=in_specs, out_specs=out_specs, check_vma=False)
```

```python
from functools import partial

import jax
import jax.numpy as jnp
from jax import lax
from jax.experimental import pallas as pl
from jax.experimental.pallas import tpu as pltpu
from jax.sharding import PartitionSpec as P

H = 12
HD = 64
PARTS = 2
BLOCK = 256
VMEM_BYTES = 32 * 1024 * 1024
NT = (((1,), (1,)), ((), ()))
TN = (((0,), (0,)), ((), ()))
NN = (((1,), (0,)), ((), ()))
F32 = jnp.float32
BF16 = jnp.bfloat16
STRETCH = 6
SIDE, LENGTH, CORE, WHICH = 0, 1, 2, 3


def shape(dims, dtype):
    return jax.ShapeDtypeStruct(dims, dtype)


def call(kernel, scalars, arrays, out_shape, in_specs=None, out_specs=None, grid=(1,), scratch=(), micros=2):
    def whole(array):
        return pl.BlockSpec(array.shape, lambda *_, dims=len(array.shape): (0,) * dims)

    return pl.pallas_call(
        kernel,
        grid_spec=pltpu.PrefetchScalarGridSpec(
            num_scalar_prefetch=1,
            grid=grid,
            in_specs=[s or whole(a) for s, a in zip(in_specs or [None] * len(arrays), arrays)],
            out_specs=[
                s or whole(o) for s, o in zip(out_specs or [None] * len(out_shape), out_shape)
            ],
            scratch_shapes=list(scratch),
        ),
        out_shape=out_shape,
        compiler_params=pltpu.CompilerParams(vmem_limit_bytes=VMEM_BYTES),
        cost_estimate=pl.CostEstimate(
            flops=STRETCH * micros * 1_150_000_000,
            bytes_accessed=STRETCH * micros * 3_600_000,
            transcendentals=0,
        ),
    )(scalars, *arrays)


def dot(left, right, dims=NN):
    return lax.dot_general(left, right, dims, preferred_element_type=F32)


def pick(flag, left, right):
    return jnp.where(flag, left.astype(F32), right.astype(F32)).astype(left.dtype)


def across(values):
    return lax.ppermute(values, "tensor", [(0, 1), (1, 0)])


def flip(values, bit):
    return lax.ppermute(values, "dp", [(d, d ^ bit) for d in range(lax.axis_size("dp"))])


def halves(values, which):
    half = values.shape[0] // 2
    return (
        lax.dynamic_slice_in_dim(values, which * half, half, 0),
        lax.dynamic_slice_in_dim(values, (1 - which) * half, half, 0),
    )


def join(own, other, which):
    return jnp.concatenate(
        [jnp.where(which == 0, own, other), jnp.where(which == 0, other, own)], axis=0
    )


def slabs(values, which):
    half = values.shape[1] // 2
    return (
        lax.dynamic_slice_in_dim(values, which * half, half, 1),
        lax.dynamic_slice_in_dim(values, (1 - which) * half, half, 1),
    )


def after(values, *found):
    return lax.optimization_barrier((values, found))[0]


def dp_bits():
    return [1 << k for k in range(lax.axis_size("dp").bit_length() - 1)]


def fold_kernel(scalars, own_ref, got_ref, keep_ref, send_ref):
    half = keep_ref.shape[0]
    which = scalars[0]
    for out_ref, part in ((keep_ref, which), (send_ref, 1 - which)):
        rows = pl.ds(pl.multiple_of(part * half, half), half)
        out_ref[...] = (own_ref[rows, :].astype(F32) + got_ref[rows, :].astype(F32)).astype(BF16)


def join_kernel(scalars, own_ref, got_ref, out_ref):
    half = own_ref.shape[0]
    which = scalars[0]
    for in_ref, part in ((own_ref, which), (got_ref, 1 - which)):
        out_ref[pl.ds(pl.multiple_of(part * half, half), half), :] = in_ref[...]


class Chain:
    def __init__(self, keep, send, place):
        self.state, self.place, self.pending = (keep, send), place, None
        bits = dp_bits()
        self.steps = [("halve", bit, later) for bit, later in zip(bits, bits[1:] + [0])]
        self.steps += [("double", bit, 0) for bit in reversed(bits)]

    def which(self, bit):
        return (self.place // bit) % 2

    def send(self):
        self.merge()
        if self.steps:
            self.pending = self.steps.pop(0)
            self.state += (flip(self.state[-1], self.pending[1]),)

    def merge(self):
        if not self.pending:
            return
        (kind, bit, following), self.pending = self.pending, None
        own, got = self.state[0], self.state[-1]
        rows, columns = got.shape
        which = self.which(following if kind == "halve" else bit)[None]
        if kind == "double" and bit == 1:
            return
        if kind == "double" and rows % 16 == 0:
            out = [shape((2 * rows, columns), BF16)]
            self.state = tuple(call(join_kernel, which, [own, got], out))
        elif kind == "double":
            self.state = (join(own, got, which[0]),)
        elif following and rows % 32 == 0:
            out = [shape((rows // 2, columns), BF16)] * 2
            self.state = tuple(call(fold_kernel, which, [own, got], out))
        else:
            total = (own.astype(F32) + got.astype(F32)).astype(BF16)
            self.state = halves(total, which[0]) if following else (total,)

    def step(self):
        self.send()
        self.merge()


def advance(chains, counts):
    for chain, count in zip(chains, counts):
        for _ in range(count):
            chain.step()


def hold(chains, *values):
    states, values = lax.optimization_barrier(([c.state for c in chains], values))
    for chain, state in zip(chains, states):
        chain.state = state
    return values if len(values) != 1 else values[0]


def unit_rows(values):
    centred = values - jnp.mean(values, axis=-1, keepdims=True)
    spread = jnp.mean(centred * centred, axis=-1, keepdims=True)
    scale = lax.rsqrt(spread + 1e-05)
    return centred * scale, scale


def unit_rows_back(unit, scale, grad):
    inner = jnp.mean(grad * unit, axis=-1, keepdims=True)
    return scale * (grad - jnp.mean(grad, axis=-1, keepdims=True) - unit * inner)


def column_sum(values):
    return jnp.sum(values, axis=0, keepdims=True)


def row_spec(width, place=lambda i: i):
    return pl.BlockSpec((BLOCK, width), lambda i, scalars: (place(i), 0))


def valid_rows(scalars, block, rows):
    position = scalars[SIDE] * rows + block * BLOCK
    position = position + lax.broadcasted_iota(jnp.int32, (BLOCK, 1), 0)
    return (position < scalars[LENGTH]).astype(F32)


def norm_kernel(scalars, x_ref, gain_ref, bias_ref, out_ref):
    unit, _ = unit_rows(x_ref[...].astype(F32))
    out_ref[...] = (unit * gain_ref[...] + bias_ref[...]).astype(BF16)


def norm(scalars, values, gain, bias):
    rows, width = values.shape
    return call(
        norm_kernel,
        scalars,
        [values, gain[None], bias[None]],
        [shape((rows, width), BF16)],
        [row_spec(width), None, None],
        [row_spec(width)],
        (rows // BLOCK,),
    )[0]


def project_kernel(
    scalars, x_ref, x_got_ref, w_ref, qb_ref, vb_ref, reused_ref, reused_got_ref, q_ref, k_ref, v_ref
):
    width, fresh = q_ref.shape[1], vb_ref.shape[1]
    own = pl.program_id(0) < pl.num_programs(0) // 2

    def work(x_ref, reused_ref):
        found = dot(x_ref[...], w_ref[...])
        q_ref[...] = (found[:, :width] + qb_ref[...]).astype(BF16)
        k_ref[...] = found[:, width : 2 * width].astype(BF16)
        values = (found[:, 2 * width :] + vb_ref[...]).astype(BF16)
        reused = reused_ref[...]
        for head in range(fresh // HD):
            part = slice(head * HD, (head + 1) * HD)
            v_ref[:, 2 * head * HD : 2 * (head + 1) * HD] = jnp.concatenate(
                [values[:, part], reused[:, part]], axis=1
            )

    pl.when(own)(lambda: work(x_ref, reused_ref))
    pl.when(jnp.logical_not(own))(lambda: work(x_got_ref, reused_got_ref))


def project(scalars, normed, normed_got, weight, query_bias, value_bias, reused, reused_got):
    local, depth = normed.shape
    width, fresh = query_bias.shape[0], value_bias.shape[0]
    blocks = local // BLOCK
    x_spec, r_spec = (row_spec(w, lambda i: jnp.minimum(i, blocks - 1)) for w in (depth, fresh))
    x_got_spec, r_got_spec = (
        row_spec(w, lambda i: jnp.maximum(i - blocks, 0)) for w in (depth, fresh)
    )
    out_spec = pl.BlockSpec(
        (BLOCK, width),
        lambda i, scalars: (lax.rem(i + scalars[SIDE] * blocks, 2 * blocks), 0),
    )
    return call(
        project_kernel,
        scalars,
        [normed, normed_got, weight, query_bias[None], value_bias[None], reused, reused_got],
        [shape((2 * local, width), BF16)] * 3,
        [x_spec, x_got_spec, None, None, None, r_spec, r_got_spec],
        [out_spec] * 3,
        (2 * blocks,),
        micros=4,
    )


def mix_kernel(
    scalars, keep_ref, got_ref, w_ref, w_other_ref, x_ref, ob_ref, gain_ref, bias_ref, mid_ref, out_ref
):
    attention = dot(keep_ref[...], w_ref[...]) + dot(got_ref[...], w_other_ref[...])
    middle = x_ref[...].astype(F32) + attention + ob_ref[...]
    mid_ref[...] = middle
    unit, _ = unit_rows(middle)
    out_ref[...] = (unit * gain_ref[...] + bias_ref[...]).astype(BF16)


def mix(scalars, keep, got, w_out, w_out_other, tokens, out_bias, gain, bias):
    rows, width = tokens.shape
    half, whole = row_spec(got.shape[1]), row_spec(width)
    kept = pl.BlockSpec((None, BLOCK, got.shape[1]), lambda i, scalars: (0, i, 0))
    return call(
        mix_kernel,
        scalars,
        [keep, got, w_out, w_out_other, tokens, out_bias[None], gain[None], bias[None]],
        [shape((rows, width), F32), shape((rows, width), BF16)],
        [kept, half, None, None, whole, None, None, None],
        [whole, whole],
        (rows // BLOCK,),
        micros=3,
    )


def turn_kernel(
    scalars,
    mid_ref,
    cot_ref,
    back_ref,
    back_got_ref,
    gain_ref,
    w_ref,
    w_other_ref,
    mid_grad_ref,
    grad_ref,
    own_ref,
    send_ref,
    sums_ref,
):
    block = pl.program_id(0)
    rows = pl.num_programs(0) * BLOCK
    out_grad = cot_ref[...].astype(F32) * valid_rows(scalars, block, rows)
    unit, scale = unit_rows(mid_ref[...])
    normed_grad = back_ref[...] + back_got_ref[...].astype(F32)
    middle_grad = out_grad + unit_rows_back(unit, scale, normed_grad * gain_ref[...])
    mid_grad_ref[...] = middle_grad
    grad = middle_grad.astype(BF16)
    grad_ref[...] = grad
    own_ref[...] = dot(grad, w_ref[...], NT).astype(BF16)
    send_ref[...] = dot(grad, w_other_ref[...], NT).astype(BF16)

    @pl.when(block == 0)
    def _():
        sums_ref[...] = jnp.zeros_like(sums_ref)

    for k, part in enumerate((normed_grad * unit, normed_grad, middle_grad, out_grad)):
        sums_ref[k : k + 1, :] += column_sum(part)


def turn(scalars, middle, cotangent, back, back_got, gain, w_out, w_out_other):
    rows, width = middle.shape
    whole, half = row_spec(width), row_spec(w_out.shape[0])
    return call(
        turn_kernel,
        scalars,
        [middle, cotangent, back, back_got, gain[None], w_out, w_out_other],
        [shape((rows, width), F32), shape((rows, width), BF16)]
        + [shape((rows, w_out.shape[0]), BF16)] * 2
        + [shape((8, width), F32)],
        [whole, whole, whole, whole, None, None, None],
        [whole, whole, half, half, None],
        (rows // BLOCK,),
        micros=4,
    )


def close_kernel(
    scalars,
    x_ref,
    gain_ref,
    keep_ref,
    got_ref,
    got_late_ref,
    mid_grad_ref,
    grad_ref,
    sums_ref,
):
    unit, scale = unit_rows(x_ref[...].astype(F32))
    early = pl.program_id(0) < pl.num_programs(0) // 2
    normed_grad = keep_ref[...] + pick(early, got_ref[...], got_late_ref[...]).astype(F32)
    grad_ref[...] = mid_grad_ref[...] + unit_rows_back(unit, scale, normed_grad * gain_ref[...])

    @pl.when(pl.program_id(0) == 0)
    def _():
        sums_ref[...] = jnp.zeros_like(sums_ref)

    for k, part in enumerate((normed_grad * unit, normed_grad)):
        sums_ref[k : k + 1, :] += column_sum(part)


def close(scalars, tokens, gain, keep, got, got_late, middle_grad):
    rows, width = tokens.shape
    whole = row_spec(width)
    last = rows // BLOCK // 2 - 1
    first_half = row_spec(width, lambda i: jnp.minimum(i, last))
    second_half = row_spec(width, lambda i: jnp.maximum(i - last - 1, 0))
    return call(
        close_kernel,
        scalars,
        [tokens, gain[None], keep, got, got_late, middle_grad],
        [shape((rows, width), F32), shape((8, width), F32)],
        [whole, None, whole, first_half, second_half, whole],
        [whole, None],
        (rows // BLOCK,),
        micros=3,
    )


def score_parts(k_ref, query, begin, length, sure):
    parts = []
    for first, last in ((0, begin), (begin, begin + BLOCK)):
        if last > first:
            part = dot(k_ref[first:last, :], query, NT)
            keys = lax.broadcasted_iota(jnp.int32, part.shape, 0) + first
            if first == begin:
                queries = lax.broadcasted_iota(jnp.int32, part.shape, 1) + begin
                part = jnp.where((keys <= queries) & (keys < length), part, -1e30)
            elif last > sure:
                part = jnp.where(keys < length, part, -1e30)
            parts.append((first, last, part))
    return parts


def attend_kernel(scalars, q_ref, k_ref, v_ref, out_ref, lse_ref):
    rows = q_ref.shape[0]
    local = rows // 2
    for begin in range(0, rows, BLOCK):
        query = q_ref[begin : begin + BLOCK, :] * HD ** (-0.5)
        lane = lax.broadcasted_iota(jnp.int32, query.shape, 1)
        mixed = []
        for head in range(2):
            mine = (lane < HD) if head == 0 else (lane >= HD)
            own_query = jnp.where(mine, query, 0).astype(BF16)
            parts = score_parts(k_ref, own_query, begin, scalars[LENGTH], local)
            highest = None
            for _, _, part in parts:
                top = jnp.max(part, axis=0, keepdims=True)
                highest = top if highest is None else jnp.maximum(highest, top)
            weights = [jnp.exp(part - highest) for _, _, part in parts]
            total = sum(column_sum(w) for w in weights)
            weights = jnp.concatenate([w.astype(BF16) for w in weights], axis=0)
            mixture = dot(v_ref[: begin + BLOCK, :], weights, TN)
            mixed.append(mixture * (1.0 / total))
            lse_ref[0, head : head + 1, begin : begin + BLOCK] = highest + jnp.log(total)
        row = lax.broadcasted_iota(jnp.int32, mixed[0].shape, 0)
        both = jnp.where(row < HD, mixed[0], mixed[1]).T.astype(BF16)
        away = jnp.abs(scalars[SIDE] - begin // local)
        out_ref[away, begin % local : begin % local + BLOCK, :] = both


def pair_spec(rows):
    return pl.BlockSpec((rows, 2 * HD), lambda p, scalars: (0, p))


def sides_spec(rows):
    return pl.BlockSpec((2, rows // 2, 2 * HD), lambda p, scalars: (0, 0, p))


def attend(scalars, queries, keys, values):
    rows, width = queries.shape
    pairs = width // (2 * HD)
    return call(
        attend_kernel,
        scalars,
        [queries, keys, values],
        [shape((2, rows // 2, width), BF16), shape((pairs, 2, rows), F32)],
        [pair_spec(rows)] * 3,
        [sides_spec(rows), pl.BlockSpec((1, 2, rows), lambda p, scalars: (p, 0, 0))],
        (pairs,),
        micros=10,
    )


def inner_kernel(scalars, out_ref, grad_ref, grad_got_ref, inner_ref):
    local = grad_ref.shape[0]
    for begin in range(0, 2 * local, BLOCK):
        place = slice(begin % local, begin % local + BLOCK)
        away = jnp.abs(scalars[SIDE] - begin // local)
        grad = pick(away == 0, grad_ref[place, :], grad_got_ref[place, :])
        product = (grad.astype(F32) * out_ref[away, place, :].astype(F32)).T
        for head in range(2):
            inner_ref[0, head : head + 1, begin : begin + BLOCK] = column_sum(
                product[head * HD : (head + 1) * HD, :]
            )


def inner_sums(scalars, heads_out, grad, grad_got):
    local, width = grad.shape
    pairs = width // (2 * HD)
    half = pair_spec(local)
    return call(
        inner_kernel,
        scalars,
        [heads_out, grad, grad_got],
        [shape((pairs, 2, 2 * local), F32)],
        [sides_spec(2 * local), half, half],
        [pl.BlockSpec((1, 2, 2 * local), lambda p, scalars: (p, 0, 0))],
        (pairs,),
    )[0]


def attend_back_kernel(
    scalars,
    q_ref,
    k_ref,
    v_ref,
    inner_ref,
    lse_ref,
    grad_ref,
    grad_got_ref,
    dq_ref,
    dk_ref,
    dv_ref,
    dk_sum,
    dv_sum,
):
    rows = q_ref.shape[0]
    local = rows // 2
    dk_sum[...] = jnp.zeros_like(dk_sum)
    dv_sum[...] = jnp.zeros_like(dv_sum)
    for begin in range(0, rows, BLOCK):
        block = slice(begin, begin + BLOCK)
        place = slice(begin % local, begin % local + BLOCK)
        here = scalars[SIDE] == begin // local
        query = q_ref[block, :] * HD ** (-0.5)
        grad = pick(here, grad_ref[place, :], grad_got_ref[place, :])
        lane = lax.broadcasted_iota(jnp.int32, query.shape, 1)
        found = []
        for head in range(2):
            mine = (lane < HD) if head == 0 else (lane >= HD)
            own_query = jnp.where(mine, query, 0).astype(BF16)
            own_grad = jnp.where(mine, grad, 0).astype(BF16)
            inner = inner_ref[0, head : head + 1, block]
            lse = lse_ref[0, head : head + 1, block]
            end = begin + BLOCK
            parts = score_parts(k_ref, own_query, begin, scalars[LENGTH], local)
            chances = jnp.concatenate([jnp.exp(part - lse) for _, _, part in parts], axis=0)
            chance_grad = dot(v_ref[:end, :], own_grad, NT)
            score_grad = (chances * (chance_grad - inner)).astype(BF16)
            dv_sum[:end, :] += dot(chances.astype(BF16), own_grad)
            dk_sum[:end, :] += dot(score_grad, own_query)
            query_grad = dot(k_ref[:end, :], score_grad, TN)
            found.append(query_grad)
        row = lax.broadcasted_iota(jnp.int32, found[0].shape, 0)
        both = jnp.where(row < HD, found[0], found[1]) * HD ** (-0.5)
        dq_ref[block, :] = both.T.astype(BF16)
    dk_ref[...] = dk_sum[...].astype(BF16)
    dv_ref[...] = dv_sum[...].astype(BF16)


def attend_back(scalars, queries, keys, values, inner, lse, grad, grad_got):
    rows, width = queries.shape
    pairs = width // (2 * HD)
    half = pair_spec(rows // 2)
    return call(
        attend_back_kernel,
        scalars,
        [queries, keys, values, inner, lse, grad, grad_got],
        [shape((rows, width), BF16)] * 3,
        [pair_spec(rows)] * 3
        + [pl.BlockSpec((1, 2, rows), lambda p, scalars: (p, 0, 0))] * 2
        + [half, half],
        [pair_spec(rows)] * 3,
        (pairs,),
        [pltpu.VMEM((rows, 2 * HD), F32)] * 2,
        micros=14,
    )


def gelu_parts(hidden):
    rate = 0.7978845608028654
    square = hidden * hidden
    bend = jnp.tanh(rate * hidden * (1.0 + 0.044715 * square))
    lift = 0.5 * (1.0 + bend)
    slope = lift + 0.5 * hidden * (1.0 - bend * bend) * (rate * (1.0 + 3 * 0.044715 * square))
    return hidden * lift, slope


def feed_kernel(steps, scalars, normed_ref, grad_ref, up_ref, bias_ref, down_ref, *refs):
    branch_ref, back_ref, active_ref, hidden_grad_ref, bias_grad_ref, branch_sum, back_sum = refs[-7:]
    normed, grad = normed_ref[...], grad_ref[...]
    up, down = up_ref[...], down_ref[...]
    active, slope = gelu_parts(dot(normed, up) + bias_ref[...])
    active = active.astype(BF16)
    hidden_grad = (dot(grad, down, NT) * slope).astype(BF16)
    branch, back = dot(active, down), dot(hidden_grad, up, NT)
    active_ref[...] = active
    hidden_grad_ref[...] = hidden_grad
    bias_grad_ref[...] = column_sum(hidden_grad.astype(F32))
    for k in range(steps):

        @pl.when(pl.program_id(0) == k)
        def _():
            sums = refs[:-7] if k == 0 else (branch_sum, back_sum)
            outs = (branch_ref, back_ref) if k == steps - 1 else (branch_sum, back_sum)
            for n, (new, out_ref) in enumerate(zip((branch, back), outs)):
                total = new + sums[n][...] if sums else new
                out_ref[...] = total.astype(out_ref.dtype)


def feed(scalars, normed, grad, w_up, up_bias, w_down, dtype, part=0, parts=1, sums=()):
    rows, width = normed.shape
    hidden = w_down.shape[0] // parts
    tile = 3 * BLOCK
    steps = hidden // tile
    begin = part * steps
    line = pl.BlockSpec((1, tile), lambda i, scalars: (0, i))
    units = pl.BlockSpec((rows, tile), lambda i, scalars: (0, i))
    return call(
        partial(feed_kernel, steps),
        scalars,
        [normed, grad, w_up, up_bias[None], w_down, *sums],
        [shape((rows, width), dtype)] * 2
        + [shape((rows, hidden), BF16)] * 2
        + [shape((1, hidden), F32)],
        [
            None,
            None,
            pl.BlockSpec((width, tile), lambda i, scalars: (0, begin + i)),
            pl.BlockSpec((1, tile), lambda i, scalars: (0, begin + i)),
            pl.BlockSpec((tile, width), lambda i, scalars: (begin + i, 0)),
        ]
        + [None] * len(sums),
        [None, None, units, units, line],
        (steps,),
        [pltpu.VMEM((rows, width), F32)] * 2,
        micros=10 // parts,
    )


def feed_weights_kernel(scalars, *refs):
    actives, hidden_grads, normeds, grads = refs[0:2], refs[2:4], refs[4:6], refs[6:8]
    keep_ref, send_ref = refs[8:]
    step = pl.program_id(0)
    down = sum(dot(a[...], g[...], TN) for a, g in zip(actives, grads)).astype(BF16)
    up = sum(dot(n[...], h[...], TN) for n, h in zip(normeds, hidden_grads)).astype(BF16)
    for k in range(keep_ref.shape[0] // BLOCK):
        lines = slice(k * BLOCK, (k + 1) * BLOCK)

        @pl.when((step == k) & (scalars[CORE] == 0))
        def _():
            keep_ref[lines, :] = down
            send_ref[:, lines] = up

        @pl.when((step == k) & (scalars[CORE] == 1))
        def _():
            send_ref[lines, :] = down
            keep_ref[:, lines] = up


def feed_weights(scalars, part, own, other, normeds, grads):
    rows, width = normeds[0].shape
    hidden = other[2].shape[1]
    steps = hidden // BLOCK
    of_all = pl.BlockSpec((rows, BLOCK), lambda i, scalars: (0, part * steps + i))
    of_part = pl.BlockSpec((rows, BLOCK), lambda i, scalars: (0, i))
    return call(
        feed_weights_kernel,
        scalars,
        [own[2], other[2], own[3], other[3], *normeds, *grads],
        [shape((hidden, width), BF16)] * 2,
        [of_all, of_part, of_all, of_part] + [None] * 4,
        None,
        (steps,),
        micros=5,
    )


def fresh_columns(values):
    return jnp.concatenate(
        [values[:, k * HD : (k + 1) * HD] for k in range(0, values.shape[1] // HD, 2)], axis=1
    )


def reused_columns(values):
    return jnp.concatenate(
        [values[:, k * HD : (k + 1) * HD] for k in range(1, values.shape[1] // HD, 2)], axis=1
    )


def last_weights_kernel(
    scalars, x_ref, x_got_ref, dq_ref, dk_ref, dv_ref, wo_ref, wo_got_ref, keep_ref, send_ref, q_sum_ref, v_sum_ref
):
    size, half = dq_ref.shape[1], wo_ref.shape[1] // 2
    local = x_ref.shape[0]
    sides = (scalars[SIDE], 1 - scalars[SIDE])
    spans = [pl.ds(pl.multiple_of(s * local, local), local) for s in sides]
    xs = (x_ref, x_got_ref)
    fresh = [fresh_columns(dv_ref[s, :]) for s in spans]
    for out_ref, h in ((keep_ref, scalars[CORE]), (send_ref, 1 - scalars[CORE])):
        lines = pl.ds(pl.multiple_of(h * half, half), half)
        wo = wo_ref[:, lines] + wo_got_ref[:, lines].astype(F32)
        out_ref[:, :half] = wo.astype(BF16)
        for k, d_ref in enumerate((dq_ref, dk_ref)):
            total = sum(dot(x[:, lines], d_ref[s, :], TN) for x, s in zip(xs, spans))
            out_ref[:, half + k * size : half + (k + 1) * size] = total.astype(BF16)
        total = sum(dot(x[:, lines], f, TN) for x, f in zip(xs, fresh)).astype(BF16)
        padding = out_ref.shape[1] - half - 2 * size - total.shape[1]
        out_ref[:, half + 2 * size :] = jnp.pad(total, ((0, 0), (0, padding)))
    q_sum_ref[...] = column_sum(dq_ref[...].astype(F32))
    v_sum_ref[...] = sum(column_sum(f.astype(F32)) for f in fresh)


def last_weights(scalars, normed, normed_got, query_grad, key_grad, value_grad, wo, wo_got):
    width, size = normed.shape[1], query_grad.shape[1]
    columns = -(-(width // 2 + 5 * size // 2) // 128) * 128
    return call(
        last_weights_kernel,
        scalars,
        [normed, normed_got, query_grad, key_grad, value_grad, wo, wo_got],
        [shape((width // 2, columns), BF16)] * 2
        + [shape((1, size), F32), shape((1, size // 2), F32)],
        micros=4,
    )


def inputs_back_kernel(scalars, *refs):
    w_ref, keep_ref, send_ref, keep_reused_ref, send_reused_ref = refs[6:]
    for (dq_ref, dk_ref, dv_ref), out_ref, reused_ref in (
        (refs[0:3], keep_ref, keep_reused_ref),
        (refs[3:6], send_ref, send_reused_ref),
    ):
        size = dq_ref.shape[1]
        total = dot(dq_ref[...], w_ref[:, :size], NT)
        total = total + dot(dk_ref[...], w_ref[:, size : 2 * size], NT)
        total = total + dot(fresh_columns(dv_ref[...]), w_ref[:, 2 * size :], NT)
        out_ref[...] = total.astype(out_ref.dtype)
        reused_ref[...] = reused_columns(dv_ref[...])


def inputs_back(scalars, query_grad, key_grad, value_grad, w_in):
    rows, size = query_grad.shape
    half, width = rows // 2, w_in.shape[0]
    blocks = half // BLOCK
    keep = pl.BlockSpec((BLOCK, size), lambda i, scalars: (scalars[SIDE] * blocks + i, 0))
    send = pl.BlockSpec((BLOCK, size), lambda i, scalars: ((1 - scalars[SIDE]) * blocks + i, 0))
    grads = [query_grad, key_grad, value_grad]
    return call(
        inputs_back_kernel,
        scalars,
        [*grads, *grads, w_in],
        [shape((half, width), F32), shape((half, width), BF16)]
        + [shape((half, size // 2), BF16)] * 2,
        [keep] * 3 + [send] * 3 + [None],
        [row_spec(width)] * 2 + [row_spec(size // 2)] * 2,
        (blocks,),
        micros=4,
    )


def feed_out_kernel(scalars, *refs):
    down_ref, up_ref = refs[-2:]
    first = scalars[CORE] == 0
    for part in range(PARTS):
        own_ref, got_ref = refs[2 * part : 2 * part + 2]

        @pl.when(pl.program_id(0) == part)
        def _():
            own, got = own_ref[...].astype(F32), got_ref[...].astype(F32)
            down_ref[...] = jnp.where(first, own, got)
            up_ref[...] = jnp.where(first, got, own)


def feed_out(scalars, chains):
    arrays = [a for chain in chains for a in chain.state]
    rows, width = arrays[0].shape
    return call(
        feed_out_kernel,
        scalars,
        arrays,
        [shape((PARTS * rows, width), F32), shape((width, PARTS * rows), F32)],
        None,
        [
            pl.BlockSpec((rows, width), lambda i, scalars: (i, 0)),
            pl.BlockSpec((width, rows), lambda i, scalars: (0, i)),
        ],
        (PARTS,),
        micros=5,
    )


def last_out_kernel(scalars, own_ref, got_ref, wo_ref, wq_ref, wk_ref, wv_ref):
    half = own_ref.shape[0]
    size = wq_ref.shape[1]
    first = scalars[CORE] == 0
    own, got = own_ref[...].astype(F32), got_ref[...].astype(F32)
    for h, part in enumerate((jnp.where(first, own, got), jnp.where(first, got, own))):
        lines = slice(h * half, (h + 1) * half)
        wo_ref[:, lines] = part[:, :half]
        wq_ref[lines, :] = part[:, half : half + size]
        wk_ref[lines, :] = part[:, half + size : half + 2 * size]
        wv_ref[:, lines] = part[:, half + 2 * size : half + 2 * size + size // 2].T


def last_out(scalars, chain, size):
    own, got = chain.state
    half = own.shape[0]
    return call(
        last_out_kernel,
        scalars,
        [own, got],
        [shape((size, 2 * half), F32)]
        + [shape((2 * half, size), F32)] * 2
        + [shape((size // 2, 2 * half), F32)],
        micros=3,
    )


def shards(
    tokens,
    first_values,
    lengths,
    reuse_index,
    ln1_gain,
    ln1_bias,
    w_query,
    query_bias,
    w_key,
    w_value,
    value_bias,
    w_out,
    out_bias,
    ln2_gain,
    ln2_bias,
    w_up,
    up_bias,
    w_down,
    down_bias,
    cotangent,
):
    place, side = lax.axis_index("dp"), lax.axis_index("tensor")
    core = place % 2
    local_rows, width = tokens.shape
    query_size, value_size = query_bias.shape[0], value_bias.shape[0]
    length = lengths[0]
    scalars = jnp.stack([side, length, core]).astype(jnp.int32)
    positions = jnp.arange(local_rows)[:, None]
    own_valid = side * local_rows + positions < length
    other_valid = (1 - side) * local_rows + positions < length

    early, late = cotangent[: local_rows // 2], cotangent[local_rows // 2 :]
    normed_one = norm(scalars, tokens, ln1_gain, ln1_bias)
    one_got = across(normed_one)
    picks = reuse_index[jnp.arange(2 * value_size) // HD]
    selector = (
        (jnp.arange(width)[:, None] // HD == picks[None, :])
        & ((jnp.arange(width) % HD)[:, None] == (jnp.arange(2 * value_size) % HD)[None, :])
    ).astype(BF16)
    first_values, selector = after((first_values, selector), normed_one)
    chosen = dot(first_values, selector).astype(BF16)
    own_chosen, other_chosen = slabs(chosen, side)
    chosen_got = across(other_chosen)
    w_in = jnp.concatenate([w_query, w_key, w_value], axis=1)
    branch_grad = jnp.where(own_valid, cotangent, 0)
    out_piece = halves(w_out, core)[0]
    one_got, chosen_got, w_in, branch_grad, out_piece, early, late = lax.optimization_barrier(
        (one_got, chosen_got, w_in, branch_grad, out_piece, early, late)
    )
    out_got = across(out_piece)
    early_got = across(early)
    queries, keys, values = project(
        scalars, normed_one, one_got, w_in, query_bias, value_bias, own_chosen, chosen_got
    )
    heads_out, lse = attend(scalars, queries, keys, values)
    heads_out, out_got, early_got = lax.optimization_barrier((heads_out, out_got, early_got))
    heads_got = across(heads_out[1])
    w_out_other = join(out_got, flip(out_got, 1), core)
    heads_got, w_out_other, late = lax.optimization_barrier((heads_got, w_out_other, late))
    middle, normed_two = mix(
        scalars, heads_out, heads_got, w_out, w_out_other, tokens, out_bias, ln2_gain, ln2_bias
    )

    normed_two, late = lax.optimization_barrier((normed_two, late))
    two_got = across(normed_two)
    late_got = across(late)
    own = feed(scalars, normed_two, branch_grad, w_up, up_bias, w_down, F32)
    two_got, late_got, own = lax.optimization_barrier((two_got, late_got, own))
    branch_grad_got = jnp.where(other_valid, jnp.concatenate([early_got, late_got], axis=0), 0)
    normeds, grads = (normed_two, two_got), (branch_grad, branch_grad_got)
    chains = []

    def add_chain(part, other):
        keep, send = feed_weights(scalars, part, own, other, normeds, grads)
        chains.append(Chain(keep, send, place))

    first = feed(scalars, two_got, branch_grad_got, w_up, up_bias, w_down, F32, 0, PARTS)
    add_chain(0, first)
    sums = hold(chains, *first[:2])
    advance(chains, [1])
    second = feed(scalars, two_got, branch_grad_got, w_up, up_bias, w_down, BF16, 1, PARTS, sums)
    up_bias_grad = (own[4] + jnp.concatenate([first[4], second[4]], axis=1))[0]
    branch_send, back_send = hold(chains, *second[:2])
    back_got = across(back_send)
    chains[0].send()
    add_chain(1, second)

    turned = turn(
        scalars, middle, cotangent, own[1], back_got, ln2_gain, w_out, w_out_other
    )
    middle_grad, attention_grad, heads_grad, heads_grad_send, two_sums = hold(chains, *turned)
    heads_grad_got = across(heads_grad_send)
    out_grad_send = dot(heads_got, attention_grad, TN).astype(BF16)
    out_grad_own = dot(heads_out[0], attention_grad, TN)
    for chain in chains:
        chain.send()
    inner = inner_sums(scalars, heads_out, heads_grad, heads_grad_got)
    heads_grad_got, inner, out_grad_send, out_grad_own = hold(
        chains, heads_grad_got, inner, out_grad_send, out_grad_own
    )
    out_grad_got = across(out_grad_send)
    query_grad, key_grad, value_grad = attend_back(
        scalars, queries, keys, values, inner, lse, heads_grad, heads_grad_got
    )
    advance(chains, [1, 1])
    middle_rows = local_rows // 2
    out_grad_got, query_grad, key_grad, value_grad, branch_send = hold(
        chains, out_grad_got, query_grad, key_grad, value_grad, branch_send
    )
    keep, send, query_sums, value_sums = last_weights(
        scalars, normed_one, one_got, query_grad, key_grad, value_grad, out_grad_own, out_grad_got
    )
    chains.append(Chain(keep, send, place))

    branch_got = across(branch_send[:middle_rows])
    advance(chains, [1, 1, 1])
    branch_send, branch_got, query_grad, key_grad, value_grad = hold(
        chains, branch_send, branch_got, query_grad, key_grad, value_grad
    )
    back_keep, back_send, first_keep, first_send = inputs_back(
        scalars, query_grad, key_grad, value_grad, w_in
    )
    back_got = across(back_send[:middle_rows])
    advance(chains, [1, 1, 1])
    back_keep, back_got, back_send, first_keep, first_send = hold(
        chains, back_keep, back_got, back_send, first_keep, first_send
    )
    back_late = across(back_send[middle_rows:])
    first_got = across(first_send)
    advance(chains, [1, 1, 1])
    back_late, first_got, branch_send = hold(chains, back_late, first_got, branch_send)
    branch_late = across(branch_send[middle_rows:])
    tokens_grad, one_sums = close(
        scalars, tokens, ln1_gain, back_keep, back_got, back_late, middle_grad
    )
    advance(chains, [1, 1, 1])
    tokens_grad, one_sums, branch_late, first_got = hold(
        chains, tokens_grad, one_sums, branch_late, first_got
    )
    first_grads = jnp.concatenate(
        [jnp.where(side == 0, first_keep, first_got), jnp.where(side == 0, first_got, first_keep)],
        axis=1,
    )
    first_values_grad = dot(first_grads, selector, NT)
    whole = jnp.concatenate([one_sums[:2], two_sums[2:3], two_sums[:2], two_sums[3:4]]).reshape(-1)
    whole = whole + across(whole)
    small = jnp.concatenate([whole, query_sums[0], value_sums[0], up_bias_grad])
    bits = dp_bits()
    small = small + flip(small, 1)
    advance(chains, [0, 1, 1])
    small, first_values_grad = hold(chains, small, first_values_grad)
    small = small + flip(small, bits[1])
    small = small + flip(small, bits[2])
    advance(chains, [0, 0, 1])
    small = hold(chains, small)
    for bit in bits[3:]:
        small = small + flip(small, bit)
    branch_all = jnp.concatenate([branch_got, branch_late], axis=0).astype(F32)
    result = (middle + own[0] + branch_all + down_bias) * own_valid.astype(F32)
    result = result.astype(BF16)
    advance(chains, [99, 99, len(chains[2].steps) - 1])
    small, result, first_values_grad = hold(chains, small, result, first_values_grad)
    advance(chains, [0, 0, 1])
    w_down_grad, w_up_grad = feed_out(scalars, chains[:PARTS])
    w_out_grad, w_query_grad, w_key_grad, w_value_grad = last_out(scalars, chains[-1], query_size)
    w_value_grad = w_value_grad.T
    ln1_gain_grad, ln1_bias_grad, out_bias_grad, ln2_gain_grad, ln2_bias_grad, down_bias_grad = (
        small[k * width : (k + 1) * width] for k in range(6)
    )
    query_bias_grad = small[6 * width : 6 * width + query_size]
    value_bias_grad = small[6 * width + query_size : 6 * width + query_size + value_size]
    up_bias_grad = small[6 * width + query_size + value_size :]
    return (
        result,
        tokens_grad,
        first_values_grad,
        ln1_gain_grad,
        ln1_bias_grad,
        w_query_grad,
        query_bias_grad,
        w_key_grad,
        w_value_grad,
        value_bias_grad,
        w_out_grad,
        out_bias_grad,
        ln2_gain_grad,
        ln2_bias_grad,
        w_up_grad,
        up_bias_grad,
        w_down_grad,
        down_bias_grad,
    )


def solution(mesh):
    in_specs = (
        P(("dp", "tensor"), None),
        P(("dp", "tensor"), None),
        P("dp"),
        P(),
        P(),
        P(),
        P(None, "tensor"),
        P("tensor"),
        P(None, "tensor"),
        P(None, "tensor"),
        P("tensor"),
        P("tensor", None),
        P(),
        P(),
        P(),
        P(None, "tensor"),
        P("tensor"),
        P("tensor", None),
        P(),
        P(("dp", "tensor"), None),
    )
    out_specs = (
        P(("dp", "tensor"), None),
        P(("dp", "tensor"), None),
        P(("dp", "tensor"), None),
        P(),
        P(),
        P(None, "tensor"),
        P("tensor"),
        P(None, "tensor"),
        P(None, "tensor"),
        P("tensor"),
        P("tensor", None),
        P(),
        P(),
        P(),
        P(None, "tensor"),
        P("tensor"),
        P("tensor", None),
        P(),
    )
    return jax.shard_map(shards, mesh=mesh, in_specs=in_specs, out_specs=out_specs, check_vma=False)
```

```python
from functools import partial

import jax
import jax.numpy as jnp
from jax import lax
from jax.experimental import pallas as pl
from jax.experimental.pallas import tpu as pltpu
from jax.sharding import PartitionSpec as P

H = 12
HD = 64
PARTS = 2
BLOCK = 256
VMEM_BYTES = 32 * 1024 * 1024
NT = (((1,), (1,)), ((), ()))
TN = (((0,), (0,)), ((), ()))
NN = (((1,), (0,)), ((), ()))
F32 = jnp.float32
BF16 = jnp.bfloat16
STRETCH = 6
SIDE, LENGTH, CORE, WHICH = 0, 1, 2, 3


def shape(dims, dtype):
    return jax.ShapeDtypeStruct(dims, dtype)


def call(kernel, scalars, arrays, out_shape, in_specs=None, out_specs=None, grid=(1,), scratch=(), micros=2):
    def whole(array):
        return pl.BlockSpec(array.shape, lambda *_, dims=len(array.shape): (0,) * dims)

    return pl.pallas_call(
        kernel,
        grid_spec=pltpu.PrefetchScalarGridSpec(
            num_scalar_prefetch=1,
            grid=grid,
            in_specs=[s or whole(a) for s, a in zip(in_specs or [None] * len(arrays), arrays)],
            out_specs=[
                s or whole(o) for s, o in zip(out_specs or [None] * len(out_shape), out_shape)
            ],
            scratch_shapes=list(scratch),
        ),
        out_shape=out_shape,
        compiler_params=pltpu.CompilerParams(vmem_limit_bytes=VMEM_BYTES),
        cost_estimate=pl.CostEstimate(
            flops=STRETCH * micros * 1_150_000_000,
            bytes_accessed=STRETCH * micros * 3_600_000,
            transcendentals=0,
        ),
    )(scalars, *arrays)


def dot(left, right, dims=NN):
    return lax.dot_general(left, right, dims, preferred_element_type=F32)


def pick(flag, left, right):
    return jnp.where(flag, left.astype(F32), right.astype(F32)).astype(left.dtype)


def across(values):
    return lax.ppermute(values, "tensor", [(0, 1), (1, 0)])


def flip(values, bit):
    return lax.ppermute(values, "dp", [(d, d ^ bit) for d in range(lax.axis_size("dp"))])


def halves(values, which):
    half = values.shape[0] // 2
    return (
        lax.dynamic_slice_in_dim(values, which * half, half, 0),
        lax.dynamic_slice_in_dim(values, (1 - which) * half, half, 0),
    )


def join(own, other, which):
    return jnp.concatenate(
        [jnp.where(which == 0, own, other), jnp.where(which == 0, other, own)], axis=0
    )


def slabs(values, which):
    half = values.shape[1] // 2
    return (
        lax.dynamic_slice_in_dim(values, which * half, half, 1),
        lax.dynamic_slice_in_dim(values, (1 - which) * half, half, 1),
    )


def after(values, *found):
    return lax.optimization_barrier((values, found))[0]


def dp_bits():
    return [1 << k for k in range(lax.axis_size("dp").bit_length() - 1)]


def fold_kernel(scalars, own_ref, got_ref, keep_ref, send_ref):
    half = keep_ref.shape[0]
    which = scalars[0]
    for out_ref, part in ((keep_ref, which), (send_ref, 1 - which)):
        rows = pl.ds(pl.multiple_of(part * half, half), half)
        out_ref[...] = (own_ref[rows, :].astype(F32) + got_ref[rows, :].astype(F32)).astype(BF16)


def join_kernel(scalars, own_ref, got_ref, out_ref):
    half = own_ref.shape[0]
    which = scalars[0]
    for in_ref, part in ((own_ref, which), (got_ref, 1 - which)):
        out_ref[pl.ds(pl.multiple_of(part * half, half), half), :] = in_ref[...]


class Chain:
    def __init__(self, keep, send, place):
        self.state, self.place, self.pending = (keep, send), place, None
        bits = dp_bits()
        self.steps = [("halve", bit, later) for bit, later in zip(bits, bits[1:] + [0])]
        self.steps += [("double", bit, 0) for bit in reversed(bits)]

    def which(self, bit):
        return (self.place // bit) % 2

    def send(self):
        self.merge()
        if self.steps:
            self.pending = self.steps.pop(0)
            self.state += (flip(self.state[-1], self.pending[1]),)

    def merge(self):
        if not self.pending:
            return
        (kind, bit, following), self.pending = self.pending, None
        own, got = self.state[0], self.state[-1]
        rows, columns = got.shape
        which = self.which(following if kind == "halve" else bit)[None]
        if kind == "double" and bit == 1:
            return
        if kind == "double" and rows % 16 == 0:
            out = [shape((2 * rows, columns), BF16)]
            self.state = tuple(call(join_kernel, which, [own, got], out))
        elif kind == "double":
            self.state = (join(own, got, which[0]),)
        elif following and rows % 32 == 0:
            out = [shape((rows // 2, columns), BF16)] * 2
            self.state = tuple(call(fold_kernel, which, [own, got], out))
        else:
            total = (own.astype(F32) + got.astype(F32)).astype(BF16)
            self.state = halves(total, which[0]) if following else (total,)

    def step(self):
        self.send()
        self.merge()


def advance(chains, counts):
    for chain, count in zip(chains, counts):
        for _ in range(count):
            chain.step()


def hold(chains, *values):
    states, values = lax.optimization_barrier(([c.state for c in chains], values))
    for chain, state in zip(chains, states):
        chain.state = state
    return values if len(values) != 1 else values[0]


def unit_rows(values):
    centred = values - jnp.mean(values, axis=-1, keepdims=True)
    spread = jnp.mean(centred * centred, axis=-1, keepdims=True)
    scale = lax.rsqrt(spread + 1e-05)
    return centred * scale, scale


def unit_rows_back(unit, scale, grad):
    inner = jnp.mean(grad * unit, axis=-1, keepdims=True)
    return scale * (grad - jnp.mean(grad, axis=-1, keepdims=True) - unit * inner)


def column_sum(values):
    return jnp.sum(values, axis=0, keepdims=True)


def row_spec(width, place=lambda i: i):
    return pl.BlockSpec((BLOCK, width), lambda i, scalars: (place(i), 0))


def valid_rows(scalars, block, rows):
    position = scalars[SIDE] * rows + block * BLOCK
    position = position + lax.broadcasted_iota(jnp.int32, (BLOCK, 1), 0)
    return (position < scalars[LENGTH]).astype(F32)


def norm_kernel(scalars, x_ref, gain_ref, bias_ref, out_ref):
    unit, _ = unit_rows(x_ref[...].astype(F32))
    out_ref[...] = (unit * gain_ref[...] + bias_ref[...]).astype(BF16)


def norm(scalars, values, gain, bias):
    rows, width = values.shape
    return call(
        norm_kernel,
        scalars,
        [values, gain[None], bias[None]],
        [shape((rows, width), BF16)],
        [row_spec(width), None, None],
        [row_spec(width)],
        (rows // BLOCK,),
    )[0]


def project_kernel(
    scalars, x_ref, x_got_ref, w_ref, qb_ref, vb_ref, reused_ref, reused_got_ref, q_ref, k_ref, v_ref
):
    width, fresh = q_ref.shape[1], vb_ref.shape[1]
    own = pl.program_id(0) < pl.num_programs(0) // 2

    def work(x_ref, reused_ref):
        found = dot(x_ref[...], w_ref[...])
        q_ref[...] = (found[:, :width] + qb_ref[...]).astype(BF16)
        k_ref[...] = found[:, width : 2 * width].astype(BF16)
        values = (found[:, 2 * width :] + vb_ref[...]).astype(BF16)
        reused = reused_ref[...]
        for head in range(fresh // HD):
            part = slice(head * HD, (head + 1) * HD)
            v_ref[:, 2 * head * HD : 2 * (head + 1) * HD] = jnp.concatenate(
                [values[:, part], reused[:, part]], axis=1
            )

    pl.when(own)(lambda: work(x_ref, reused_ref))
    pl.when(jnp.logical_not(own))(lambda: work(x_got_ref, reused_got_ref))


def project(scalars, normed, normed_got, weight, query_bias, value_bias, reused, reused_got):
    local, depth = normed.shape
    width, fresh = query_bias.shape[0], value_bias.shape[0]
    blocks = local // BLOCK
    x_spec, r_spec = (row_spec(w, lambda i: jnp.minimum(i, blocks - 1)) for w in (depth, fresh))
    x_got_spec, r_got_spec = (
        row_spec(w, lambda i: jnp.maximum(i - blocks, 0)) for w in (depth, fresh)
    )
    out_spec = pl.BlockSpec(
        (BLOCK, width),
        lambda i, scalars: (lax.rem(i + scalars[SIDE] * blocks, 2 * blocks), 0),
    )
    return call(
        project_kernel,
        scalars,
        [normed, normed_got, weight, query_bias[None], value_bias[None], reused, reused_got],
        [shape((2 * local, width), BF16)] * 3,
        [x_spec, x_got_spec, None, None, None, r_spec, r_got_spec],
        [out_spec] * 3,
        (2 * blocks,),
        micros=4,
    )


def mix_kernel(
    scalars, keep_ref, got_ref, w_ref, w_other_ref, x_ref, ob_ref, gain_ref, bias_ref, mid_ref, out_ref
):
    attention = dot(keep_ref[...], w_ref[...]) + dot(got_ref[...], w_other_ref[...])
    middle = x_ref[...].astype(F32) + attention + ob_ref[...]
    mid_ref[...] = middle
    unit, _ = unit_rows(middle)
    out_ref[...] = (unit * gain_ref[...] + bias_ref[...]).astype(BF16)


def mix(scalars, keep, got, w_out, w_out_other, tokens, out_bias, gain, bias):
    rows, width = tokens.shape
    half, whole = row_spec(got.shape[1]), row_spec(width)
    kept = pl.BlockSpec((None, BLOCK, got.shape[1]), lambda i, scalars: (0, i, 0))
    return call(
        mix_kernel,
        scalars,
        [keep, got, w_out, w_out_other, tokens, out_bias[None], gain[None], bias[None]],
        [shape((rows, width), F32), shape((rows, width), BF16)],
        [kept, half, None, None, whole, None, None, None],
        [whole, whole],
        (rows // BLOCK,),
        micros=3,
    )


def turn_kernel(
    scalars,
    mid_ref,
    cot_ref,
    back_ref,
    back_got_ref,
    gain_ref,
    w_ref,
    w_other_ref,
    mid_grad_ref,
    grad_ref,
    own_ref,
    send_ref,
    sums_ref,
):
    block = pl.program_id(0)
    rows = pl.num_programs(0) * BLOCK
    out_grad = cot_ref[...].astype(F32) * valid_rows(scalars, block, rows)
    unit, scale = unit_rows(mid_ref[...])
    normed_grad = back_ref[...] + back_got_ref[...].astype(F32)
    middle_grad = out_grad + unit_rows_back(unit, scale, normed_grad * gain_ref[...])
    mid_grad_ref[...] = middle_grad
    grad = middle_grad.astype(BF16)
    grad_ref[...] = grad
    own_ref[...] = dot(grad, w_ref[...], NT).astype(BF16)
    send_ref[...] = dot(grad, w_other_ref[...], NT).astype(BF16)

    @pl.when(block == 0)
    def _():
        sums_ref[...] = jnp.zeros_like(sums_ref)

    for k, part in enumerate((normed_grad * unit, normed_grad, middle_grad, out_grad)):
        sums_ref[k : k + 1, :] += column_sum(part)


def turn(scalars, middle, cotangent, back, back_got, gain, w_out, w_out_other):
    rows, width = middle.shape
    whole, half = row_spec(width), row_spec(w_out.shape[0])
    return call(
        turn_kernel,
        scalars,
        [middle, cotangent, back, back_got, gain[None], w_out, w_out_other],
        [shape((rows, width), F32), shape((rows, width), BF16)]
        + [shape((rows, w_out.shape[0]), BF16)] * 2
        + [shape((8, width), F32)],
        [whole, whole, whole, whole, None, None, None],
        [whole, whole, half, half, None],
        (rows // BLOCK,),
        micros=4,
    )


def close_kernel(
    scalars,
    x_ref,
    gain_ref,
    keep_ref,
    got_ref,
    got_late_ref,
    mid_grad_ref,
    grad_ref,
    sums_ref,
):
    unit, scale = unit_rows(x_ref[...].astype(F32))
    early = pl.program_id(0) < pl.num_programs(0) // 2
    normed_grad = keep_ref[...] + pick(early, got_ref[...], got_late_ref[...]).astype(F32)
    grad_ref[...] = mid_grad_ref[...] + unit_rows_back(unit, scale, normed_grad * gain_ref[...])

    @pl.when(pl.program_id(0) == 0)
    def _():
        sums_ref[...] = jnp.zeros_like(sums_ref)

    for k, part in enumerate((normed_grad * unit, normed_grad)):
        sums_ref[k : k + 1, :] += column_sum(part)


def close(scalars, tokens, gain, keep, got, got_late, middle_grad):
    rows, width = tokens.shape
    whole = row_spec(width)
    last = rows // BLOCK // 2 - 1
    first_half = row_spec(width, lambda i: jnp.minimum(i, last))
    second_half = row_spec(width, lambda i: jnp.maximum(i - last - 1, 0))
    return call(
        close_kernel,
        scalars,
        [tokens, gain[None], keep, got, got_late, middle_grad],
        [shape((rows, width), F32), shape((8, width), F32)],
        [whole, None, whole, first_half, second_half, whole],
        [whole, None],
        (rows // BLOCK,),
        micros=3,
    )


def score_parts(k_ref, query, begin, length, sure):
    parts = []
    for first, last in ((0, begin), (begin, begin + BLOCK)):
        if last > first:
            part = dot(k_ref[first:last, :], query, NT)
            keys = lax.broadcasted_iota(jnp.int32, part.shape, 0) + first
            if first == begin:
                queries = lax.broadcasted_iota(jnp.int32, part.shape, 1) + begin
                part = jnp.where((keys <= queries) & (keys < length), part, -1e30)
            elif last > sure:
                part = jnp.where(keys < length, part, -1e30)
            parts.append((first, last, part))
    return parts


def attend_kernel(scalars, q_ref, k_ref, v_ref, out_ref, lse_ref):
    rows = q_ref.shape[0]
    local = rows // 2
    for begin in range(0, rows, BLOCK):
        query = q_ref[begin : begin + BLOCK, :] * HD ** (-0.5)
        lane = lax.broadcasted_iota(jnp.int32, query.shape, 1)
        mixed = []
        for head in range(2):
            mine = (lane < HD) if head == 0 else (lane >= HD)
            own_query = jnp.where(mine, query, 0).astype(BF16)
            parts = score_parts(k_ref, own_query, begin, scalars[LENGTH], local)
            highest = None
            for _, _, part in parts:
                top = jnp.max(part, axis=0, keepdims=True)
                highest = top if highest is None else jnp.maximum(highest, top)
            weights = [jnp.exp(part - highest) for _, _, part in parts]
            total = sum(column_sum(w) for w in weights)
            weights = jnp.concatenate([w.astype(BF16) for w in weights], axis=0)
            mixture = dot(v_ref[: begin + BLOCK, :], weights, TN)
            mixed.append(mixture * (1.0 / total))
            lse_ref[0, head : head + 1, begin : begin + BLOCK] = highest + jnp.log(total)
        row = lax.broadcasted_iota(jnp.int32, mixed[0].shape, 0)
        both = jnp.where(row < HD, mixed[0], mixed[1]).T.astype(BF16)
        away = jnp.abs(scalars[SIDE] - begin // local)
        out_ref[away, begin % local : begin % local + BLOCK, :] = both


def pair_spec(rows):
    return pl.BlockSpec((rows, 2 * HD), lambda p, scalars: (0, p))


def sides_spec(rows):
    return pl.BlockSpec((2, rows // 2, 2 * HD), lambda p, scalars: (0, 0, p))


def attend(scalars, queries, keys, values):
    rows, width = queries.shape
    pairs = width // (2 * HD)
    return call(
        attend_kernel,
        scalars,
        [queries, keys, values],
        [shape((2, rows // 2, width), BF16), shape((pairs, 2, rows), F32)],
        [pair_spec(rows)] * 3,
        [sides_spec(rows), pl.BlockSpec((1, 2, rows), lambda p, scalars: (p, 0, 0))],
        (pairs,),
        micros=10,
    )


def inner_kernel(scalars, out_ref, grad_ref, grad_got_ref, inner_ref):
    local = grad_ref.shape[0]
    for begin in range(0, 2 * local, BLOCK):
        place = slice(begin % local, begin % local + BLOCK)
        away = jnp.abs(scalars[SIDE] - begin // local)
        grad = pick(away == 0, grad_ref[place, :], grad_got_ref[place, :])
        product = (grad.astype(F32) * out_ref[away, place, :].astype(F32)).T
        for head in range(2):
            inner_ref[0, head : head + 1, begin : begin + BLOCK] = column_sum(
                product[head * HD : (head + 1) * HD, :]
            )


def inner_sums(scalars, heads_out, grad, grad_got):
    local, width = grad.shape
    pairs = width // (2 * HD)
    half = pair_spec(local)
    return call(
        inner_kernel,
        scalars,
        [heads_out, grad, grad_got],
        [shape((pairs, 2, 2 * local), F32)],
        [sides_spec(2 * local), half, half],
        [pl.BlockSpec((1, 2, 2 * local), lambda p, scalars: (p, 0, 0))],
        (pairs,),
    )[0]


def attend_back_kernel(
    scalars,
    q_ref,
    k_ref,
    v_ref,
    inner_ref,
    lse_ref,
    grad_ref,
    grad_got_ref,
    dq_ref,
    dk_ref,
    dv_ref,
    dk_sum,
    dv_sum,
):
    rows = q_ref.shape[0]
    local = rows // 2
    dk_sum[...] = jnp.zeros_like(dk_sum)
    dv_sum[...] = jnp.zeros_like(dv_sum)
    for begin in range(0, rows, BLOCK):
        block = slice(begin, begin + BLOCK)
        place = slice(begin % local, begin % local + BLOCK)
        here = scalars[SIDE] == begin // local
        query = q_ref[block, :] * HD ** (-0.5)
        grad = pick(here, grad_ref[place, :], grad_got_ref[place, :])
        lane = lax.broadcasted_iota(jnp.int32, query.shape, 1)
        found = []
        for head in range(2):
            mine = (lane < HD) if head == 0 else (lane >= HD)
            own_query = jnp.where(mine, query, 0).astype(BF16)
            own_grad = jnp.where(mine, grad, 0).astype(BF16)
            inner = inner_ref[0, head : head + 1, block]
            lse = lse_ref[0, head : head + 1, block]
            end = begin + BLOCK
            parts = score_parts(k_ref, own_query, begin, scalars[LENGTH], local)
            chances = jnp.concatenate([jnp.exp(part - lse) for _, _, part in parts], axis=0)
            chance_grad = dot(v_ref[:end, :], own_grad, NT)
            score_grad = (chances * (chance_grad - inner)).astype(BF16)
            dv_sum[:end, :] += dot(chances.astype(BF16), own_grad)
            dk_sum[:end, :] += dot(score_grad, own_query)
            query_grad = dot(k_ref[:end, :], score_grad, TN)
            found.append(query_grad)
        row = lax.broadcasted_iota(jnp.int32, found[0].shape, 0)
        both = jnp.where(row < HD, found[0], found[1]) * HD ** (-0.5)
        dq_ref[block, :] = both.T.astype(BF16)
    dk_ref[...] = dk_sum[...].astype(BF16)
    dv_ref[...] = dv_sum[...].astype(BF16)


def attend_back(scalars, queries, keys, values, inner, lse, grad, grad_got):
    rows, width = queries.shape
    pairs = width // (2 * HD)
    half = pair_spec(rows // 2)
    return call(
        attend_back_kernel,
        scalars,
        [queries, keys, values, inner, lse, grad, grad_got],
        [shape((rows, width), BF16)] * 3,
        [pair_spec(rows)] * 3
        + [pl.BlockSpec((1, 2, rows), lambda p, scalars: (p, 0, 0))] * 2
        + [half, half],
        [pair_spec(rows)] * 3,
        (pairs,),
        [pltpu.VMEM((rows, 2 * HD), F32)] * 2,
        micros=14,
    )


def gelu_parts(hidden):
    rate = 0.7978845608028654
    square = hidden * hidden
    bend = jnp.tanh(rate * hidden * (1.0 + 0.044715 * square))
    lift = 0.5 * (1.0 + bend)
    slope = lift + 0.5 * hidden * (1.0 - bend * bend) * (rate * (1.0 + 3 * 0.044715 * square))
    return hidden * lift, slope


def feed_kernel(steps, scalars, normed_ref, grad_ref, up_ref, bias_ref, down_ref, *refs):
    branch_ref, back_ref, active_ref, hidden_grad_ref, bias_grad_ref, branch_sum, back_sum = refs[-7:]
    normed, grad = normed_ref[...], grad_ref[...]
    up, down = up_ref[...], down_ref[...]
    active, slope = gelu_parts(dot(normed, up) + bias_ref[...])
    active = active.astype(BF16)
    hidden_grad = (dot(grad, down, NT) * slope).astype(BF16)
    branch, back = dot(active, down), dot(hidden_grad, up, NT)
    active_ref[...] = active
    hidden_grad_ref[...] = hidden_grad
    bias_grad_ref[...] = column_sum(hidden_grad.astype(F32))
    for k in range(steps):

        @pl.when(pl.program_id(0) == k)
        def _():
            sums = refs[:-7] if k == 0 else (branch_sum, back_sum)
            outs = (branch_ref, back_ref) if k == steps - 1 else (branch_sum, back_sum)
            for n, (new, out_ref) in enumerate(zip((branch, back), outs)):
                total = new + sums[n][...] if sums else new
                out_ref[...] = total.astype(out_ref.dtype)


def feed(scalars, normed, grad, w_up, up_bias, w_down, dtype, part=0, parts=1, sums=()):
    rows, width = normed.shape
    hidden = w_down.shape[0] // parts
    tile = 3 * BLOCK
    steps = hidden // tile
    begin = part * steps
    line = pl.BlockSpec((1, tile), lambda i, scalars: (0, i))
    units = pl.BlockSpec((rows, tile), lambda i, scalars: (0, i))
    return call(
        partial(feed_kernel, steps),
        scalars,
        [normed, grad, w_up, up_bias[None], w_down, *sums],
        [shape((rows, width), dtype)] * 2
        + [shape((rows, hidden), BF16)] * 2
        + [shape((1, hidden), F32)],
        [
            None,
            None,
            pl.BlockSpec((width, tile), lambda i, scalars: (0, begin + i)),
            pl.BlockSpec((1, tile), lambda i, scalars: (0, begin + i)),
            pl.BlockSpec((tile, width), lambda i, scalars: (begin + i, 0)),
        ]
        + [None] * len(sums),
        [None, None, units, units, line],
        (steps,),
        [pltpu.VMEM((rows, width), F32)] * 2,
        micros=10 // parts,
    )


def feed_weights_kernel(scalars, *refs):
    actives, hidden_grads, normeds, grads = refs[0:2], refs[2:4], refs[4:6], refs[6:8]
    keep_ref, send_ref = refs[8:]
    step = pl.program_id(0)
    down = sum(dot(a[...], g[...], TN) for a, g in zip(actives, grads)).astype(BF16)
    up = sum(dot(n[...], h[...], TN) for n, h in zip(normeds, hidden_grads)).astype(BF16)
    for k in range(keep_ref.shape[0] // BLOCK):
        lines = slice(k * BLOCK, (k + 1) * BLOCK)

        @pl.when((step == k) & (scalars[CORE] == 0))
        def _():
            keep_ref[lines, :] = down
            send_ref[:, lines] = up

        @pl.when((step == k) & (scalars[CORE] == 1))
        def _():
            send_ref[lines, :] = down
            keep_ref[:, lines] = up


def feed_weights(scalars, part, own, other, normeds, grads):
    rows, width = normeds[0].shape
    hidden = other[2].shape[1]
    steps = hidden // BLOCK
    of_all = pl.BlockSpec((rows, BLOCK), lambda i, scalars: (0, part * steps + i))
    of_part = pl.BlockSpec((rows, BLOCK), lambda i, scalars: (0, i))
    return call(
        feed_weights_kernel,
        scalars,
        [own[2], other[2], own[3], other[3], *normeds, *grads],
        [shape((hidden, width), BF16)] * 2,
        [of_all, of_part, of_all, of_part] + [None] * 4,
        None,
        (steps,),
        micros=5,
    )


def fresh_columns(values):
    return jnp.concatenate(
        [values[:, k * HD : (k + 1) * HD] for k in range(0, values.shape[1] // HD, 2)], axis=1
    )


def reused_columns(values):
    return jnp.concatenate(
        [values[:, k * HD : (k + 1) * HD] for k in range(1, values.shape[1] // HD, 2)], axis=1
    )


def last_weights_kernel(
    scalars, x_ref, x_got_ref, dq_ref, dk_ref, dv_ref, wo_ref, wo_got_ref, keep_ref, send_ref, q_sum_ref, v_sum_ref
):
    size, half = dq_ref.shape[1], wo_ref.shape[1] // 2
    local = x_ref.shape[0]
    sides = (scalars[SIDE], 1 - scalars[SIDE])
    spans = [pl.ds(pl.multiple_of(s * local, local), local) for s in sides]
    xs = (x_ref, x_got_ref)
    fresh = [fresh_columns(dv_ref[s, :]) for s in spans]
    for out_ref, h in ((keep_ref, scalars[CORE]), (send_ref, 1 - scalars[CORE])):
        lines = pl.ds(pl.multiple_of(h * half, half), half)
        wo = wo_ref[:, lines] + wo_got_ref[:, lines].astype(F32)
        out_ref[:, :half] = wo.astype(BF16)
        for k, d_ref in enumerate((dq_ref, dk_ref)):
            total = sum(dot(x[:, lines], d_ref[s, :], TN) for x, s in zip(xs, spans))
            out_ref[:, half + k * size : half + (k + 1) * size] = total.astype(BF16)
        total = sum(dot(x[:, lines], f, TN) for x, f in zip(xs, fresh)).astype(BF16)
        padding = out_ref.shape[1] - half - 2 * size - total.shape[1]
        out_ref[:, half + 2 * size :] = jnp.pad(total, ((0, 0), (0, padding)))
    q_sum_ref[...] = column_sum(dq_ref[...].astype(F32))
    v_sum_ref[...] = sum(column_sum(f.astype(F32)) for f in fresh)


def last_weights(scalars, normed, normed_got, query_grad, key_grad, value_grad, wo, wo_got):
    width, size = normed.shape[1], query_grad.shape[1]
    columns = -(-(width // 2 + 5 * size // 2) // 128) * 128
    return call(
        last_weights_kernel,
        scalars,
        [normed, normed_got, query_grad, key_grad, value_grad, wo, wo_got],
        [shape((width // 2, columns), BF16)] * 2
        + [shape((1, size), F32), shape((1, size // 2), F32)],
        micros=4,
    )


def inputs_back_kernel(scalars, *refs):
    w_ref, keep_ref, send_ref, keep_reused_ref, send_reused_ref = refs[6:]
    for (dq_ref, dk_ref, dv_ref), out_ref, reused_ref in (
        (refs[0:3], keep_ref, keep_reused_ref),
        (refs[3:6], send_ref, send_reused_ref),
    ):
        size = dq_ref.shape[1]
        total = dot(dq_ref[...], w_ref[:, :size], NT)
        total = total + dot(dk_ref[...], w_ref[:, size : 2 * size], NT)
        total = total + dot(fresh_columns(dv_ref[...]), w_ref[:, 2 * size :], NT)
        out_ref[...] = total.astype(out_ref.dtype)
        reused_ref[...] = reused_columns(dv_ref[...])


def inputs_back(scalars, query_grad, key_grad, value_grad, w_in):
    rows, size = query_grad.shape
    half, width = rows // 2, w_in.shape[0]
    blocks = half // BLOCK
    keep = pl.BlockSpec((BLOCK, size), lambda i, scalars: (scalars[SIDE] * blocks + i, 0))
    send = pl.BlockSpec((BLOCK, size), lambda i, scalars: ((1 - scalars[SIDE]) * blocks + i, 0))
    grads = [query_grad, key_grad, value_grad]
    return call(
        inputs_back_kernel,
        scalars,
        [*grads, *grads, w_in],
        [shape((half, width), F32), shape((half, width), BF16)]
        + [shape((half, size // 2), BF16)] * 2,
        [keep] * 3 + [send] * 3 + [None],
        [row_spec(width)] * 2 + [row_spec(size // 2)] * 2,
        (blocks,),
        micros=4,
    )


def feed_out_kernel(scalars, *refs):
    down_ref, up_ref = refs[-2:]
    first = scalars[CORE] == 0
    for part in range(PARTS):
        own_ref, got_ref = refs[2 * part : 2 * part + 2]

        @pl.when(pl.program_id(0) == part)
        def _():
            own, got = own_ref[...].astype(F32), got_ref[...].astype(F32)
            down_ref[...] = jnp.where(first, own, got)
            up_ref[...] = jnp.where(first, got, own)


def feed_out(scalars, chains):
    arrays = [a for chain in chains for a in chain.state]
    rows, width = arrays[0].shape
    return call(
        feed_out_kernel,
        scalars,
        arrays,
        [shape((PARTS * rows, width), F32), shape((width, PARTS * rows), F32)],
        None,
        [
            pl.BlockSpec((rows, width), lambda i, scalars: (i, 0)),
            pl.BlockSpec((width, rows), lambda i, scalars: (0, i)),
        ],
        (PARTS,),
        micros=5,
    )


def last_out_kernel(scalars, own_ref, got_ref, wo_ref, wq_ref, wk_ref, wv_ref):
    half = own_ref.shape[0]
    size = wq_ref.shape[1]
    first = scalars[CORE] == 0
    own, got = own_ref[...].astype(F32), got_ref[...].astype(F32)
    for h, part in enumerate((jnp.where(first, own, got), jnp.where(first, got, own))):
        lines = slice(h * half, (h + 1) * half)
        wo_ref[:, lines] = part[:, :half]
        wq_ref[lines, :] = part[:, half : half + size]
        wk_ref[lines, :] = part[:, half + size : half + 2 * size]
        wv_ref[:, lines] = part[:, half + 2 * size : half + 2 * size + size // 2].T


def last_out(scalars, chain, size):
    own, got = chain.state
    half = own.shape[0]
    return call(
        last_out_kernel,
        scalars,
        [own, got],
        [shape((size, 2 * half), F32)]
        + [shape((2 * half, size), F32)] * 2
        + [shape((size // 2, 2 * half), F32)],
        micros=3,
    )


def shards(
    tokens,
    first_values,
    lengths,
    reuse_index,
    ln1_gain,
    ln1_bias,
    w_query,
    query_bias,
    w_key,
    w_value,
    value_bias,
    w_out,
    out_bias,
    ln2_gain,
    ln2_bias,
    w_up,
    up_bias,
    w_down,
    down_bias,
    cotangent,
):
    place, side = lax.axis_index("dp"), lax.axis_index("tensor")
    core = place % 2
    local_rows, width = tokens.shape
    query_size, value_size = query_bias.shape[0], value_bias.shape[0]
    length = lengths[0]
    scalars = jnp.stack([side, length, core]).astype(jnp.int32)
    positions = jnp.arange(local_rows)[:, None]
    own_valid = side * local_rows + positions < length
    other_valid = (1 - side) * local_rows + positions < length

    early, late = cotangent[: local_rows // 2], cotangent[local_rows // 2 :]
    normed_one = norm(scalars, tokens, ln1_gain, ln1_bias)
    one_got = across(normed_one)
    picks = reuse_index[jnp.arange(2 * value_size) // HD]
    selector = (
        (jnp.arange(width)[:, None] // HD == picks[None, :])
        & ((jnp.arange(width) % HD)[:, None] == (jnp.arange(2 * value_size) % HD)[None, :])
    ).astype(BF16)
    first_values, selector = after((first_values, selector), normed_one)
    chosen = dot(first_values, selector).astype(BF16)
    own_chosen, other_chosen = slabs(chosen, side)
    chosen_got = across(other_chosen)
    w_in = jnp.concatenate([w_query, w_key, w_value], axis=1)
    branch_grad = jnp.where(own_valid, cotangent, 0)
    out_piece = halves(w_out, core)[0]
    one_got, chosen_got, w_in, branch_grad, out_piece, early, late = lax.optimization_barrier(
        (one_got, chosen_got, w_in, branch_grad, out_piece, early, late)
    )
    out_got = across(out_piece)
    early_got = across(early)
    queries, keys, values = project(
        scalars, normed_one, one_got, w_in, query_bias, value_bias, own_chosen, chosen_got
    )
    heads_out, lse = attend(scalars, queries, keys, values)
    heads_out, out_got, early_got = lax.optimization_barrier((heads_out, out_got, early_got))
    heads_got = across(heads_out[1])
    w_out_other = join(out_got, flip(out_got, 1), core)
    heads_got, w_out_other, late = lax.optimization_barrier((heads_got, w_out_other, late))
    middle, normed_two = mix(
        scalars, heads_out, heads_got, w_out, w_out_other, tokens, out_bias, ln2_gain, ln2_bias
    )

    normed_two, late = lax.optimization_barrier((normed_two, late))
    two_got = across(normed_two)
    late_got = across(late)
    own = feed(scalars, normed_two, branch_grad, w_up, up_bias, w_down, F32)
    two_got, late_got, own = lax.optimization_barrier((two_got, late_got, own))
    branch_grad_got = jnp.where(other_valid, jnp.concatenate([early_got, late_got], axis=0), 0)
    normeds, grads = (normed_two, two_got), (branch_grad, branch_grad_got)
    chains = []

    def add_chain(part, other):
        keep, send = feed_weights(scalars, part, own, other, normeds, grads)
        chains.append(Chain(keep, send, place))

    first = feed(scalars, two_got, branch_grad_got, w_up, up_bias, w_down, F32, 0, PARTS)
    add_chain(0, first)
    sums = hold(chains, *first[:2])
    advance(chains, [1])
    second = feed(scalars, two_got, branch_grad_got, w_up, up_bias, w_down, BF16, 1, PARTS, sums)
    up_bias_grad = (own[4] + jnp.concatenate([first[4], second[4]], axis=1)).reshape(-1)
    branch_send, back_send = hold(chains, *second[:2])
    back_got = across(back_send)
    chains[0].send()
    add_chain(1, second)

    turned = turn(
        scalars, middle, cotangent, own[1], back_got, ln2_gain, w_out, w_out_other
    )
    middle_grad, attention_grad, heads_grad, heads_grad_send, two_sums, up_bias_grad = hold(
        chains, *turned, up_bias_grad
    )
    heads_grad_got = across(heads_grad_send)
    out_grad_send = dot(heads_got, attention_grad, TN).astype(BF16)
    out_grad_own = dot(heads_out[0], attention_grad, TN)
    for chain in chains:
        chain.send()
    inner = inner_sums(scalars, heads_out, heads_grad, heads_grad_got)
    heads_grad_got, inner, out_grad_send, out_grad_own = hold(
        chains, heads_grad_got, inner, out_grad_send, out_grad_own
    )
    out_grad_got = across(out_grad_send)
    query_grad, key_grad, value_grad = attend_back(
        scalars, queries, keys, values, inner, lse, heads_grad, heads_grad_got
    )
    advance(chains, [1, 1])
    middle_rows = local_rows // 2
    out_grad_got, query_grad, key_grad, value_grad, branch_send = hold(
        chains, out_grad_got, query_grad, key_grad, value_grad, branch_send
    )
    keep, send, query_sums, value_sums = last_weights(
        scalars, normed_one, one_got, query_grad, key_grad, value_grad, out_grad_own, out_grad_got
    )
    chains.append(Chain(keep, send, place))

    branch_got = across(branch_send[:middle_rows])
    advance(chains, [1, 1, 1])
    branch_send, branch_got, query_grad, key_grad, value_grad = hold(
        chains, branch_send, branch_got, query_grad, key_grad, value_grad
    )
    back_keep, back_send, first_keep, first_send = inputs_back(
        scalars, query_grad, key_grad, value_grad, w_in
    )
    back_got = across(back_send[:middle_rows])
    advance(chains, [1, 1, 1])
    back_keep, back_got, back_send, first_keep, first_send = hold(
        chains, back_keep, back_got, back_send, first_keep, first_send
    )
    back_late = across(back_send[middle_rows:])
    first_got = across(first_send)
    advance(chains, [1, 1, 1])
    back_late, first_got, branch_send = hold(chains, back_late, first_got, branch_send)
    branch_late = across(branch_send[middle_rows:])
    tokens_grad, one_sums = close(
        scalars, tokens, ln1_gain, back_keep, back_got, back_late, middle_grad
    )
    advance(chains, [1, 1, 1])
    tokens_grad, one_sums, branch_late, first_got = hold(
        chains, tokens_grad, one_sums, branch_late, first_got
    )
    first_grads = jnp.concatenate(
        [jnp.where(side == 0, first_keep, first_got), jnp.where(side == 0, first_got, first_keep)],
        axis=1,
    )
    first_values_grad = dot(first_grads, selector, NT)
    whole = jnp.concatenate([one_sums[:2], two_sums[2:3], two_sums[:2], two_sums[3:4]]).reshape(-1)
    whole = whole + across(whole)
    small = jnp.concatenate(
        [whole, query_sums.reshape(-1), value_sums.reshape(-1), up_bias_grad]
    )
    bits = dp_bits()
    small = small + flip(small, 1)
    advance(chains, [0, 1, 1])
    small, first_values_grad = hold(chains, small, first_values_grad)
    small = small + flip(small, bits[1])
    small = small + flip(small, bits[2])
    advance(chains, [0, 0, 1])
    small = hold(chains, small)
    for bit in bits[3:]:
        small = small + flip(small, bit)
    branch_all = jnp.concatenate([branch_got, branch_late], axis=0).astype(F32)
    result = (middle + own[0] + branch_all + down_bias) * own_valid.astype(F32)
    result = result.astype(BF16)
    advance(chains, [99, 99, len(chains[2].steps) - 1])
    vectors = [small[k * width : (k + 1) * width] for k in range(6)]
    vectors.append(small[6 * width : 6 * width + query_size])
    vectors.append(small[6 * width + query_size : 6 * width + query_size + value_size])
    vectors.append(small[6 * width + query_size + value_size :])
    vectors, result, first_values_grad = hold(chains, vectors, result, first_values_grad)
    ln1_gain_grad, ln1_bias_grad, out_bias_grad, ln2_gain_grad, ln2_bias_grad, down_bias_grad = (
        vectors[:6]
    )
    query_bias_grad, value_bias_grad, up_bias_grad = vectors[6:]
    advance(chains, [0, 0, 1])
    w_down_grad, w_up_grad = feed_out(scalars, chains[:PARTS])
    w_out_grad, w_query_grad, w_key_grad, w_value_grad = last_out(scalars, chains[-1], query_size)
    w_value_grad = w_value_grad.T
    return (
        result,
        tokens_grad,
        first_values_grad,
        ln1_gain_grad,
        ln1_bias_grad,
        w_query_grad,
        query_bias_grad,
        w_key_grad,
        w_value_grad,
        value_bias_grad,
        w_out_grad,
        out_bias_grad,
        ln2_gain_grad,
        ln2_bias_grad,
        w_up_grad,
        up_bias_grad,
        w_down_grad,
        down_bias_grad,
    )


def solution(mesh):
    in_specs = (
        P(("dp", "tensor"), None),
        P(("dp", "tensor"), None),
        P("dp"),
        P(),
        P(),
        P(),
        P(None, "tensor"),
        P("tensor"),
        P(None, "tensor"),
        P(None, "tensor"),
        P("tensor"),
        P("tensor", None),
        P(),
        P(),
        P(),
        P(None, "tensor"),
        P("tensor"),
        P("tensor", None),
        P(),
        P(("dp", "tensor"), None),
    )
    out_specs = (
        P(("dp", "tensor"), None),
        P(("dp", "tensor"), None),
        P(("dp", "tensor"), None),
        P(),
        P(),
        P(None, "tensor"),
        P("tensor"),
        P(None, "tensor"),
        P(None, "tensor"),
        P("tensor"),
        P("tensor", None),
        P(),
        P(),
        P(),
        P(None, "tensor"),
        P("tensor"),
        P("tensor", None),
        P(),
    )
    return jax.shard_map(shards, mesh=mesh, in_specs=in_specs, out_specs=out_specs, check_vma=False)
```
